256 devices in a mesh: gx: 32 (over x, z), gy: 8 (over y, core).
Axes of the slice: x: 4, y: 4, z: 8, core: 2. Of those that a mesh axis runs over, the one named last changes fastest.
Arguments:
- forcing: float32 [3, 256, 128, 512], P(None, 'gx', 'gy'), may hold values from -6.5 to 6.5
- phase_ids: int32 [256, 128, 512], P('gx', 'gy'), may hold values from 0 to 3
Outputs:
- velocity: float32 [3, 256, 128, 512], P(None, 'gx', 'gy')
The draws below stay inside these ranges and needn't reach their ends.
All inputs are finite; a program needn't handle non-finite values.
Results may differ from the reference program's by a relative error of at most 0.0003.
Values sent between devices are 32-bit elements; how exact they have to be, the bound alone decides.
No kernel may reach another device: no remote copies, remote signals or barrier semaphores. Data moves between devices by JAX's collectives and lax.ppermute only.
A program may use at most 128 MiB of HBM per device.

```python
import jax
import jax.numpy as jnp
from jax import lax

NZ = 512
COARSE_SWEEPS = 6
NX = 256
NY = 128


def draw_forcing(key, part):
    base = jax.random.normal(key, (3, NX, NY, NZ), jnp.float32)
    return jnp.clip(base, -6.0, 6.0)


def with_ends(array, key, low, top_value):
    shape = array.shape
    place = [jax.random.randint(jax.random.fold_in(key, axis), (), 0, shape[axis]) for axis in range(len(shape))]
    array = array.at[tuple(place)].set(low)
    longest = shape.index(max(shape))
    place[longest] = (place[longest] + 1) % shape[longest]
    return array.at[tuple(place)].set(top_value)


def setup_inputs(seed: int = 0) -> dict:
    arg_keys = jax.random.split(jax.random.key(seed), 3)
    forcing = draw_forcing(jax.random.fold_in(arg_keys[2], 71), 0)
    phase_ids = with_ends(jax.random.randint(arg_keys[1], (NX, NY, NZ), 0, 4), jax.random.fold_in(arg_keys[1], 1), 0, 3).astype(jnp.int32)
    return {"forcing": forcing, "phase_ids": phase_ids}


viscosities = (0.2, 0.6, 1.5, 4.0)
relax_weight = 2.0 / 3.0


def lookup(phase_ids):
    viscosity = jnp.zeros(phase_ids.shape, jnp.float32)
    for material, visc_value in enumerate(viscosities):
        viscosity = viscosity + jnp.where(phase_ids == material, jnp.float32(visc_value), jnp.float32(0.0))
    return viscosity


def restrict(values):
    extent = values.shape
    leading = extent[:-3]
    blocks = values.reshape(leading + (extent[-3] // 2, 2, extent[-2] // 2, 2, extent[-1] // 2, 2))
    return jnp.mean(blocks, axis=(-5, -3, -1))


def prolong(values):
    return jnp.repeat(jnp.repeat(jnp.repeat(values, 2, axis=-3), 2, axis=-2), 2, axis=-1)


def pad_plane(values, width):
    padding = [(0, 0)] * (values.ndim - 3) + [(width, width), (width, width), (0, 0)]
    return jnp.pad(values, padding)


def face_set(wide_visc, spacing):
    center = wide_visc[1:-1, 1:-1, :]
    z_padded = jnp.pad(center, ((0, 0), (0, 0), (1, 1)))
    besides = (wide_visc[2:, 1:-1, :], wide_visc[:-2, 1:-1, :], wide_visc[1:-1, 2:, :],
               wide_visc[1:-1, :-2, :], z_padded[:, :, 2:], z_padded[:, :, :-2])
    coeffs = tuple(jnp.where(beside > 0.0, 0.5 * (center + beside), center) / spacing for beside in besides)
    diagonal = coeffs[0]
    for entry in coeffs[1:]:
        diagonal = diagonal + entry
    inside = center > 0.0
    inverse = jnp.where(inside, 1.0 / jnp.where(inside, diagonal, 1.0), 0.0)
    return coeffs, inverse


def apply_operator(wide_field, coeffs):
    center = wide_field[..., 1:-1, 1:-1, :]
    padding = [(0, 0)] * (center.ndim - 1) + [(1, 1)]
    z_padded = jnp.pad(center, padding)
    besides = (wide_field[..., 2:, 1:-1, :], wide_field[..., :-2, 1:-1, :], wide_field[..., 1:-1, 2:, :],
               wide_field[..., 1:-1, :-2, :], z_padded[..., 2:], z_padded[..., :-2])
    summed = jnp.zeros_like(center)
    for face_coeff, beside in zip(coeffs, besides):
        summed = summed + face_coeff * (center - beside)
    return summed


def reference(forcing, phase_ids):
    viscosity = lookup(phase_ids)
    level_sets = []
    for level_index in range(3):
        level_sets.append(face_set(pad_plane(viscosity, 1), 4.0 ** level_index))
        if level_index < 2:
            viscosity = restrict(viscosity)

    def jacobi_sweep(current, source, level_set):
        coeffs, inverse = level_set
        return current + relax_weight * (source - apply_operator(pad_plane(current, 1), coeffs)) * inverse

    def descend(source, level_set):
        coeffs, inverse = level_set
        current = relax_weight * source * inverse
        current = jacobi_sweep(current, source, level_set)
        residual = source - apply_operator(pad_plane(current, 1), coeffs)
        return current, restrict(residual)

    def single(source):
        fine_velocity, source_one = descend(source, level_sets[0])
        middle, source_two = descend(source_one, level_sets[1])
        coarse = relax_weight * source_two * level_sets[2][1]
        for repeat in range(COARSE_SWEEPS - 1):
            coarse = jacobi_sweep(coarse, source_two, level_sets[2])
        middle = middle + prolong(coarse)
        middle = jacobi_sweep(middle, source_one, level_sets[1])
        middle = jacobi_sweep(middle, source_one, level_sets[1])
        fine_velocity = fine_velocity + prolong(middle)
        fine_velocity = jacobi_sweep(fine_velocity, source, level_sets[0])
        fine_velocity = jacobi_sweep(fine_velocity, source, level_sets[0])
        return fine_velocity

    return lax.map(single, forcing)
```

```python
import functools

import jax
import jax.numpy as jnp
from jax import lax
from jax.experimental import pallas as pl
from jax.experimental.pallas import tpu as pltpu
from jax.sharding import PartitionSpec as P

F32 = jnp.float32
BF16 = jnp.bfloat16
WEIGHT = 2.0 / 3.0
VMEM_LIMIT = 40 * 1024 * 1024


def materials(ids):
    eta = jnp.where(ids == 3, F32(4.0), F32(0.0))
    eta = jnp.where(ids == 2, F32(1.5), eta)
    eta = jnp.where(ids == 1, F32(0.6), eta)
    return jnp.where(ids == 0, F32(0.2), eta)


def lanes_of(shape):
    return lax.broadcasted_iota(jnp.int32, shape, len(shape) - 1)


def next_row(v):
    return pltpu.roll(v, v.shape[0] - 1, 0)


def last_row(v):
    return pltpu.roll(v, 1, 0)


def next_lane(v):
    return pltpu.roll(v, v.shape[1] - 1, 1)


def last_lane(v):
    return pltpu.roll(v, 1, 1)


def split_dot(rows, matrix):
    high = rows.astype(BF16)
    low = (rows - high.astype(F32)).astype(BF16)
    return jnp.dot(high, matrix, preferred_element_type=F32) + jnp.dot(
        low, matrix, preferred_element_type=F32
    )


def pair_matrix(fine):
    shape = (fine, fine // 2)
    row = lax.broadcasted_iota(jnp.int32, shape, 0)
    col = lax.broadcasted_iota(jnp.int32, shape, 1)
    return jnp.where((row == 2 * col) | (row == 2 * col + 1), F32(1), F32(0)).astype(BF16)


def copy_matrix(coarse):
    shape = (coarse, 2 * coarse)
    row = lax.broadcasted_iota(jnp.int32, shape, 0)
    col = lax.broadcasted_iota(jnp.int32, shape, 1)
    return jnp.where((col == 2 * row) | (col == 2 * row + 1), F32(1), F32(0)).astype(BF16)


YP, YM, ZP, ZM, DG, EI = range(6)


def coefficients(eta, cx, cf, layers, scale):
    half = 0.5 * scale

    def face(i, _):
        cx[i] = half * (eta[i] + eta[i + 1])
        return 0

    lax.fori_loop(0, layers + 1, face, 0)

    def body(i, _):
        here = eta[i + 1]
        lane = lanes_of(here.shape)
        first = lane == 0
        final = lane == here.shape[1] - 1
        yp, ym = next_row(here), last_row(here)
        zp, zm = next_lane(here), last_lane(here)
        cf[YP, i] = half * (here + yp)
        cf[YM, i] = half * (here + ym)
        cf[ZP, i] = jnp.where(final, 0.0, half * (here + zp))
        cf[ZM, i] = jnp.where(first, 0.0, half * (here + zm))

        def ghost(q):
            return jnp.where(q > 0.0, q, here)

        around = ghost(yp) + ghost(ym) + ghost(eta[i]) + ghost(eta[i + 2])
        around = around + jnp.where(final, here, zp) + jnp.where(first, here, zm)
        diag = scale * (3.0 * here + 0.5 * around)
        cf[DG, i] = diag
        cf[EI, i] = jnp.where(here > 0.0, WEIGHT / diag, 0.0)
        return 0

    lax.fori_loop(0, layers, body, 0)


def gather_sum(v, comp, i, cx, cf, k):
    here = v[comp, i]
    total = cx[k] * v[comp, i - 1] + cx[k + 1] * v[comp, i + 1]
    total = total + cf[YP, k] * next_row(here) + cf[YM, k] * last_row(here)
    total = total + cf[ZP, k] * next_lane(here) + cf[ZM, k] * last_lane(here)
    return here, total


def sweep(v, vo, g, go, cx, cf, co, out, oo, low, high):
    vo, go, co, oo = vo + low, go + low, co + low, oo + low

    def body(n, _):
        for comp in range(3):
            here, total = gather_sum(v, comp, n + vo, cx, cf, n + co)
            out[comp, n + oo] = (1.0 / 3.0) * here + cf[EI, n + co] * (g[comp, n + go] + total)
        return 0

    lax.fori_loop(0, high - low, body, 0)


def residual(v, vo, g, go, cx, cf, co, comp, x):
    here, total = gather_sum(v, comp, x + vo, cx, cf, x + co)
    return g[comp, x + go] - cf[DG, x + co] * here + total


def pack_fine_x(f, ids, up, down):
    for c in range(3):
        for k in range(3):
            up[3 * c + k] = f[c, 5 + k]
            down[3 * c + k] = f[c, k]
    for k in range(4):
        up[9 + k] = materials(ids[4 + k])
        down[9 + k] = materials(ids[k])


def fine_source(f, low, high, c, x):
    if x < 0:
        return low[3 * c + x + 3]
    if x < 8:
        return f[c, x]
    return high[3 * c + x - 8]


def fine_eta(ids, low, high, x):
    if x < 0:
        return low[9 + x + 4]
    if x < 8:
        return materials(ids[x])
    return high[9 + x - 8]


def pack_fine_y(f, ids, low, high, up, down):
    for i in range(14):
        rows = [fine_source(f, low, high, c, i - 3) for c in range(3)]
        for out, at in ((up, 13), (down, 0)):
            out[i, 0:3] = rows[0][at : at + 3]
            out[i, 3:6] = rows[1][at : at + 3]
            out[i, 6:8] = rows[2][at : at + 2]
            out[14 + i // 8, i % 8 : i % 8 + 1] = rows[2][at + 2 : at + 3]
    for out in (up, down):
        out[15, 6:8] = jnp.zeros((2, f.shape[-1]), F32)
    for j in range(16):
        eta = fine_eta(ids, low, high, j - 4)
        at = 4 * (j % 2)
        up[16 + j // 2, at : at + 4] = eta[12:16]
        down[16 + j // 2, at : at + 4] = eta[0:4]


def fine_down(f, ids, xlow, xhigh, ylow, yhigh, v0, g, cx, cf, f1, eta1, up, down, eta, va, pairs, rest):
    nz = f.shape[-1]
    blank = jnp.zeros((1, nz), F32)
    for c in range(3):
        for i in range(14):
            g[c, i, 4:20] = fine_source(f, xlow, xhigh, c, i - 3)
            for side, at in ((ylow, 1), (yhigh, 20)):
                if c < 2:
                    g[c, i, at : at + 3] = side[i, 3 * c : 3 * c + 3]
                else:
                    g[c, i, at : at + 2] = side[i, 6:8]
                    g[c, i, at + 2 : at + 3] = side[14 + i // 8, i % 8 : i % 8 + 1]
            g[c, i, 0:1] = blank
            g[c, i, 23:24] = blank
    for j in range(16):
        eta[j, 4:20] = fine_eta(ids, xlow, xhigh, j - 4)
        at = 4 * (j % 2)
        eta[j, 0:4] = ylow[16 + j // 2, at : at + 4]
        eta[j, 20:24] = yhigh[16 + j // 2, at : at + 4]

    coefficients(eta, cx, cf, 14, 1.0)

    def start(i, _):
        for c in range(3):
            va[c, i] = cf[EI, i] * g[c, i]
        return 0

    lax.fori_loop(0, 14, start, 0)
    sweep(va, 3, g, 3, cx, cf, 3, v0, 2, -2, 10)

    def down_pair(k, _):
        for c in range(3):
            x = 2 * k
            total = residual(v0, 2, g, 3, cx, cf, 3, c, x) + residual(v0, 2, g, 3, cx, cf, 3, c, x + 1)
            put_plane(pairs, c * 4 + k, total)
        return 0

    lax.fori_loop(0, 4, down_pair, 0)

    def eta_pair(k, _):
        put_plane(pairs, 12 + k, eta[2 * k + 2] + eta[2 * k + 3])
        return 0

    lax.fori_loop(0, 6, eta_pair, 0)
    for n in range(18):
        row_pairs(pairs, n, 4, 8, rest, n * 8)
    coarse = split_dot(rest[...], pair_matrix(nz)) * 0.125
    for n in range(12):
        block = coarse[n * 8 : n * 8 + 8]
        f1[n // 4, n % 4] = block
        up[n] = block
        down[n] = block
    for n in range(6):
        block = coarse[96 + n * 8 : 96 + n * 8 + 8]
        eta1[n] = block
        if n < 5:
            up[12 + n] = block
        if n > 0:
            down[12 + n - 1] = block


def lane_blocks(planes, nz):
    width = min(nz, 128)
    return (planes, nz // width, 24, width)


def put_plane(ref, n, value):
    width = ref.shape[-1]
    for b in range(ref.shape[1]):
        ref[n, b] = value[:, b * width : b * width + width]


def row_pairs(ref, n, at, count, out, row):
    width = ref.shape[-1]
    for b in range(ref.shape[1]):
        total = ref[n, b, pl.ds(at, count, stride=2), :] + ref[n, b, pl.ds(at + 1, count, stride=2), :]
        out[row : row + count, b * width : b * width + width] = total


def row_copies(ref, n, value):
    width = ref.shape[-1]
    count = value.shape[0]
    for b in range(ref.shape[1]):
        block = value[:, b * width : b * width + width]
        ref[n, b, pl.ds(0, count, stride=2), :] = block
        ref[n, b, pl.ds(1, count, stride=2), :] = block


def get_plane(ref, n):
    return jnp.concatenate([ref[n, b] for b in range(ref.shape[1])], axis=1)


def pack_middle_y(f1, eta1, low, high, up, down):
    def source(c, x):
        if x < 0:
            return low[4 * c + x + 4]
        if x < 4:
            return f1[c, x]
        return high[4 * c + x - 4]

    def viscosity(x):
        if x < 0:
            return low[12 + x + 5]
        if x < 4:
            return eta1[x + 1]
        return high[12 + x - 4]

    for i in range(12):
        rows = [source(c, i - 4) for c in range(3)]
        for out, at in ((up, 4), (down, 0)):
            out[i, 0:4] = rows[0][at : at + 4]
            out[i, 4:8] = rows[1][at : at + 4]
            out[12 + i + 1, 0:4] = rows[2][at : at + 4]
    for out in (up, down):
        out[12, 0:4] = jnp.zeros((4, f1.shape[-1]), F32)
        out[25, 0:4] = jnp.zeros((4, f1.shape[-1]), F32)
        out[27, 6:8] = jnp.zeros((2, f1.shape[-1]), F32)
    for j in range(14):
        eta = viscosity(j - 5)
        up[12 + j, 4:8] = eta[4:8]
        down[12 + j, 4:8] = eta[0:4]
        up[26 + j // 8, j % 8 : j % 8 + 1] = eta[3:4]
        down[26 + j // 8, j % 8 : j % 8 + 1] = eta[4:5]


def middle_down(f1, eta1, xlow, xhigh, ylow, yhigh, v1, g, cx, cf, own, up, down, far_up, far_down, eta, va, pairs, rest):
    nz = f1.shape[-1]
    blank = jnp.zeros((4, nz), F32)

    def source(c, x):
        if x < 0:
            return xlow[4 * c + x + 4]
        if x < 4:
            return f1[c, x]
        return xhigh[4 * c + x - 4]

    def viscosity(x):
        if x < 0:
            return xlow[12 + x + 5]
        if x < 4:
            return eta1[x + 1]
        return xhigh[12 + x - 4]

    for c in range(3):
        for i in range(12):
            g[c, i, 8:16] = source(c, i - 4)
            g[c, i, 0:4] = blank
            g[c, i, 20:24] = blank
            for side, at in ((ylow, 4), (yhigh, 16)):
                if c < 2:
                    g[c, i, at : at + 4] = side[i, 4 * c : 4 * c + 4]
                else:
                    g[c, i, at : at + 4] = side[13 + i, 0:4]
    for j in range(14):
        eta[j, 0:4] = blank
        eta[j, 20:24] = blank
        eta[j, 8:16] = viscosity(j - 5)
        eta[j, 4:8] = ylow[12 + j, 4:8]
        eta[j, 3:4] = ylow[26 + j // 8, j % 8 : j % 8 + 1]
        eta[j, 16:20] = yhigh[12 + j, 4:8]
        eta[j, 20:21] = yhigh[26 + j // 8, j % 8 : j % 8 + 1]

    coefficients(eta, cx, cf, 12, 0.25)

    plane = jnp.zeros((24, nz), F32)
    for c in range(3):
        for i in (0, 13):
            va[c, i] = plane
            v1[c, i] = plane

    def start(i, _):
        for c in range(3):
            va[c, i + 1] = cf[EI, i] * g[c, i]
        return 0

    lax.fori_loop(0, 12, start, 0)
    sweep(va, 5, g, 4, cx, cf, 4, v1, 5, -4, 8)

    def down_pair(k, _):
        for c in range(3):
            x = 2 * k
            total = residual(v1, 1, g, 0, cx, cf, 0, c, x) + residual(v1, 1, g, 0, cx, cf, 0, c, x + 1)
            put_plane(pairs, c * 6 + k, total)
        return 0

    lax.fori_loop(0, 6, down_pair, 0)

    def eta_pair(k, _):
        put_plane(pairs, 18 + k, eta[2 * k + 1] + eta[2 * k + 2])
        return 0

    lax.fori_loop(0, 6, eta_pair, 0)
    for k in range(6):
        for c in range(3):
            row_pairs(pairs, c * 6 + k, 8, 4, rest, 16 * k + 4 * c)
        row_pairs(pairs, 18 + k, 8, 4, rest, 16 * k + 12)
    coarse = split_dot(rest[...], pair_matrix(nz)) * 0.125
    for k in range(6):
        own[k] = coarse[16 * k : 16 * k + 16]
    for t in range(4):
        source_rows = own[t + 1, 0:12]
        up[t, 0:12] = source_rows
        up[t, 12:16] = own[t, 12:16]
        down[t, 0:12] = source_rows
        down[t, 12:16] = own[t + 2, 12:16]
        if t < 2:
            far_up[t, 0:12] = source_rows
            far_up[t, 12:16] = own[t, 12:16]
        else:
            far_down[t - 2, 0:12] = source_rows
            far_down[t - 2, 12:16] = own[t + 2, 12:16]


def pack_coarse_y(own, low2, low3, high2, high3, strip):
    strip[0, 0:12] = jnp.zeros((12, own.shape[-1]), F32)
    strip[17, 0:12] = jnp.zeros((12, own.shape[-1]), F32)
    for t in range(2):
        strip[1 + t, 0:12] = low3[t, 0:12]
        strip[t, 12:16] = low3[t, 12:16]
        strip[15 + t, 0:12] = high3[t, 0:12]
        strip[16 + t, 12:16] = high3[t, 12:16]
    for t in range(4):
        strip[3 + t, 0:12] = low2[t, 0:12]
        strip[2 + t, 12:16] = low2[t, 12:16]
        strip[7 + t, 0:12] = own[1 + t, 0:12]
        strip[11 + t, 0:12] = high2[t, 0:12]
        strip[12 + t, 12:16] = high2[t, 12:16]
    for t in range(6):
        strip[6 + t, 12:16] = own[t, 12:16]
    for plane, outer, mine in ((6, 5, 0), (11, 12, 5)):
        inside = strip[outer, 12:16] > 0.0
        for c in range(3):
            rows = slice(4 * c, 4 * c + 4)
            strip[plane, rows] = jnp.where(inside, strip[plane, rows], own[mine, rows])


def ascend(
    mid, ym1, ym2, yp1, yp2, v1, g1, cx1, cf1, v0, g0, cx0, cf0, out,
    eta2, g2, cx2, cf2, va2, vb2, rows2, wide1, va1, vb1, rows1, wide0, va0, vb0,
):
    nz2, nz1, nz0 = mid.shape[-1], v1.shape[-1], v0.shape[-1]
    blank = jnp.zeros((4, nz2), F32)
    for j in range(18):
        for n, side in enumerate((ym2, ym1, mid, yp1, yp2)):
            eta2[j, 4 * n : 4 * n + 4] = side[j, 12:16]
        eta2[j, 20:24] = blank
    for i in range(16):
        for c in range(3):
            for n, side in enumerate((ym2, ym1, mid, yp1, yp2)):
                g2[c, i, 4 * n : 4 * n + 4] = side[i + 1, 4 * c : 4 * c + 4]
            g2[c, i, 20:24] = blank
    coefficients(eta2, cx2, cf2, 16, 0.0625)

    def start(i, _):
        for c in range(3):
            va2[c, i] = cf2[EI, i] * g2[c, i]
        return 0

    lax.fori_loop(0, 16, start, 0)
    source, target = va2, vb2
    for s in range(1, 6):
        sweep(source, 0, g2, 0, cx2, cf2, 0, target, 0, s, 16 - s)
        source, target = target, source

    for c in range(3):
        for k in range(6):
            rows2[(c * 6 + k) * 16 : (c * 6 + k) * 16 + 16] = source[c, 5 + k, 4:20]
    spread = split_dot(rows2[...], copy_matrix(nz2))
    for n in range(18):
        block = spread[n * 16 : n * 16 + 12]
        row_copies(wide1, n, block)
    for c in range(3):
        for i in range(10):
            va1[c, i] = v1[c, i + 2] + get_plane(wide1, c * 6 + (i - 3) // 2 + 2)
    sweep(va1, 3, g1, 4, cx1, cf1, 4, vb1, 3, -2, 6)
    sweep(vb1, 3, g1, 4, cx1, cf1, 4, va1, 3, -1, 5)

    for c in range(3):
        for k in range(6):
            rows1[(c * 6 + k) * 16 : (c * 6 + k) * 16 + 16] = va1[c, 2 + k, 6:22]
    spread = split_dot(rows1[...], copy_matrix(nz1))
    for n in range(18):
        block = spread[n * 16 : n * 16 + 12]
        row_copies(wide0, n, block)

    def correct(k, _):
        for c in range(3):
            block = get_plane(wide0, c * 6 + k)
            va0[c, 2 * k] = v0[c, 2 * k] + block
            va0[c, 2 * k + 1] = v0[c, 2 * k + 1] + block
        return 0

    lax.fori_loop(0, 6, correct, 0)
    sweep(va0, 2, g0, 3, cx0, cf0, 3, vb0, 2, -1, 9)

    def final(x, _):
        for c in range(3):
            here, total = gather_sum(vb0, c, x + 2, cx0, cf0, x + 3)
            value = (1.0 / 3.0) * here + cf0[EI, x + 3] * (g0[c, x + 3] + total)
            out[c, x] = value[4:20]
        return 0

    lax.fori_loop(0, 8, final, 0)


def call(body, outs, *args, scratch=()):
    vmem = pl.BlockSpec(memory_space=pltpu.VMEM)
    return pl.pallas_call(
        body,
        out_shape=[jax.ShapeDtypeStruct(shape, F32) for shape in outs],
        in_specs=[vmem] * len(args),
        out_specs=[vmem] * len(outs),
        scratch_shapes=[pltpu.VMEM(shape, F32) for shape in scratch],
        compiler_params=pltpu.CompilerParams(vmem_limit_bytes=VMEM_LIMIT),
    )(*args)


def moved(array, axis, step):
    size = lax.axis_size(axis)
    pairs = [(i, i + step) for i in range(size) if 0 <= i + step < size]
    if not pairs:
        return jnp.zeros_like(array)
    return lax.ppermute(array, axis, pairs)


def per_device(forcing, phase_ids):
    z0 = forcing.shape[-1]
    z1, z2 = z0 // 2, z0 // 4
    up, down = call(pack_fine_x, [(13, 16, z0)] * 2, forcing, phase_ids)
    xlow, xhigh = moved(up, "gx", 1), moved(down, "gx", -1)
    up, down = call(pack_fine_y, [(24, 8, z0)] * 2, forcing, phase_ids, xlow, xhigh)
    ylow, yhigh = moved(up, "gy", 1), moved(down, "gy", -1)
    v0, g0, cx0, cf0, f1, eta1, up, down = call(
        fine_down,
        [(3, 12, 24, z0), (3, 14, 24, z0), (15, 24, z0), (6, 14, 24, z0), (3, 4, 8, z1), (6, 8, z1), (17, 8, z1), (17, 8, z1)],
        forcing, phase_ids, xlow, xhigh, ylow, yhigh,
        scratch=[(16, 24, z0), (3, 14, 24, z0), lane_blocks(18, z0), (144, z0)],
    )
    xlow, xhigh = moved(up, "gx", 1), moved(down, "gx", -1)
    up, down = call(pack_middle_y, [(28, 8, z1)] * 2, f1, eta1, xlow, xhigh)
    ylow, yhigh = moved(up, "gy", 1), moved(down, "gy", -1)
    v1, g1, cx1, cf1, own, up, down, far_up, far_down = call(
        middle_down,
        [(3, 14, 24, z1), (3, 12, 24, z1), (13, 24, z1), (6, 12, 24, z1), (6, 16, z2), (4, 16, z2), (4, 16, z2), (2, 16, z2), (2, 16, z2)],
        f1, eta1, xlow, xhigh, ylow, yhigh,
        scratch=[(14, 24, z1), (3, 14, 24, z1), lane_blocks(24, z1), (96, z1)],
    )
    low2, high2 = moved(up, "gx", 2), moved(down, "gx", -2)
    low3, high3 = moved(far_up, "gx", 3), moved(far_down, "gx", -3)
    (strip,) = call(pack_coarse_y, [(18, 16, z2)], own, low2, low3, high2, high3)
    ym1, yp1 = moved(strip, "gy", 1), moved(strip, "gy", -1)
    ym2, yp2 = moved(strip, "gy", 2), moved(strip, "gy", -2)
    (velocity,) = call(
        ascend,
        [forcing.shape],
        strip, ym1, ym2, yp1, yp2, v1, g1, cx1, cf1, v0, g0, cx0, cf0,
        scratch=[
            (18, 24, z2), (3, 16, 24, z2), (17, 24, z2), (6, 16, 24, z2), (3, 16, 24, z2), (3, 16, 24, z2),
            (288, z2), lane_blocks(18, z1), (3, 10, 24, z1), (3, 10, 24, z1),
            (288, z1), lane_blocks(18, z0), (3, 12, 24, z0), (3, 12, 24, z0),
        ],
    )
    return velocity


def solution(mesh):
    return jax.shard_map(
        per_device,
        mesh=mesh,
        in_specs=(P(None, "gx", "gy", None), P("gx", "gy", None)),
        out_specs=P(None, "gx", "gy", None),
        check_vma=False,
    )
```

```python
import functools

import jax
import jax.numpy as jnp
from jax import lax
from jax.experimental import pallas as pl
from jax.experimental.pallas import tpu as pltpu
from jax.sharding import PartitionSpec as P

F32 = jnp.float32
BF16 = jnp.bfloat16
WEIGHT = 2.0 / 3.0
VMEM_LIMIT = 40 * 1024 * 1024
U0, U1, U2 = 2, 4, 16


def materials(ids):
    eta = jnp.where(ids == 3, F32(4.0), F32(0.0))
    eta = jnp.where(ids == 2, F32(1.5), eta)
    eta = jnp.where(ids == 1, F32(0.6), eta)
    return jnp.where(ids == 0, F32(0.2), eta)


def lanes_of(shape):
    return lax.broadcasted_iota(jnp.int32, shape, len(shape) - 1)


def next_row(v):
    return pltpu.roll(v, v.shape[0] - 1, 0)


def last_row(v):
    return pltpu.roll(v, 1, 0)


def next_lane(v):
    return pltpu.roll(v, v.shape[1] - 1, 1)


def last_lane(v):
    return pltpu.roll(v, 1, 1)


def planes(count, body, unroll):
    steps = count // unroll if unroll < count else 0

    def step(n, _):
        for k in range(unroll):
            body(n * unroll + k)
        return 0

    if steps > 0:
        lax.fori_loop(0, steps, step, 0)
    for i in range(steps * unroll, count):
        body(i)


def kept(axis, step, value):
    place = lax.axis_index(axis) - step
    return jnp.where((place >= 0) & (place < lax.axis_size(axis)), value, 0.0)


def split_dot(rows, matrix):
    high = rows.astype(BF16)
    low = (rows - high.astype(F32)).astype(BF16)
    return jnp.dot(high, matrix, preferred_element_type=F32) + jnp.dot(
        low, matrix, preferred_element_type=F32
    )


def pair_matrix(fine):
    shape = (fine, fine // 2)
    row = lax.broadcasted_iota(jnp.int32, shape, 0)
    col = lax.broadcasted_iota(jnp.int32, shape, 1)
    return jnp.where((row == 2 * col) | (row == 2 * col + 1), F32(1), F32(0)).astype(BF16)


def copy_matrix(coarse):
    shape = (coarse, 2 * coarse)
    row = lax.broadcasted_iota(jnp.int32, shape, 0)
    col = lax.broadcasted_iota(jnp.int32, shape, 1)
    return jnp.where((col == 2 * row) | (col == 2 * row + 1), F32(1), F32(0)).astype(BF16)


YP, YM, ZP, ZM, DG, EI = range(6)


def coefficients(eta, cx, cf, layers, scale, unroll):
    half = 0.5 * scale

    def face(i):
        cx[i] = half * (eta[i] + eta[i + 1])

    planes(layers + 1, face, unroll)

    def body(i):
        here = eta[i + 1]
        lane = lanes_of(here.shape)
        first = lane == 0
        final = lane == here.shape[1] - 1
        yp, ym = next_row(here), last_row(here)
        zp, zm = next_lane(here), last_lane(here)
        cf[YP, i] = half * (here + yp)
        cf[YM, i] = half * (here + ym)
        cf[ZP, i] = jnp.where(final, 0.0, half * (here + zp))
        cf[ZM, i] = jnp.where(first, 0.0, half * (here + zm))

        def ghost(q):
            return jnp.where(q > 0.0, q, here)

        around = ghost(yp) + ghost(ym) + ghost(eta[i]) + ghost(eta[i + 2])
        around = around + jnp.where(final, here, zp) + jnp.where(first, here, zm)
        diag = scale * (3.0 * here + 0.5 * around)
        cf[DG, i] = diag
        cf[EI, i] = jnp.where(here > 0.0, WEIGHT / diag, 0.0)

    planes(layers, body, unroll)


def gather_sum(v, comp, i, cx, cf, k):
    here = v[comp, i]
    total = cx[k] * v[comp, i - 1] + cx[k + 1] * v[comp, i + 1]
    total = total + cf[YP, k] * next_row(here) + cf[YM, k] * last_row(here)
    total = total + cf[ZP, k] * next_lane(here) + cf[ZM, k] * last_lane(here)
    return here, total


def sweep(v, vo, g, go, cx, cf, co, out, oo, low, high, unroll):
    vo, go, co, oo = vo + low, go + low, co + low, oo + low

    def body(n):
        for comp in range(3):
            here, total = gather_sum(v, comp, n + vo, cx, cf, n + co)
            out[comp, n + oo] = (1.0 / 3.0) * here + cf[EI, n + co] * (g[comp, n + go] + total)

    planes(high - low, body, unroll)


def residual(v, vo, g, go, cx, cf, co, comp, x):
    here, total = gather_sum(v, comp, x + vo, cx, cf, x + co)
    return g[comp, x + go] - cf[DG, x + co] * here + total


def pack_fine_x(f, ids, up, down):
    for c in range(3):
        for k in range(3):
            up[3 * c + k] = f[c, 5 + k]
            down[3 * c + k] = f[c, k]
    for k in range(4):
        up[9 + k] = materials(ids[4 + k])
        down[9 + k] = materials(ids[k])


def fine_source(f, low, high, c, x):
    if x < 0:
        return low[3 * c + x + 3]
    if x < 8:
        return f[c, x]
    return high[3 * c + x - 8]


def fine_eta(ids, low, high, x):
    if x < 0:
        return low[9 + x + 4]
    if x < 8:
        return materials(ids[x])
    return high[9 + x - 8]


def pack_fine_y(f, ids, low, high, up, down):
    for i in range(14):
        rows = [fine_source(f, low, high, c, i - 3) for c in range(3)]
        for out, at in ((up, 13), (down, 0)):
            out[i, 0:3] = rows[0][at : at + 3]
            out[i, 3:6] = rows[1][at : at + 3]
            out[i, 6:8] = rows[2][at : at + 2]
            out[14 + i // 8, i % 8 : i % 8 + 1] = rows[2][at + 2 : at + 3]
    for out in (up, down):
        out[15, 6:8] = jnp.zeros((2, f.shape[-1]), F32)
    for j in range(16):
        eta = fine_eta(ids, low, high, j - 4)
        at = 4 * (j % 2)
        up[16 + j // 2, at : at + 4] = eta[12:16]
        down[16 + j // 2, at : at + 4] = eta[0:4]


def fine_down(f, ids, xlow, xhigh, ylow, yhigh, v0, g, cx, cf, f1, eta1, up, down, eta, va, pairs, rest):
    nz = f.shape[-1]
    blank = jnp.zeros((1, nz), F32)
    for c in range(3):
        for i in range(14):
            g[c, i, 4:20] = fine_source(f, xlow, xhigh, c, i - 3)
            for side, at in ((ylow, 1), (yhigh, 20)):
                if c < 2:
                    g[c, i, at : at + 3] = side[i, 3 * c : 3 * c + 3]
                else:
                    g[c, i, at : at + 2] = side[i, 6:8]
                    g[c, i, at + 2 : at + 3] = side[14 + i // 8, i % 8 : i % 8 + 1]
            g[c, i, 0:1] = blank
            g[c, i, 23:24] = blank
    for j in range(16):
        eta[j, 4:20] = fine_eta(ids, xlow, xhigh, j - 4)
        at = 4 * (j % 2)
        eta[j, 0:4] = ylow[16 + j // 2, at : at + 4]
        eta[j, 20:24] = yhigh[16 + j // 2, at : at + 4]

    coefficients(eta, cx, cf, 14, 1.0, U0)

    def start(i):
        for c in range(3):
            va[c, i] = cf[EI, i] * g[c, i]

    planes(14, start, U0)
    sweep(va, 3, g, 3, cx, cf, 3, v0, 2, -2, 10, U0)

    def down_pair(k):
        for c in range(3):
            x = 2 * k
            total = residual(v0, 2, g, 3, cx, cf, 3, c, x) + residual(v0, 2, g, 3, cx, cf, 3, c, x + 1)
            put_plane(pairs, c * 4 + k, total)

    planes(4, down_pair, U0)

    def eta_pair(k):
        put_plane(pairs, 12 + k, eta[2 * k + 2] + eta[2 * k + 3])

    planes(6, eta_pair, U0)
    for n in range(18):
        row_pairs(pairs, n, 4, 8, rest, n * 8)
    coarse = split_dot(rest[...], pair_matrix(nz)) * 0.125
    for n in range(12):
        block = coarse[n * 8 : n * 8 + 8]
        f1[n // 4, n % 4] = block
        up[n] = block
        down[n] = block
    for n in range(6):
        block = coarse[96 + n * 8 : 96 + n * 8 + 8]
        eta1[n] = block
        if n < 5:
            up[12 + n] = block
        if n > 0:
            down[12 + n - 1] = block


def lane_blocks(planes, nz):
    width = min(nz, 128)
    return (planes, nz // width, 24, width)


def put_plane(ref, n, value):
    width = ref.shape[-1]
    for b in range(ref.shape[1]):
        ref[n, b] = value[:, b * width : b * width + width]


def row_pairs(ref, n, at, count, out, row):
    width = ref.shape[-1]
    for b in range(ref.shape[1]):
        total = ref[n, b, pl.ds(at, count, stride=2), :] + ref[n, b, pl.ds(at + 1, count, stride=2), :]
        out[row : row + count, b * width : b * width + width] = total


def row_copies(ref, n, value):
    width = ref.shape[-1]
    count = value.shape[0]
    for b in range(ref.shape[1]):
        block = value[:, b * width : b * width + width]
        ref[n, b, pl.ds(0, count, stride=2), :] = block
        ref[n, b, pl.ds(1, count, stride=2), :] = block


def get_plane(ref, n):
    return jnp.concatenate([ref[n, b] for b in range(ref.shape[1])], axis=1)


def pack_middle_y(f1, eta1, low, high, up, down):
    def source(c, x):
        if x < 0:
            return kept("gx", 1, low[4 * c + x + 4])
        if x < 4:
            return f1[c, x]
        return kept("gx", -1, high[4 * c + x - 4])

    def viscosity(x):
        if x < 0:
            return kept("gx", 1, low[12 + x + 5])
        if x < 4:
            return eta1[x + 1]
        return kept("gx", -1, high[12 + x - 4])

    for i in range(12):
        rows = [source(c, i - 4) for c in range(3)]
        for out, at in ((up, 4), (down, 0)):
            out[i, 0:4] = rows[0][at : at + 4]
            out[i, 4:8] = rows[1][at : at + 4]
            out[12 + i + 1, 0:4] = rows[2][at : at + 4]
    for out in (up, down):
        out[12, 0:4] = jnp.zeros((4, f1.shape[-1]), F32)
        out[25, 0:4] = jnp.zeros((4, f1.shape[-1]), F32)
        out[27, 6:8] = jnp.zeros((2, f1.shape[-1]), F32)
    for j in range(14):
        eta = viscosity(j - 5)
        up[12 + j, 4:8] = eta[4:8]
        down[12 + j, 4:8] = eta[0:4]
        up[26 + j // 8, j % 8 : j % 8 + 1] = eta[3:4]
        down[26 + j // 8, j % 8 : j % 8 + 1] = eta[4:5]


def middle_down(f1, eta1, xlow, xhigh, ylow, yhigh, v1, g, cx, cf, own, up, down, far_up, far_down, eta, va, pairs, rest):
    nz = f1.shape[-1]
    blank = jnp.zeros((4, nz), F32)

    def source(c, x):
        if x < 0:
            return kept("gx", 1, xlow[4 * c + x + 4])
        if x < 4:
            return f1[c, x]
        return kept("gx", -1, xhigh[4 * c + x - 4])

    def viscosity(x):
        if x < 0:
            return kept("gx", 1, xlow[12 + x + 5])
        if x < 4:
            return eta1[x + 1]
        return kept("gx", -1, xhigh[12 + x - 4])

    for c in range(3):
        for i in range(12):
            g[c, i, 8:16] = source(c, i - 4)
            g[c, i, 0:4] = blank
            g[c, i, 20:24] = blank
            for side, at, step in ((ylow, 4, 1), (yhigh, 16, -1)):
                rows = side[i, 4 * c : 4 * c + 4] if c < 2 else side[13 + i, 0:4]
                g[c, i, at : at + 4] = kept("gy", step, rows)
    for j in range(14):
        eta[j, 0:4] = blank
        eta[j, 20:24] = blank
        eta[j, 8:16] = viscosity(j - 5)
        eta[j, 4:8] = kept("gy", 1, ylow[12 + j, 4:8])
        eta[j, 3:4] = kept("gy", 1, ylow[26 + j // 8, j % 8 : j % 8 + 1])
        eta[j, 16:20] = kept("gy", -1, yhigh[12 + j, 4:8])
        eta[j, 20:21] = kept("gy", -1, yhigh[26 + j // 8, j % 8 : j % 8 + 1])

    coefficients(eta, cx, cf, 12, 0.25, U1)

    plane = jnp.zeros((24, nz), F32)
    for c in range(3):
        for i in (0, 13):
            va[c, i] = plane
            v1[c, i] = plane

    def start(i):
        for c in range(3):
            va[c, i + 1] = cf[EI, i] * g[c, i]

    planes(12, start, U1)
    sweep(va, 5, g, 4, cx, cf, 4, v1, 5, -4, 8, U1)

    def down_pair(k):
        for c in range(3):
            x = 2 * k
            total = residual(v1, 1, g, 0, cx, cf, 0, c, x) + residual(v1, 1, g, 0, cx, cf, 0, c, x + 1)
            put_plane(pairs, c * 6 + k, total)

    planes(6, down_pair, U1)

    def eta_pair(k):
        put_plane(pairs, 18 + k, eta[2 * k + 1] + eta[2 * k + 2])

    planes(6, eta_pair, U1)
    for k in range(6):
        for c in range(3):
            row_pairs(pairs, c * 6 + k, 8, 4, rest, 16 * k + 4 * c)
        row_pairs(pairs, 18 + k, 8, 4, rest, 16 * k + 12)
    coarse = split_dot(rest[...], pair_matrix(nz)) * 0.125
    for k in range(6):
        own[k] = coarse[16 * k : 16 * k + 16]
    for t in range(4):
        source_rows = own[t + 1, 0:12]
        up[t, 0:12] = source_rows
        up[t, 12:16] = own[t, 12:16]
        down[t, 0:12] = source_rows
        down[t, 12:16] = own[t + 2, 12:16]
        if t < 2:
            far_up[t, 0:12] = source_rows
            far_up[t, 12:16] = own[t, 12:16]
        else:
            far_down[t - 2, 0:12] = source_rows
            far_down[t - 2, 12:16] = own[t + 2, 12:16]


def pack_coarse_y(own, low2, low3, high2, high3, strip):
    strip[0, 0:12] = jnp.zeros((12, own.shape[-1]), F32)
    strip[17, 0:12] = jnp.zeros((12, own.shape[-1]), F32)
    for t in range(2):
        rows = kept("gx", 3, low3[t])
        strip[1 + t, 0:12] = rows[0:12]
        strip[t, 12:16] = rows[12:16]
        rows = kept("gx", -3, high3[t])
        strip[15 + t, 0:12] = rows[0:12]
        strip[16 + t, 12:16] = rows[12:16]
    for t in range(4):
        rows = kept("gx", 2, low2[t])
        strip[3 + t, 0:12] = rows[0:12]
        strip[2 + t, 12:16] = rows[12:16]
        strip[7 + t, 0:12] = own[1 + t, 0:12]
        rows = kept("gx", -2, high2[t])
        strip[11 + t, 0:12] = rows[0:12]
        strip[12 + t, 12:16] = rows[12:16]
    for t in range(6):
        strip[6 + t, 12:16] = own[t, 12:16]
    for plane, outer, mine in ((6, 5, 0), (11, 12, 5)):
        inside = strip[outer, 12:16] > 0.0
        for c in range(3):
            rows = slice(4 * c, 4 * c + 4)
            strip[plane, rows] = jnp.where(inside, strip[plane, rows], own[mine, rows])


def ascend(
    mid, ym1, ym2, yp1, yp2, v1, g1, cx1, cf1, v0, g0, cx0, cf0, out,
    eta2, g2, cx2, cf2, va2, vb2, rows2, wide1, va1, vb1, rows1, wide0, va0, vb0,
):
    nz2, nz1, nz0 = mid.shape[-1], v1.shape[-1], v0.shape[-1]
    blank = jnp.zeros((4, nz2), F32)
    sides = ((ym2, 2), (ym1, 1), (mid, 0), (yp1, -1), (yp2, -2))
    for j in range(18):
        for n, (side, step) in enumerate(sides):
            rows = kept("gy", step, side[j]) if step else side[j]
            eta2[j, 4 * n : 4 * n + 4] = rows[12:16]
            if 1 <= j <= 16:
                for c in range(3):
                    g2[c, j - 1, 4 * n : 4 * n + 4] = rows[4 * c : 4 * c + 4]
        eta2[j, 20:24] = blank
        if 1 <= j <= 16:
            for c in range(3):
                g2[c, j - 1, 20:24] = blank
    coefficients(eta2, cx2, cf2, 16, 0.0625, U2)

    def start(i):
        for c in range(3):
            va2[c, i] = cf2[EI, i] * g2[c, i]

    planes(16, start, U2)
    source, target = va2, vb2
    for s in range(1, 6):
        sweep(source, 0, g2, 0, cx2, cf2, 0, target, 0, s, 16 - s, U2)
        source, target = target, source

    for c in range(3):
        for k in range(6):
            rows2[(c * 6 + k) * 16 : (c * 6 + k) * 16 + 16] = source[c, 5 + k, 4:20]
    spread = split_dot(rows2[...], copy_matrix(nz2))
    for n in range(18):
        block = spread[n * 16 : n * 16 + 12]
        row_copies(wide1, n, block)
    for c in range(3):
        for i in range(10):
            va1[c, i] = v1[c, i + 2] + get_plane(wide1, c * 6 + (i - 3) // 2 + 2)
    sweep(va1, 3, g1, 4, cx1, cf1, 4, vb1, 3, -2, 6, U1)
    sweep(vb1, 3, g1, 4, cx1, cf1, 4, va1, 3, -1, 5, U1)

    for c in range(3):
        for k in range(6):
            rows1[(c * 6 + k) * 16 : (c * 6 + k) * 16 + 16] = va1[c, 2 + k, 6:22]
    spread = split_dot(rows1[...], copy_matrix(nz1))
    for n in range(18):
        block = spread[n * 16 : n * 16 + 12]
        row_copies(wide0, n, block)

    def correct(k):
        for c in range(3):
            block = get_plane(wide0, c * 6 + k)
            va0[c, 2 * k] = v0[c, 2 * k] + block
            va0[c, 2 * k + 1] = v0[c, 2 * k + 1] + block

    planes(6, correct, U0)
    sweep(va0, 2, g0, 3, cx0, cf0, 3, vb0, 2, -1, 9, U0)

    def final(x):
        for c in range(3):
            here, total = gather_sum(vb0, c, x + 2, cx0, cf0, x + 3)
            value = (1.0 / 3.0) * here + cf0[EI, x + 3] * (g0[c, x + 3] + total)
            out[c, x] = value[4:20]

    planes(8, final, U0)


def call(body, outs, *args, scratch=()):
    vmem = pl.BlockSpec(memory_space=pltpu.VMEM)
    return pl.pallas_call(
        body,
        out_shape=[jax.ShapeDtypeStruct(shape, F32) for shape in outs],
        in_specs=[vmem] * len(args),
        out_specs=[vmem] * len(outs),
        scratch_shapes=[pltpu.VMEM(shape, F32) for shape in scratch],
        compiler_params=pltpu.CompilerParams(vmem_limit_bytes=VMEM_LIMIT),
    )(*args)


def moved(array, axis, step):
    size = lax.axis_size(axis)
    return lax.ppermute(array, axis, [(i, i + step) for i in range(size) if 0 <= i + step < size])


def cycled(array, axis, step):
    size = lax.axis_size(axis)
    return lax.ppermute(array, axis, [(i, (i + step) % size) for i in range(size)])


def per_device(forcing, phase_ids):
    z0 = forcing.shape[-1]
    z1, z2 = z0 // 2, z0 // 4
    up, down = call(pack_fine_x, [(13, 16, z0)] * 2, forcing, phase_ids)
    xlow, xhigh = moved(up, "gx", 1), moved(down, "gx", -1)
    up, down = call(pack_fine_y, [(24, 8, z0)] * 2, forcing, phase_ids, xlow, xhigh)
    ylow, yhigh = moved(up, "gy", 1), moved(down, "gy", -1)
    v0, g0, cx0, cf0, f1, eta1, up, down = call(
        fine_down,
        [(3, 12, 24, z0), (3, 14, 24, z0), (15, 24, z0), (6, 14, 24, z0), (3, 4, 8, z1), (6, 8, z1), (17, 8, z1), (17, 8, z1)],
        forcing, phase_ids, xlow, xhigh, ylow, yhigh,
        scratch=[(16, 24, z0), (3, 14, 24, z0), lane_blocks(18, z0), (144, z0)],
    )
    xlow, xhigh = cycled(up, "gx", 1), cycled(down, "gx", -1)
    up, down = call(pack_middle_y, [(28, 8, z1)] * 2, f1, eta1, xlow, xhigh)
    ylow, yhigh = cycled(up, "gy", 1), cycled(down, "gy", -1)
    v1, g1, cx1, cf1, own, up, down, far_up, far_down = call(
        middle_down,
        [(3, 14, 24, z1), (3, 12, 24, z1), (13, 24, z1), (6, 12, 24, z1), (6, 16, z2), (4, 16, z2), (4, 16, z2), (2, 16, z2), (2, 16, z2)],
        f1, eta1, xlow, xhigh, ylow, yhigh,
        scratch=[(14, 24, z1), (3, 14, 24, z1), lane_blocks(24, z1), (96, z1)],
    )
    low2, high2 = cycled(up, "gx", 2), cycled(down, "gx", -2)
    low3, high3 = cycled(far_up, "gx", 3), cycled(far_down, "gx", -3)
    (strip,) = call(pack_coarse_y, [(18, 16, z2)], own, low2, low3, high2, high3)
    ym1, yp1 = cycled(strip, "gy", 1), cycled(strip, "gy", -1)
    ym2, yp2 = cycled(strip, "gy", 2), cycled(strip, "gy", -2)
    (velocity,) = call(
        ascend,
        [forcing.shape],
        strip, ym1, ym2, yp1, yp2, v1, g1, cx1, cf1, v0, g0, cx0, cf0,
        scratch=[
            (18, 24, z2), (3, 16, 24, z2), (17, 24, z2), (6, 16, 24, z2), (3, 16, 24, z2), (3, 16, 24, z2),
            (288, z2), lane_blocks(18, z1), (3, 10, 24, z1), (3, 10, 24, z1),
            (288, z1), lane_blocks(18, z0), (3, 12, 24, z0), (3, 12, 24, z0),
        ],
    )
    return velocity


def solution(mesh):
    return jax.shard_map(
        per_device,
        mesh=mesh,
        in_specs=(P(None, "gx", "gy", None), P("gx", "gy", None)),
        out_specs=P(None, "gx", "gy", None),
        check_vma=False,
    )
```

```python
import functools

import jax
import jax.numpy as jnp
from jax import lax
from jax.experimental import pallas as pl
from jax.experimental.pallas import tpu as pltpu
from jax.sharding import PartitionSpec as P

F32 = jnp.float32
BF16 = jnp.bfloat16
WEIGHT = 2.0 / 3.0
VMEM_LIMIT = 40 * 1024 * 1024
U0, U1, U2 = 2, 4, 16


def materials(ids):
    eta = jnp.where(ids == 3, F32(4.0), F32(0.0))
    eta = jnp.where(ids == 2, F32(1.5), eta)
    eta = jnp.where(ids == 1, F32(0.6), eta)
    return jnp.where(ids == 0, F32(0.2), eta)


def lanes_of(shape):
    return lax.broadcasted_iota(jnp.int32, shape, len(shape) - 1)


def next_row(v):
    return pltpu.roll(v, v.shape[0] - 1, 0)


def last_row(v):
    return pltpu.roll(v, 1, 0)


def next_lane(v):
    return pltpu.roll(v, v.shape[1] - 1, 1)


def last_lane(v):
    return pltpu.roll(v, 1, 1)


def planes(count, body, unroll):
    steps = count // unroll if unroll < count else 0

    def step(n, _):
        for k in range(unroll):
            body(n * unroll + k)
        return 0

    if steps > 0:
        lax.fori_loop(0, steps, step, 0)
    for i in range(steps * unroll, count):
        body(i)


def kept(axis, step, value):
    place = lax.axis_index(axis) - step
    return jnp.where((place >= 0) & (place < lax.axis_size(axis)), value, 0.0)


def split_dot(rows, matrix):
    high = rows.astype(BF16)
    low = (rows - high.astype(F32)).astype(BF16)
    return jnp.dot(high, matrix, preferred_element_type=F32) + jnp.dot(
        low, matrix, preferred_element_type=F32
    )


def pair_matrix(fine):
    shape = (fine, fine // 2)
    row = lax.broadcasted_iota(jnp.int32, shape, 0)
    col = lax.broadcasted_iota(jnp.int32, shape, 1)
    return jnp.where((row == 2 * col) | (row == 2 * col + 1), F32(1), F32(0)).astype(BF16)


def copy_matrix(coarse):
    shape = (coarse, 2 * coarse)
    row = lax.broadcasted_iota(jnp.int32, shape, 0)
    col = lax.broadcasted_iota(jnp.int32, shape, 1)
    return jnp.where((col == 2 * row) | (col == 2 * row + 1), F32(1), F32(0)).astype(BF16)


YP, YM, ZP, ZM, DG, EI = range(6)


def coefficients(eta, cx, cf, layers, scale, unroll):
    half = 0.5 * scale

    def face(i):
        cx[i] = half * (eta[i] + eta[i + 1])

    planes(layers + 1, face, unroll)

    def body(i):
        here = eta[i + 1]
        lane = lanes_of(here.shape)
        first = lane == 0
        final = lane == here.shape[1] - 1
        yp, ym = next_row(here), last_row(here)
        zp, zm = next_lane(here), last_lane(here)
        cf[YP, i] = half * (here + yp)
        cf[YM, i] = half * (here + ym)
        cf[ZP, i] = jnp.where(final, 0.0, half * (here + zp))
        cf[ZM, i] = jnp.where(first, 0.0, half * (here + zm))

        def ghost(q):
            return jnp.where(q > 0.0, q, here)

        around = ghost(yp) + ghost(ym) + ghost(eta[i]) + ghost(eta[i + 2])
        around = around + jnp.where(final, here, zp) + jnp.where(first, here, zm)
        diag = scale * (3.0 * here + 0.5 * around)
        cf[DG, i] = diag
        cf[EI, i] = jnp.where(here > 0.0, WEIGHT / diag, 0.0)

    planes(layers, body, unroll)


def gather_sum(v, comp, i, cx, cf, k):
    here = v[comp, i]
    total = cx[k] * v[comp, i - 1] + cx[k + 1] * v[comp, i + 1]
    total = total + cf[YP, k] * next_row(here) + cf[YM, k] * last_row(here)
    total = total + cf[ZP, k] * next_lane(here) + cf[ZM, k] * last_lane(here)
    return here, total


def sweep(v, vo, g, go, cx, cf, co, out, oo, low, high, unroll):
    vo, go, co, oo = vo + low, go + low, co + low, oo + low

    def body(n):
        for comp in range(3):
            here, total = gather_sum(v, comp, n + vo, cx, cf, n + co)
            out[comp, n + oo] = (1.0 / 3.0) * here + cf[EI, n + co] * (g[comp, n + go] + total)

    planes(high - low, body, unroll)


def residual(v, vo, g, go, cx, cf, co, comp, x):
    here, total = gather_sum(v, comp, x + vo, cx, cf, x + co)
    return g[comp, x + go] - cf[DG, x + co] * here + total


def pack_fine(f, ids, xup, xdown, yup, ydown):
    for c in range(3):
        for k in range(3):
            xup[3 * c + k] = f[c, 5 + k]
            xdown[3 * c + k] = f[c, k]
    for x in range(8):
        eta = materials(ids[x])
        if x < 4:
            xdown[9 + x] = eta
        else:
            xup[9 + x - 4] = eta
        for out, at, eta_at in ((yup, 13, 12), (ydown, 0, 0)):
            pack_rows(out, x, 8, [f[c, x, at : at + 3] for c in range(3)])
            put_eta_rows(out, 9, x, eta[eta_at : eta_at + 4])


def pack_rows(out, n, spill, rows):
    out[n, 0:3] = rows[0]
    out[n, 3:6] = rows[1]
    out[n, 6:8] = rows[2][0:2]
    out[spill + n // 8, n % 8 : n % 8 + 1] = rows[2][2:3]


def put_eta_rows(out, first, n, rows):
    at = 4 * (n % 2)
    out[first + n // 2, at : at + 4] = rows


def fine_source(f, low, high, c, x):
    if x < 0:
        return kept("gx", 1, low[3 * c + x + 3])
    if x < 8:
        return f[c, x]
    return kept("gx", -1, high[3 * c + x - 8])


def fine_eta(ids, low, high, x):
    if x < 0:
        return kept("gx", 1, low[9 + x + 4])
    if x < 8:
        return materials(ids[x])
    return kept("gx", -1, high[9 + x - 8])


def pack_corners(low, high, up, down):
    for n, x in enumerate((-3, -2, -1, 8, 9, 10)):
        rows = [fine_source(None, low, high, c, x) for c in range(3)]
        for out, at in ((up, 13), (down, 0)):
            pack_rows(out, n, 6, [row[at : at + 3] for row in rows])
    for n, x in enumerate((-4, -3, -2, -1, 8, 9, 10, 11)):
        eta = fine_eta(None, low, high, x)
        put_eta_rows(up, 7, n, eta[12:16])
        put_eta_rows(down, 7, n, eta[0:4])
    for out in (up, down):
        out[6, 6:8] = jnp.zeros((2, low.shape[-1]), F32)


def fine_down(f, ids, xlow, xhigh, ylow, yhigh, clow, chigh, v0, g, cx, cf, f1, eta1, up, down, eta, va, pairs, rest):
    nz = f.shape[-1]
    blank = jnp.zeros((1, nz), F32)
    for i in range(14):
        x = i - 3
        for c in range(3):
            g[c, i, 4:20] = fine_source(f, xlow, xhigh, c, x)
            g[c, i, 0:1] = blank
            g[c, i, 23:24] = blank
        for own, corner, at, step in ((ylow, clow, 1, 1), (yhigh, chigh, 20, -1)):
            if 0 <= x < 8:
                side, n, spill = own, x, 8
            else:
                side, n, spill = corner, (i if x < 0 else x - 5), 6
            tile = kept("gy", step, side[n])
            g[0, i, at : at + 3] = tile[0:3]
            g[1, i, at : at + 3] = tile[3:6]
            g[2, i, at : at + 2] = tile[6:8]
            g[2, i, at + 2 : at + 3] = kept("gy", step, side[spill, n : n + 1])
    for j in range(16):
        x = j - 4
        eta[j, 4:20] = fine_eta(ids, xlow, xhigh, x)
        for own, corner, row, step in ((ylow, clow, 0, 1), (yhigh, chigh, 20, -1)):
            if 0 <= x < 8:
                side, n, first = own, x, 9
            else:
                side, n, first = corner, (j if x < 0 else x - 4), 7
            at = 4 * (n % 2)
            eta[j, row : row + 4] = kept("gy", step, side[first + n // 2, at : at + 4])

    coefficients(eta, cx, cf, 14, 1.0, U0)

    def start(i):
        for c in range(3):
            va[c, i] = cf[EI, i] * g[c, i]

    planes(14, start, U0)
    sweep(va, 3, g, 3, cx, cf, 3, v0, 2, -2, 10, U0)

    def down_pair(k):
        for c in range(3):
            x = 2 * k
            total = residual(v0, 2, g, 3, cx, cf, 3, c, x) + residual(v0, 2, g, 3, cx, cf, 3, c, x + 1)
            put_plane(pairs, c * 4 + k, total)

    planes(4, down_pair, U0)

    def eta_pair(k):
        put_plane(pairs, 12 + k, eta[2 * k + 2] + eta[2 * k + 3])

    planes(6, eta_pair, U0)
    for n in range(18):
        row_pairs(pairs, n, 4, 8, rest, n * 8)
    coarse = split_dot(rest[...], pair_matrix(nz)) * 0.125
    for n in range(12):
        block = coarse[n * 8 : n * 8 + 8]
        f1[n // 4, n % 4] = block
        up[n] = block
        down[n] = block
    for n in range(6):
        block = coarse[96 + n * 8 : 96 + n * 8 + 8]
        eta1[n] = block
        if n < 5:
            up[12 + n] = block
        if n > 0:
            down[12 + n - 1] = block


def lane_blocks(planes, nz):
    width = min(nz, 128)
    return (planes, nz // width, 24, width)


def put_plane(ref, n, value):
    width = ref.shape[-1]
    for b in range(ref.shape[1]):
        ref[n, b] = value[:, b * width : b * width + width]


def row_pairs(ref, n, at, count, out, row):
    width = ref.shape[-1]
    for b in range(ref.shape[1]):
        total = ref[n, b, pl.ds(at, count, stride=2), :] + ref[n, b, pl.ds(at + 1, count, stride=2), :]
        out[row : row + count, b * width : b * width + width] = total


def row_copies(ref, n, value):
    width = ref.shape[-1]
    count = value.shape[0]
    for b in range(ref.shape[1]):
        block = value[:, b * width : b * width + width]
        ref[n, b, pl.ds(0, count, stride=2), :] = block
        ref[n, b, pl.ds(1, count, stride=2), :] = block


def get_plane(ref, n):
    return jnp.concatenate([ref[n, b] for b in range(ref.shape[1])], axis=1)


def pack_middle_y(f1, eta1, low, high, up, down):
    def source(c, x):
        if x < 0:
            return kept("gx", 1, low[4 * c + x + 4])
        if x < 4:
            return f1[c, x]
        return kept("gx", -1, high[4 * c + x - 4])

    def viscosity(x):
        if x < 0:
            return kept("gx", 1, low[12 + x + 5])
        if x < 4:
            return eta1[x + 1]
        return kept("gx", -1, high[12 + x - 4])

    for i in range(12):
        rows = [source(c, i - 4) for c in range(3)]
        for out, at in ((up, 4), (down, 0)):
            out[i, 0:4] = rows[0][at : at + 4]
            out[i, 4:8] = rows[1][at : at + 4]
            out[12 + i + 1, 0:4] = rows[2][at : at + 4]
    for out in (up, down):
        out[12, 0:4] = jnp.zeros((4, f1.shape[-1]), F32)
        out[25, 0:4] = jnp.zeros((4, f1.shape[-1]), F32)
        out[27, 6:8] = jnp.zeros((2, f1.shape[-1]), F32)
    for j in range(14):
        eta = viscosity(j - 5)
        up[12 + j, 4:8] = eta[4:8]
        down[12 + j, 4:8] = eta[0:4]
        up[26 + j // 8, j % 8 : j % 8 + 1] = eta[3:4]
        down[26 + j // 8, j % 8 : j % 8 + 1] = eta[4:5]


def middle_down(f1, eta1, xlow, xhigh, ylow, yhigh, v1, g, cx, cf, own, up, down, far_up, far_down, eta, va, pairs, rest):
    nz = f1.shape[-1]
    blank = jnp.zeros((4, nz), F32)

    def source(c, x):
        if x < 0:
            return kept("gx", 1, xlow[4 * c + x + 4])
        if x < 4:
            return f1[c, x]
        return kept("gx", -1, xhigh[4 * c + x - 4])

    def viscosity(x):
        if x < 0:
            return kept("gx", 1, xlow[12 + x + 5])
        if x < 4:
            return eta1[x + 1]
        return kept("gx", -1, xhigh[12 + x - 4])

    for c in range(3):
        for i in range(12):
            g[c, i, 8:16] = source(c, i - 4)
            g[c, i, 0:4] = blank
            g[c, i, 20:24] = blank
            for side, at, step in ((ylow, 4, 1), (yhigh, 16, -1)):
                rows = side[i, 4 * c : 4 * c + 4] if c < 2 else side[13 + i, 0:4]
                g[c, i, at : at + 4] = kept("gy", step, rows)
    for j in range(14):
        eta[j, 0:4] = blank
        eta[j, 20:24] = blank
        eta[j, 8:16] = viscosity(j - 5)
        eta[j, 4:8] = kept("gy", 1, ylow[12 + j, 4:8])
        eta[j, 3:4] = kept("gy", 1, ylow[26 + j // 8, j % 8 : j % 8 + 1])
        eta[j, 16:20] = kept("gy", -1, yhigh[12 + j, 4:8])
        eta[j, 20:21] = kept("gy", -1, yhigh[26 + j // 8, j % 8 : j % 8 + 1])

    coefficients(eta, cx, cf, 12, 0.25, U1)

    plane = jnp.zeros((24, nz), F32)
    for c in range(3):
        for i in (0, 13):
            va[c, i] = plane
            v1[c, i] = plane

    def start(i):
        for c in range(3):
            va[c, i + 1] = cf[EI, i] * g[c, i]

    planes(12, start, U1)
    sweep(va, 5, g, 4, cx, cf, 4, v1, 5, -4, 8, U1)

    def down_pair(k):
        for c in range(3):
            x = 2 * k
            total = residual(v1, 1, g, 0, cx, cf, 0, c, x) + residual(v1, 1, g, 0, cx, cf, 0, c, x + 1)
            put_plane(pairs, c * 6 + k, total)

    planes(6, down_pair, U1)

    def eta_pair(k):
        put_plane(pairs, 18 + k, eta[2 * k + 1] + eta[2 * k + 2])

    planes(6, eta_pair, U1)
    for k in range(6):
        for c in range(3):
            row_pairs(pairs, c * 6 + k, 8, 4, rest, 16 * k + 4 * c)
        row_pairs(pairs, 18 + k, 8, 4, rest, 16 * k + 12)
    coarse = split_dot(rest[...], pair_matrix(nz)) * 0.125
    for k in range(6):
        own[k] = coarse[16 * k : 16 * k + 16]
    for t in range(4):
        source_rows = own[t + 1, 0:12]
        up[t, 0:12] = source_rows
        up[t, 12:16] = own[t, 12:16]
        down[t, 0:12] = source_rows
        down[t, 12:16] = own[t + 2, 12:16]
        if t < 2:
            far_up[t, 0:12] = source_rows
            far_up[t, 12:16] = own[t, 12:16]
        else:
            far_down[t - 2, 0:12] = source_rows
            far_down[t - 2, 12:16] = own[t + 2, 12:16]


def pack_coarse_y(own, low2, low3, high2, high3, strip):
    strip[0, 0:12] = jnp.zeros((12, own.shape[-1]), F32)
    strip[17, 0:12] = jnp.zeros((12, own.shape[-1]), F32)
    for t in range(2):
        rows = kept("gx", 3, low3[t])
        strip[1 + t, 0:12] = rows[0:12]
        strip[t, 12:16] = rows[12:16]
        rows = kept("gx", -3, high3[t])
        strip[15 + t, 0:12] = rows[0:12]
        strip[16 + t, 12:16] = rows[12:16]
    for t in range(4):
        rows = kept("gx", 2, low2[t])
        strip[3 + t, 0:12] = rows[0:12]
        strip[2 + t, 12:16] = rows[12:16]
        strip[7 + t, 0:12] = own[1 + t, 0:12]
        rows = kept("gx", -2, high2[t])
        strip[11 + t, 0:12] = rows[0:12]
        strip[12 + t, 12:16] = rows[12:16]
    for t in range(6):
        strip[6 + t, 12:16] = own[t, 12:16]
    for plane, outer, mine in ((6, 5, 0), (11, 12, 5)):
        inside = strip[outer, 12:16] > 0.0
        for c in range(3):
            rows = slice(4 * c, 4 * c + 4)
            strip[plane, rows] = jnp.where(inside, strip[plane, rows], own[mine, rows])


def ascend(
    mid, ym1, ym2, yp1, yp2, v1, g1, cx1, cf1, v0, g0, cx0, cf0, out,
    eta2, g2, cx2, cf2, va2, vb2, rows2, wide1, va1, vb1, rows1, wide0, va0, vb0,
):
    nz2, nz1, nz0 = mid.shape[-1], v1.shape[-1], v0.shape[-1]
    blank = jnp.zeros((4, nz2), F32)
    sides = ((ym2, 2), (ym1, 1), (mid, 0), (yp1, -1), (yp2, -2))
    for j in range(18):
        for n, (side, step) in enumerate(sides):
            rows = kept("gy", step, side[j]) if step else side[j]
            eta2[j, 4 * n : 4 * n + 4] = rows[12:16]
            if 1 <= j <= 16:
                for c in range(3):
                    g2[c, j - 1, 4 * n : 4 * n + 4] = rows[4 * c : 4 * c + 4]
        eta2[j, 20:24] = blank
        if 1 <= j <= 16:
            for c in range(3):
                g2[c, j - 1, 20:24] = blank
    coefficients(eta2, cx2, cf2, 16, 0.0625, U2)

    def start(i):
        for c in range(3):
            va2[c, i] = cf2[EI, i] * g2[c, i]

    planes(16, start, U2)
    source, target = va2, vb2
    for s in range(1, 6):
        sweep(source, 0, g2, 0, cx2, cf2, 0, target, 0, s, 16 - s, U2)
        source, target = target, source

    for c in range(3):
        for k in range(6):
            rows2[(c * 6 + k) * 16 : (c * 6 + k) * 16 + 16] = source[c, 5 + k, 4:20]
    spread = split_dot(rows2[...], copy_matrix(nz2))
    for n in range(18):
        block = spread[n * 16 : n * 16 + 12]
        row_copies(wide1, n, block)
    for c in range(3):
        for i in range(10):
            va1[c, i] = v1[c, i + 2] + get_plane(wide1, c * 6 + (i - 3) // 2 + 2)
    sweep(va1, 3, g1, 4, cx1, cf1, 4, vb1, 3, -2, 6, U1)
    sweep(vb1, 3, g1, 4, cx1, cf1, 4, va1, 3, -1, 5, U1)

    for c in range(3):
        for k in range(6):
            rows1[(c * 6 + k) * 16 : (c * 6 + k) * 16 + 16] = va1[c, 2 + k, 6:22]
    spread = split_dot(rows1[...], copy_matrix(nz1))
    for n in range(18):
        block = spread[n * 16 : n * 16 + 12]
        row_copies(wide0, n, block)

    def correct(k):
        for c in range(3):
            block = get_plane(wide0, c * 6 + k)
            va0[c, 2 * k] = v0[c, 2 * k] + block
            va0[c, 2 * k + 1] = v0[c, 2 * k + 1] + block

    planes(6, correct, U0)
    sweep(va0, 2, g0, 3, cx0, cf0, 3, vb0, 2, -1, 9, U0)

    def final(x):
        for c in range(3):
            here, total = gather_sum(vb0, c, x + 2, cx0, cf0, x + 3)
            value = (1.0 / 3.0) * here + cf0[EI, x + 3] * (g0[c, x + 3] + total)
            out[c, x] = value[4:20]

    planes(8, final, U0)


def call(body, outs, *args, scratch=()):
    vmem = pl.BlockSpec(memory_space=pltpu.VMEM)
    return pl.pallas_call(
        body,
        out_shape=[jax.ShapeDtypeStruct(shape, F32) for shape in outs],
        in_specs=[vmem] * len(args),
        out_specs=[vmem] * len(outs),
        scratch_shapes=[pltpu.VMEM(shape, F32) for shape in scratch],
        compiler_params=pltpu.CompilerParams(vmem_limit_bytes=VMEM_LIMIT),
    )(*args)


def cycled(array, axis, step):
    size = lax.axis_size(axis)
    return lax.ppermute(array, axis, [(i, (i + step) % size) for i in range(size)])


def per_device(forcing, phase_ids):
    z0 = forcing.shape[-1]
    z1, z2 = z0 // 2, z0 // 4
    xup, xdown, yup, ydown = call(pack_fine, [(13, 16, z0)] * 2 + [(13, 8, z0)] * 2, forcing, phase_ids)
    xlow, xhigh = cycled(xup, "gx", 1), cycled(xdown, "gx", -1)
    ylow, yhigh = cycled(yup, "gy", 1), cycled(ydown, "gy", -1)
    up, down = call(pack_corners, [(11, 8, z0)] * 2, xlow, xhigh)
    clow, chigh = cycled(up, "gy", 1), cycled(down, "gy", -1)
    v0, g0, cx0, cf0, f1, eta1, up, down = call(
        fine_down,
        [(3, 12, 24, z0), (3, 14, 24, z0), (15, 24, z0), (6, 14, 24, z0), (3, 4, 8, z1), (6, 8, z1), (17, 8, z1), (17, 8, z1)],
        forcing, phase_ids, xlow, xhigh, ylow, yhigh, clow, chigh,
        scratch=[(16, 24, z0), (3, 14, 24, z0), lane_blocks(18, z0), (144, z0)],
    )
    xlow, xhigh = cycled(up, "gx", 1), cycled(down, "gx", -1)
    up, down = call(pack_middle_y, [(28, 8, z1)] * 2, f1, eta1, xlow, xhigh)
    ylow, yhigh = cycled(up, "gy", 1), cycled(down, "gy", -1)
    v1, g1, cx1, cf1, own, up, down, far_up, far_down = call(
        middle_down,
        [(3, 14, 24, z1), (3, 12, 24, z1), (13, 24, z1), (6, 12, 24, z1), (6, 16, z2), (4, 16, z2), (4, 16, z2), (2, 16, z2), (2, 16, z2)],
        f1, eta1, xlow, xhigh, ylow, yhigh,
        scratch=[(14, 24, z1), (3, 14, 24, z1), lane_blocks(24, z1), (96, z1)],
    )
    low2, high2 = cycled(up, "gx", 2), cycled(down, "gx", -2)
    low3, high3 = cycled(far_up, "gx", 3), cycled(far_down, "gx", -3)
    (strip,) = call(pack_coarse_y, [(18, 16, z2)], own, low2, low3, high2, high3)
    ym1, yp1 = cycled(strip, "gy", 1), cycled(strip, "gy", -1)
    ym2, yp2 = cycled(strip, "gy", 2), cycled(strip, "gy", -2)
    (velocity,) = call(
        ascend,
        [forcing.shape],
        strip, ym1, ym2, yp1, yp2, v1, g1, cx1, cf1, v0, g0, cx0, cf0,
        scratch=[
            (18, 24, z2), (3, 16, 24, z2), (17, 24, z2), (6, 16, 24, z2), (3, 16, 24, z2), (3, 16, 24, z2),
            (288, z2), lane_blocks(18, z1), (3, 10, 24, z1), (3, 10, 24, z1),
            (288, z1), lane_blocks(18, z0), (3, 12, 24, z0), (3, 12, 24, z0),
        ],
    )
    return velocity


def solution(mesh):
    return jax.shard_map(
        per_device,
        mesh=mesh,
        in_specs=(P(None, "gx", "gy", None), P("gx", "gy", None)),
        out_specs=P(None, "gx", "gy", None),
        check_vma=False,
    )
```

```python
import functools

import jax
import jax.numpy as jnp
from jax import lax
from jax.experimental import pallas as pl
from jax.experimental.pallas import tpu as pltpu
from jax.sharding import PartitionSpec as P

F32 = jnp.float32
BF16 = jnp.bfloat16
WEIGHT = 2.0 / 3.0
VMEM_LIMIT = 40 * 1024 * 1024
U0, U1, U2 = 2, 4, 16


def materials(ids):
    eta = jnp.where(ids == 3, F32(4.0), F32(0.0))
    eta = jnp.where(ids == 2, F32(1.5), eta)
    eta = jnp.where(ids == 1, F32(0.6), eta)
    return jnp.where(ids == 0, F32(0.2), eta)


def lanes_of(shape):
    return lax.broadcasted_iota(jnp.int32, shape, len(shape) - 1)


def next_row(v):
    return pltpu.roll(v, v.shape[0] - 1, 0)


def last_row(v):
    return pltpu.roll(v, 1, 0)


def next_lane(v):
    return pltpu.roll(v, v.shape[1] - 1, 1)


def last_lane(v):
    return pltpu.roll(v, 1, 1)


def planes(count, body, unroll):
    steps = count // unroll if unroll < count else 0

    def step(n, _):
        for k in range(unroll):
            body(n * unroll + k)
        return 0

    if steps > 0:
        lax.fori_loop(0, steps, step, 0)
    for i in range(steps * unroll, count):
        body(i)


def kept(axis, step, value):
    place = lax.axis_index(axis) - step
    return jnp.where((place >= 0) & (place < lax.axis_size(axis)), value, 0.0)


def split_dot(rows, matrix):
    high = rows.astype(BF16)
    low = (rows - high.astype(F32)).astype(BF16)
    return jnp.dot(high, matrix, preferred_element_type=F32) + jnp.dot(
        low, matrix, preferred_element_type=F32
    )


def pair_matrix(fine):
    shape = (fine, fine // 2)
    row = lax.broadcasted_iota(jnp.int32, shape, 0)
    col = lax.broadcasted_iota(jnp.int32, shape, 1)
    return jnp.where((row == 2 * col) | (row == 2 * col + 1), F32(1), F32(0)).astype(BF16)


def copy_matrix(coarse):
    shape = (coarse, 2 * coarse)
    row = lax.broadcasted_iota(jnp.int32, shape, 0)
    col = lax.broadcasted_iota(jnp.int32, shape, 1)
    return jnp.where((col == 2 * row) | (col == 2 * row + 1), F32(1), F32(0)).astype(BF16)


YP, YM, ZP, ZM, DG, EI = range(6)


def coefficients(eta, cx, cf, layers, scale, unroll):
    half = 0.5 * scale

    def face(i):
        cx[i] = half * (eta[i] + eta[i + 1])

    planes(layers + 1, face, unroll)

    def body(i):
        here = eta[i + 1]
        lane = lanes_of(here.shape)
        first = lane == 0
        final = lane == here.shape[1] - 1
        yp, ym = next_row(here), last_row(here)
        zp, zm = next_lane(here), last_lane(here)
        cf[YP, i] = half * (here + yp)
        cf[YM, i] = half * (here + ym)
        cf[ZP, i] = jnp.where(final, 0.0, half * (here + zp))
        cf[ZM, i] = jnp.where(first, 0.0, half * (here + zm))

        def ghost(q):
            return jnp.where(q > 0.0, q, here)

        around = ghost(yp) + ghost(ym) + ghost(eta[i]) + ghost(eta[i + 2])
        around = around + jnp.where(final, here, zp) + jnp.where(first, here, zm)
        diag = scale * (3.0 * here + 0.5 * around)
        cf[DG, i] = diag
        cf[EI, i] = jnp.where(here > 0.0, WEIGHT / diag, 0.0)

    planes(layers, body, unroll)


def gather_sum(v, comp, i, cx, cf, k):
    here = v[comp, i]
    total = cx[k] * v[comp, i - 1] + cx[k + 1] * v[comp, i + 1]
    total = total + cf[YP, k] * next_row(here) + cf[YM, k] * last_row(here)
    total = total + cf[ZP, k] * next_lane(here) + cf[ZM, k] * last_lane(here)
    return here, total


def sweep(v, vo, g, go, cx, cf, co, out, oo, low, high, unroll):
    vo, go, co, oo = vo + low, go + low, co + low, oo + low

    def body(n):
        for comp in range(3):
            here, total = gather_sum(v, comp, n + vo, cx, cf, n + co)
            out[comp, n + oo] = (1.0 / 3.0) * here + cf[EI, n + co] * (g[comp, n + go] + total)

    planes(high - low, body, unroll)


def residual(v, vo, g, go, cx, cf, co, comp, x):
    here, total = gather_sum(v, comp, x + vo, cx, cf, x + co)
    return g[comp, x + go] - cf[DG, x + co] * here + total


def pack_fine(f_in, ids_in, xup, xdown, yup, ydown, f, ids, arrived):
    copies = [pltpu.make_async_copy(ids_in.at[x : x + 2], ids.at[x : x + 2], arrived.at[8 + x // 2]) for x in (0, 2, 4, 6)]
    copies += [pltpu.make_async_copy(f_in.at[:, x], f.at[:, x], arrived.at[x]) for x in range(8)]
    for copy in copies:
        copy.start()
    for copy in copies:
        copy.wait()
    for c in range(3):
        for k in range(3):
            xup[3 * c + k] = f[c, 5 + k]
            xdown[3 * c + k] = f[c, k]
    for x in range(8):
        eta = materials(ids[x])
        if x < 4:
            xdown[9 + x] = eta
        else:
            xup[9 + x - 4] = eta
        for out, at, eta_at in ((yup, 13, 12), (ydown, 0, 0)):
            pack_rows(out, x, 8, [f[c, x, at : at + 3] for c in range(3)])
            put_eta_rows(out, 9, x, eta[eta_at : eta_at + 4])


def pack_rows(out, n, spill, rows):
    out[n, 0:3] = rows[0]
    out[n, 3:6] = rows[1]
    out[n, 6:8] = rows[2][0:2]
    out[spill + n // 8, n % 8 : n % 8 + 1] = rows[2][2:3]


def put_eta_rows(out, first, n, rows):
    at = 4 * (n % 2)
    out[first + n // 2, at : at + 4] = rows


def fine_source(f, low, high, c, x):
    if x < 0:
        return kept("gx", 1, low[3 * c + x + 3])
    if x < 8:
        return f[c, x]
    return kept("gx", -1, high[3 * c + x - 8])


def fine_eta(ids, low, high, x):
    if x < 0:
        return kept("gx", 1, low[9 + x + 4])
    if x < 8:
        return materials(ids[x])
    return kept("gx", -1, high[9 + x - 8])


def pack_corners(low, high, up, down):
    for n, x in enumerate((-3, -2, -1, 8, 9, 10)):
        rows = [fine_source(None, low, high, c, x) for c in range(3)]
        for out, at in ((up, 13), (down, 0)):
            pack_rows(out, n, 6, [row[at : at + 3] for row in rows])
    for n, x in enumerate((-4, -3, -2, -1, 8, 9, 10, 11)):
        eta = fine_eta(None, low, high, x)
        put_eta_rows(up, 7, n, eta[12:16])
        put_eta_rows(down, 7, n, eta[0:4])
    for out in (up, down):
        out[6, 6:8] = jnp.zeros((2, low.shape[-1]), F32)


def fine_down(f, ids, xlow, xhigh, ylow, yhigh, clow, chigh, v0, g, cx, cf, f1, eta1, up, down, eta, va, pairs, rest):
    nz = f.shape[-1]
    blank = jnp.zeros((1, nz), F32)
    for i in range(14):
        x = i - 3
        for c in range(3):
            g[c, i, 4:20] = fine_source(f, xlow, xhigh, c, x)
            g[c, i, 0:1] = blank
            g[c, i, 23:24] = blank
        for own, corner, at, step in ((ylow, clow, 1, 1), (yhigh, chigh, 20, -1)):
            if 0 <= x < 8:
                side, n, spill = own, x, 8
            else:
                side, n, spill = corner, (i if x < 0 else x - 5), 6
            tile = kept("gy", step, side[n])
            g[0, i, at : at + 3] = tile[0:3]
            g[1, i, at : at + 3] = tile[3:6]
            g[2, i, at : at + 2] = tile[6:8]
            g[2, i, at + 2 : at + 3] = kept("gy", step, side[spill, n : n + 1])
    for j in range(16):
        x = j - 4
        eta[j, 4:20] = fine_eta(ids, xlow, xhigh, x)
        for own, corner, row, step in ((ylow, clow, 0, 1), (yhigh, chigh, 20, -1)):
            if 0 <= x < 8:
                side, n, first = own, x, 9
            else:
                side, n, first = corner, (j if x < 0 else x - 4), 7
            at = 4 * (n % 2)
            eta[j, row : row + 4] = kept("gy", step, side[first + n // 2, at : at + 4])

    coefficients(eta, cx, cf, 14, 1.0, U0)

    def start(i):
        for c in range(3):
            va[c, i] = cf[EI, i] * g[c, i]

    planes(14, start, U0)
    sweep(va, 3, g, 3, cx, cf, 3, v0, 2, -2, 10, U0)

    def down_pair(k):
        for c in range(3):
            x = 2 * k
            total = residual(v0, 2, g, 3, cx, cf, 3, c, x) + residual(v0, 2, g, 3, cx, cf, 3, c, x + 1)
            put_plane(pairs, c * 4 + k, total)

    planes(4, down_pair, U0)

    def eta_pair(k):
        put_plane(pairs, 12 + k, eta[2 * k + 2] + eta[2 * k + 3])

    planes(6, eta_pair, U0)
    for n in range(18):
        row_pairs(pairs, n, 4, 8, rest, n * 8)
    coarse = split_dot(rest[...], pair_matrix(nz)) * 0.125
    for n in range(12):
        block = coarse[n * 8 : n * 8 + 8]
        f1[n // 4, n % 4] = block
        up[n] = block
        down[n] = block
    for n in range(6):
        block = coarse[96 + n * 8 : 96 + n * 8 + 8]
        eta1[n] = block
        if n < 5:
            up[12 + n] = block
        if n > 0:
            down[12 + n - 1] = block


def lane_blocks(planes, nz):
    width = min(nz, 128)
    return (planes, nz // width, 24, width)


def put_plane(ref, n, value):
    width = ref.shape[-1]
    for b in range(ref.shape[1]):
        ref[n, b] = value[:, b * width : b * width + width]


def row_pairs(ref, n, at, count, out, row):
    width = ref.shape[-1]
    for b in range(ref.shape[1]):
        total = ref[n, b, pl.ds(at, count, stride=2), :] + ref[n, b, pl.ds(at + 1, count, stride=2), :]
        out[row : row + count, b * width : b * width + width] = total


def row_copies(ref, n, value):
    width = ref.shape[-1]
    count = value.shape[0]
    for b in range(ref.shape[1]):
        block = value[:, b * width : b * width + width]
        ref[n, b, pl.ds(0, count, stride=2), :] = block
        ref[n, b, pl.ds(1, count, stride=2), :] = block


def get_plane(ref, n):
    return jnp.concatenate([ref[n, b] for b in range(ref.shape[1])], axis=1)


def pack_middle_y(f1, eta1, low, high, up, down):
    def source(c, x):
        if x < 0:
            return kept("gx", 1, low[4 * c + x + 4])
        if x < 4:
            return f1[c, x]
        return kept("gx", -1, high[4 * c + x - 4])

    def viscosity(x):
        if x < 0:
            return kept("gx", 1, low[12 + x + 5])
        if x < 4:
            return eta1[x + 1]
        return kept("gx", -1, high[12 + x - 4])

    for i in range(12):
        rows = [source(c, i - 4) for c in range(3)]
        for out, at in ((up, 4), (down, 0)):
            out[i, 0:4] = rows[0][at : at + 4]
            out[i, 4:8] = rows[1][at : at + 4]
            out[12 + i + 1, 0:4] = rows[2][at : at + 4]
    for out in (up, down):
        out[12, 0:4] = jnp.zeros((4, f1.shape[-1]), F32)
        out[25, 0:4] = jnp.zeros((4, f1.shape[-1]), F32)
        out[27, 6:8] = jnp.zeros((2, f1.shape[-1]), F32)
    for j in range(14):
        eta = viscosity(j - 5)
        up[12 + j, 4:8] = eta[4:8]
        down[12 + j, 4:8] = eta[0:4]
        up[26 + j // 8, j % 8 : j % 8 + 1] = eta[3:4]
        down[26 + j // 8, j % 8 : j % 8 + 1] = eta[4:5]


def middle_down(f1, eta1, xlow, xhigh, ylow, yhigh, v1, g, cx, cf, own, up, down, far_up, far_down, eta, va, pairs, rest):
    nz = f1.shape[-1]
    blank = jnp.zeros((4, nz), F32)

    def source(c, x):
        if x < 0:
            return kept("gx", 1, xlow[4 * c + x + 4])
        if x < 4:
            return f1[c, x]
        return kept("gx", -1, xhigh[4 * c + x - 4])

    def viscosity(x):
        if x < 0:
            return kept("gx", 1, xlow[12 + x + 5])
        if x < 4:
            return eta1[x + 1]
        return kept("gx", -1, xhigh[12 + x - 4])

    for c in range(3):
        for i in range(12):
            g[c, i, 8:16] = source(c, i - 4)
            g[c, i, 0:4] = blank
            g[c, i, 20:24] = blank
            for side, at, step in ((ylow, 4, 1), (yhigh, 16, -1)):
                rows = side[i, 4 * c : 4 * c + 4] if c < 2 else side[13 + i, 0:4]
                g[c, i, at : at + 4] = kept("gy", step, rows)
    for j in range(14):
        eta[j, 0:4] = blank
        eta[j, 20:24] = blank
        eta[j, 8:16] = viscosity(j - 5)
        eta[j, 4:8] = kept("gy", 1, ylow[12 + j, 4:8])
        eta[j, 3:4] = kept("gy", 1, ylow[26 + j // 8, j % 8 : j % 8 + 1])
        eta[j, 16:20] = kept("gy", -1, yhigh[12 + j, 4:8])
        eta[j, 20:21] = kept("gy", -1, yhigh[26 + j // 8, j % 8 : j % 8 + 1])

    coefficients(eta, cx, cf, 12, 0.25, U1)

    plane = jnp.zeros((24, nz), F32)
    for c in range(3):
        for i in (0, 13):
            va[c, i] = plane
            v1[c, i] = plane

    def start(i):
        for c in range(3):
            va[c, i + 1] = cf[EI, i] * g[c, i]

    planes(12, start, U1)
    sweep(va, 5, g, 4, cx, cf, 4, v1, 5, -4, 8, U1)

    def down_pair(k):
        for c in range(3):
            x = 2 * k
            total = residual(v1, 1, g, 0, cx, cf, 0, c, x) + residual(v1, 1, g, 0, cx, cf, 0, c, x + 1)
            put_plane(pairs, c * 6 + k, total)

    planes(6, down_pair, U1)

    def eta_pair(k):
        put_plane(pairs, 18 + k, eta[2 * k + 1] + eta[2 * k + 2])

    planes(6, eta_pair, U1)
    for k in range(6):
        for c in range(3):
            row_pairs(pairs, c * 6 + k, 8, 4, rest, 16 * k + 4 * c)
        row_pairs(pairs, 18 + k, 8, 4, rest, 16 * k + 12)
    coarse = split_dot(rest[...], pair_matrix(nz)) * 0.125
    for k in range(6):
        own[k] = coarse[16 * k : 16 * k + 16]
    for t in range(4):
        source_rows = own[t + 1, 0:12]
        up[t, 0:12] = source_rows
        up[t, 12:16] = own[t, 12:16]
        down[t, 0:12] = source_rows
        down[t, 12:16] = own[t + 2, 12:16]
        if t < 2:
            far_up[t, 0:12] = source_rows
            far_up[t, 12:16] = own[t, 12:16]
        else:
            far_down[t - 2, 0:12] = source_rows
            far_down[t - 2, 12:16] = own[t + 2, 12:16]


def pack_coarse_y(own, low2, low3, high2, high3, strip):
    strip[0, 0:12] = jnp.zeros((12, own.shape[-1]), F32)
    strip[17, 0:12] = jnp.zeros((12, own.shape[-1]), F32)
    for t in range(2):
        rows = kept("gx", 3, low3[t])
        strip[1 + t, 0:12] = rows[0:12]
        strip[t, 12:16] = rows[12:16]
        rows = kept("gx", -3, high3[t])
        strip[15 + t, 0:12] = rows[0:12]
        strip[16 + t, 12:16] = rows[12:16]
    for t in range(4):
        rows = kept("gx", 2, low2[t])
        strip[3 + t, 0:12] = rows[0:12]
        strip[2 + t, 12:16] = rows[12:16]
        strip[7 + t, 0:12] = own[1 + t, 0:12]
        rows = kept("gx", -2, high2[t])
        strip[11 + t, 0:12] = rows[0:12]
        strip[12 + t, 12:16] = rows[12:16]
    for t in range(6):
        strip[6 + t, 12:16] = own[t, 12:16]
    for plane, outer, mine in ((6, 5, 0), (11, 12, 5)):
        inside = strip[outer, 12:16] > 0.0
        for c in range(3):
            rows = slice(4 * c, 4 * c + 4)
            strip[plane, rows] = jnp.where(inside, strip[plane, rows], own[mine, rows])


def ascend(
    mid, ym1, ym2, yp1, yp2, v1, g1, cx1, cf1, v0, g0, cx0, cf0, out,
    eta2, g2, cx2, cf2, va2, vb2, rows2, wide1, va1, vb1, rows1, wide0, va0, vb0, result, sent,
):
    nz2, nz1, nz0 = mid.shape[-1], v1.shape[-1], v0.shape[-1]
    blank = jnp.zeros((4, nz2), F32)
    sides = ((ym2, 2), (ym1, 1), (mid, 0), (yp1, -1), (yp2, -2))
    for j in range(18):
        for n, (side, step) in enumerate(sides):
            rows = kept("gy", step, side[j]) if step else side[j]
            eta2[j, 4 * n : 4 * n + 4] = rows[12:16]
            if 1 <= j <= 16:
                for c in range(3):
                    g2[c, j - 1, 4 * n : 4 * n + 4] = rows[4 * c : 4 * c + 4]
        eta2[j, 20:24] = blank
        if 1 <= j <= 16:
            for c in range(3):
                g2[c, j - 1, 20:24] = blank
    coefficients(eta2, cx2, cf2, 16, 0.0625, U2)

    def start(i):
        for c in range(3):
            va2[c, i] = cf2[EI, i] * g2[c, i]

    planes(16, start, U2)
    source, target = va2, vb2
    for s in range(1, 6):
        sweep(source, 0, g2, 0, cx2, cf2, 0, target, 0, s, 16 - s, U2)
        source, target = target, source

    for c in range(3):
        for k in range(6):
            rows2[(c * 6 + k) * 16 : (c * 6 + k) * 16 + 16] = source[c, 5 + k, 4:20]
    spread = split_dot(rows2[...], copy_matrix(nz2))
    for n in range(18):
        block = spread[n * 16 : n * 16 + 12]
        row_copies(wide1, n, block)
    for c in range(3):
        for i in range(10):
            va1[c, i] = v1[c, i + 2] + get_plane(wide1, c * 6 + (i - 3) // 2 + 2)
    sweep(va1, 3, g1, 4, cx1, cf1, 4, vb1, 3, -2, 6, U1)
    sweep(vb1, 3, g1, 4, cx1, cf1, 4, va1, 3, -1, 5, U1)

    for c in range(3):
        for k in range(6):
            rows1[(c * 6 + k) * 16 : (c * 6 + k) * 16 + 16] = va1[c, 2 + k, 6:22]
    spread = split_dot(rows1[...], copy_matrix(nz1))
    for n in range(18):
        block = spread[n * 16 : n * 16 + 12]
        row_copies(wide0, n, block)

    def correct(k):
        for c in range(3):
            block = get_plane(wide0, c * 6 + k)
            va0[c, 2 * k] = v0[c, 2 * k] + block
            va0[c, 2 * k + 1] = v0[c, 2 * k + 1] + block

    planes(6, correct, U0)
    sweep(va0, 2, g0, 3, cx0, cf0, 3, vb0, 2, -1, 9, U0)

    def final(x):
        for c in range(3):
            here, total = gather_sum(vb0, c, x + 2, cx0, cf0, x + 3)
            value = (1.0 / 3.0) * here + cf0[EI, x + 3] * (g0[c, x + 3] + total)
            result[c, x] = value[4:20]
        pltpu.make_async_copy(result.at[:, x], out.at[:, x], sent.at[x]).start()

    planes(8, final, U0)
    for x in range(8):
        pltpu.make_async_copy(result.at[:, x], out.at[:, x], sent.at[x]).wait()


def call(body, outs, *args, scratch=(), copies=0, where_in=pltpu.VMEM, where_out=pltpu.VMEM):
    outs = [out if isinstance(out, jax.ShapeDtypeStruct) else jax.ShapeDtypeStruct(out, F32) for out in outs]
    scratch_shapes = [pltpu.VMEM(shape, F32) for shape in scratch]
    if copies:
        scratch_shapes.append(pltpu.SemaphoreType.DMA((copies,)))
    return pl.pallas_call(
        body,
        out_shape=outs,
        in_specs=[pl.BlockSpec(memory_space=where_in)] * len(args),
        out_specs=[pl.BlockSpec(memory_space=where_out)] * len(outs),
        scratch_shapes=scratch_shapes,
        compiler_params=pltpu.CompilerParams(vmem_limit_bytes=VMEM_LIMIT),
    )(*args)


def cycled(array, axis, step):
    size = lax.axis_size(axis)
    return lax.ppermute(array, axis, [(i, (i + step) % size) for i in range(size)])


def per_device(forcing, phase_ids):
    z0 = forcing.shape[-1]
    z1, z2 = z0 // 2, z0 // 4
    xup, xdown, yup, ydown, f0, ids0 = call(
        pack_fine,
        [(13, 16, z0)] * 2 + [(13, 8, z0)] * 2 + [forcing.shape, jax.ShapeDtypeStruct(phase_ids.shape, jnp.int32)],
        *(pltpu.with_memory_space_constraint(a, pltpu.HBM) for a in (forcing, phase_ids)), copies=12, where_in=pltpu.HBM,
    )
    xlow, xhigh = cycled(xup, "gx", 1), cycled(xdown, "gx", -1)
    ylow, yhigh = cycled(yup, "gy", 1), cycled(ydown, "gy", -1)
    up, down = call(pack_corners, [(11, 8, z0)] * 2, xlow, xhigh)
    clow, chigh = cycled(up, "gy", 1), cycled(down, "gy", -1)
    v0, g0, cx0, cf0, f1, eta1, up, down = call(
        fine_down,
        [(3, 12, 24, z0), (3, 14, 24, z0), (15, 24, z0), (6, 14, 24, z0), (3, 4, 8, z1), (6, 8, z1), (17, 8, z1), (17, 8, z1)],
        f0, ids0, xlow, xhigh, ylow, yhigh, clow, chigh,
        scratch=[(16, 24, z0), (3, 14, 24, z0), lane_blocks(18, z0), (144, z0)],
    )
    xlow, xhigh = cycled(up, "gx", 1), cycled(down, "gx", -1)
    up, down = call(pack_middle_y, [(28, 8, z1)] * 2, f1, eta1, xlow, xhigh)
    ylow, yhigh = cycled(up, "gy", 1), cycled(down, "gy", -1)
    v1, g1, cx1, cf1, own, up, down, far_up, far_down = call(
        middle_down,
        [(3, 14, 24, z1), (3, 12, 24, z1), (13, 24, z1), (6, 12, 24, z1), (6, 16, z2), (4, 16, z2), (4, 16, z2), (2, 16, z2), (2, 16, z2)],
        f1, eta1, xlow, xhigh, ylow, yhigh,
        scratch=[(14, 24, z1), (3, 14, 24, z1), lane_blocks(24, z1), (96, z1)],
    )
    low2, high2 = cycled(up, "gx", 2), cycled(down, "gx", -2)
    low3, high3 = cycled(far_up, "gx", 3), cycled(far_down, "gx", -3)
    (strip,) = call(pack_coarse_y, [(18, 16, z2)], own, low2, low3, high2, high3)
    ym1, yp1 = cycled(strip, "gy", 1), cycled(strip, "gy", -1)
    ym2, yp2 = cycled(strip, "gy", 2), cycled(strip, "gy", -2)
    (velocity,) = call(
        ascend,
        [forcing.shape],
        strip, ym1, ym2, yp1, yp2, v1, g1, cx1, cf1, v0, g0, cx0, cf0,
        scratch=[
            (18, 24, z2), (3, 16, 24, z2), (17, 24, z2), (6, 16, 24, z2), (3, 16, 24, z2), (3, 16, 24, z2),
            (288, z2), lane_blocks(18, z1), (3, 10, 24, z1), (3, 10, 24, z1),
            (288, z1), lane_blocks(18, z0), (3, 12, 24, z0), (3, 12, 24, z0), forcing.shape,
        ],
        copies=8,
        where_out=pltpu.HBM,
    )
    return velocity


def solution(mesh):
    return jax.shard_map(
        per_device,
        mesh=mesh,
        in_specs=(P(None, "gx", "gy", None), P("gx", "gy", None)),
        out_specs=P(None, "gx", "gy", None),
        check_vma=False,
    )
```

```python
import functools

import jax
import jax.numpy as jnp
from jax import lax
from jax.experimental import pallas as pl
from jax.experimental.pallas import tpu as pltpu
from jax.sharding import PartitionSpec as P

F32 = jnp.float32
BF16 = jnp.bfloat16
WEIGHT = 2.0 / 3.0
VMEM_LIMIT = 40 * 1024 * 1024
U0, U1, U2 = 2, 4, 16


def materials(ids):
    eta = jnp.where(ids == 3, F32(4.0), F32(0.0))
    eta = jnp.where(ids == 2, F32(1.5), eta)
    eta = jnp.where(ids == 1, F32(0.6), eta)
    return jnp.where(ids == 0, F32(0.2), eta)


def lanes_of(shape):
    return lax.broadcasted_iota(jnp.int32, shape, len(shape) - 1)


def next_row(v):
    return pltpu.roll(v, v.shape[0] - 1, 0)


def last_row(v):
    return pltpu.roll(v, 1, 0)


def next_lane(v):
    return pltpu.roll(v, v.shape[1] - 1, 1)


def last_lane(v):
    return pltpu.roll(v, 1, 1)


def planes(count, body, unroll):
    steps = count // unroll if unroll < count else 0

    def step(n, _):
        for k in range(unroll):
            body(n * unroll + k)
        return 0

    if steps > 0:
        lax.fori_loop(0, steps, step, 0)
    for i in range(steps * unroll, count):
        body(i)


def kept(axis, step, value):
    place = lax.axis_index(axis) - step
    return jnp.where((place >= 0) & (place < lax.axis_size(axis)), value, 0.0)


def split_dot(rows, matrix):
    high = rows.astype(BF16)
    low = (rows - high.astype(F32)).astype(BF16)
    return jnp.dot(high, matrix, preferred_element_type=F32) + jnp.dot(
        low, matrix, preferred_element_type=F32
    )


def pair_matrix(fine):
    shape = (fine, fine // 2)
    row = lax.broadcasted_iota(jnp.int32, shape, 0)
    col = lax.broadcasted_iota(jnp.int32, shape, 1)
    return jnp.where((row == 2 * col) | (row == 2 * col + 1), F32(1), F32(0)).astype(BF16)


def copy_matrix(coarse):
    shape = (coarse, 2 * coarse)
    row = lax.broadcasted_iota(jnp.int32, shape, 0)
    col = lax.broadcasted_iota(jnp.int32, shape, 1)
    return jnp.where((col == 2 * row) | (col == 2 * row + 1), F32(1), F32(0)).astype(BF16)


YP, YM, ZP, ZM, DG, EI = range(6)


def plane_coefficients(below, here, above, scale):
    half = 0.5 * scale
    lane = lanes_of(here.shape)
    first = lane == 0
    final = lane == here.shape[1] - 1
    yp, ym = next_row(here), last_row(here)
    zp, zm = next_lane(here), last_lane(here)

    def ghost(q):
        return jnp.where(q > 0.0, q, here)

    around = ghost(yp) + ghost(ym) + ghost(below) + ghost(above)
    around = around + jnp.where(final, here, zp) + jnp.where(first, here, zm)
    diag = scale * (3.0 * here + 0.5 * around)
    return (
        half * (here + yp),
        half * (here + ym),
        jnp.where(final, 0.0, half * (here + zp)),
        jnp.where(first, 0.0, half * (here + zm)),
        diag,
        jnp.where(here > 0.0, WEIGHT / diag, 0.0),
    )


def coefficients(eta, cx, cf, layers, scale, unroll):
    half = 0.5 * scale

    def face(i):
        cx[i] = half * (eta[i] + eta[i + 1])

    planes(layers + 1, face, unroll)

    def body(i):
        made = plane_coefficients(eta[i], eta[i + 1], eta[i + 2], scale)
        for n, value in enumerate(made):
            cf[n, i] = value

    planes(layers, body, unroll)


def gather_sum(v, comp, i, cx, cf, k):
    here = v[comp, i]
    total = cx[k] * v[comp, i - 1] + cx[k + 1] * v[comp, i + 1]
    total = total + cf[YP, k] * next_row(here) + cf[YM, k] * last_row(here)
    total = total + cf[ZP, k] * next_lane(here) + cf[ZM, k] * last_lane(here)
    return here, total


def sweep(v, vo, g, go, cx, cf, co, out, oo, low, high, unroll):
    vo, go, co, oo = vo + low, go + low, co + low, oo + low

    def body(n):
        for comp in range(3):
            here, total = gather_sum(v, comp, n + vo, cx, cf, n + co)
            out[comp, n + oo] = (1.0 / 3.0) * here + cf[EI, n + co] * (g[comp, n + go] + total)

    planes(high - low, body, unroll)


def residual(v, vo, g, go, cx, cf, co, comp, x):
    here, total = gather_sum(v, comp, x + vo, cx, cf, x + co)
    return g[comp, x + go] - cf[DG, x + co] * here + total


def pack_fine(f_in, ids_in, xup, xdown, yup, ydown, f, ids, arrived):
    copies = [pltpu.make_async_copy(ids_in.at[x : x + 2], ids.at[x : x + 2], arrived.at[8 + x // 2]) for x in (0, 2, 4, 6)]
    copies += [pltpu.make_async_copy(f_in.at[:, x], f.at[:, x], arrived.at[x]) for x in range(8)]
    for copy in copies:
        copy.start()
    for copy in copies:
        copy.wait()
    for c in range(3):
        for k in range(2):
            xup[2 * c + k] = f[c, 6 + k]
            xdown[2 * c + k] = f[c, k]
    for x in range(8):
        eta = materials(ids[x])
        if x < 3:
            xdown[6 + x] = eta
        if x > 4:
            xup[6 + x - 5] = eta
        for out, at, eta_at in ((yup, 13, 12), (ydown, 0, 0)):
            pack_rows(out, x, 8, [f[c, x, at : at + 3] for c in range(3)])
            put_eta_rows(out, 9, x, eta[eta_at : eta_at + 4])


def pack_rows(out, n, spill, rows):
    out[n, 0:3] = rows[0]
    out[n, 3:6] = rows[1]
    out[n, 6:8] = rows[2][0:2]
    out[spill + n // 8, n % 8 : n % 8 + 1] = rows[2][2:3]


def put_eta_rows(out, first, n, rows):
    at = 4 * (n % 2)
    out[first + n // 2, at : at + 4] = rows


def fine_source(f, low, high, c, x):
    if x < 0:
        return kept("gx", 1, low[2 * c + x + 2])
    if x < 8:
        return f[c, x]
    return kept("gx", -1, high[2 * c + x - 8])


def fine_eta(ids, low, high, x):
    if x < 0:
        return kept("gx", 1, low[6 + x + 3])
    if x < 8:
        return materials(ids[x])
    return kept("gx", -1, high[6 + x - 8])


def pack_corners(low, high, up, down):
    for n, x in enumerate((-2, -1, 8, 9)):
        rows = [fine_source(None, low, high, c, x) for c in range(3)]
        for out, at in ((up, 13), (down, 0)):
            pack_rows(out, n, 4, [row[at : at + 3] for row in rows])
    for n, x in enumerate((-3, -2, -1, 8, 9, 10)):
        eta = fine_eta(None, low, high, x)
        put_eta_rows(up, 5, n, eta[12:16])
        put_eta_rows(down, 5, n, eta[0:4])
    for out in (up, down):
        out[4, 4:8] = jnp.zeros((4, low.shape[-1]), F32)


def fine_down(f, ids, xlow, xhigh, ylow, yhigh, clow, chigh, v0, va, g, eta, cx, cf, f1, eta1, up, down, pairs, rest):
    nz = f.shape[-1]
    blank = jnp.zeros((1, nz), F32)
    for i in range(12):
        x = i - 2
        for c in range(3):
            g[c, i, 4:20] = fine_source(f, xlow, xhigh, c, x)
            g[c, i, 0:1] = blank
            g[c, i, 23:24] = blank
        for own, corner, at, step in ((ylow, clow, 1, 1), (yhigh, chigh, 20, -1)):
            if 0 <= x < 8:
                side, n, spill = own, x, 8
            else:
                side, n, spill = corner, (i if x < 0 else x - 6), 4
            tile = kept("gy", step, side[n])
            g[0, i, at : at + 3] = tile[0:3]
            g[1, i, at : at + 3] = tile[3:6]
            g[2, i, at : at + 2] = tile[6:8]
            g[2, i, at + 2 : at + 3] = kept("gy", step, side[spill, n : n + 1])
    for j in range(14):
        x = j - 3
        eta[j, 4:20] = fine_eta(ids, xlow, xhigh, x)
        for own, corner, row, step in ((ylow, clow, 0, 1), (yhigh, chigh, 20, -1)):
            if 0 <= x < 8:
                side, n, first = own, x, 9
            else:
                side, n, first = corner, (j if x < 0 else x - 5), 5
            at = 4 * (n % 2)
            eta[j, row : row + 4] = kept("gy", step, side[first + n // 2, at : at + 4])

    coefficients(eta, cx, cf, 12, 1.0, U0)

    def start(i):
        for c in range(3):
            va[c, i] = cf[EI, i] * g[c, i]

    planes(12, start, U0)
    sweep(va, 2, g, 2, cx, cf, 2, v0, 1, -1, 9, U0)

    def down_pair(k):
        for c in range(3):
            x = 2 * k
            total = residual(v0, 1, g, 2, cx, cf, 2, c, x) + residual(v0, 1, g, 2, cx, cf, 2, c, x + 1)
            put_plane(pairs, c * 4 + k, total)

    planes(4, down_pair, U0)

    def eta_pair(k):
        put_plane(pairs, 12 + k, eta[2 * k + 1] + eta[2 * k + 2])

    planes(6, eta_pair, U0)
    for n in range(18):
        row_pairs(pairs, n, 4, 8, rest, n * 8)
    coarse = split_dot(rest[...], pair_matrix(nz)) * 0.125
    for n in range(12):
        block = coarse[n * 8 : n * 8 + 8]
        f1[n // 4, n % 4] = block
        up[n] = block
        down[n] = block
    for n in range(6):
        block = coarse[96 + n * 8 : 96 + n * 8 + 8]
        eta1[n] = block
        if n < 5:
            up[12 + n] = block
        if n > 0:
            down[12 + n - 1] = block


def lane_blocks(planes, nz):
    width = min(nz, 128)
    return (planes, nz // width, 24, width)


def put_plane(ref, n, value):
    width = ref.shape[-1]
    for b in range(ref.shape[1]):
        ref[n, b] = value[:, b * width : b * width + width]


def row_pairs(ref, n, at, count, out, row):
    width = ref.shape[-1]
    for b in range(ref.shape[1]):
        total = ref[n, b, pl.ds(at, count, stride=2), :] + ref[n, b, pl.ds(at + 1, count, stride=2), :]
        out[row : row + count, b * width : b * width + width] = total


def row_copies(ref, n, value):
    width = ref.shape[-1]
    count = value.shape[0]
    for b in range(ref.shape[1]):
        block = value[:, b * width : b * width + width]
        ref[n, b, pl.ds(0, count, stride=2), :] = block
        ref[n, b, pl.ds(1, count, stride=2), :] = block


def get_plane(ref, n):
    return jnp.concatenate([ref[n, b] for b in range(ref.shape[1])], axis=1)


def fine_rim(low, high, va, g, eta, cx, cf, rim):
    nz = low.shape[-1]
    blank = jnp.zeros((4, nz), F32)

    for n, (side, step) in enumerate(((low, 1), (high, -1))):
        rows = [jnp.concatenate([blank, kept("gx", step, side[k]), blank], axis=0) for k in range(4)]
        edge, k, inner, face, far = ((0, 0, 1, 1, 0), (13, 11, 10, 11, 12))[n]
        weight = plane_coefficients(rows[3], eta[edge], eta[1 if n == 0 else 12], 1.0)[EI]
        for c in range(3):
            here = va[c, k]
            total = cx[far] * (weight * rows[c]) + cx[face] * va[c, inner]
            total = total + cf[YP, k] * next_row(here) + cf[YM, k] * last_row(here)
            total = total + cf[ZP, k] * next_lane(here) + cf[ZM, k] * last_lane(here)
            rim[c, n] = (1.0 / 3.0) * here + cf[EI, k] * (g[c, k] + total)


def pack_middle_y(f1, eta1, low, high, f, ids, up, down, late_up, late_down):
    for c in range(3):
        late_up[c] = f[c, 5]
        late_down[c] = f[c, 2]
    late_up[3] = materials(ids[4])
    late_down[3] = materials(ids[3])

    def source(c, x):
        if x < 0:
            return kept("gx", 1, low[4 * c + x + 4])
        if x < 4:
            return f1[c, x]
        return kept("gx", -1, high[4 * c + x - 4])

    def viscosity(x):
        if x < 0:
            return kept("gx", 1, low[12 + x + 5])
        if x < 4:
            return eta1[x + 1]
        return kept("gx", -1, high[12 + x - 4])

    for i in range(12):
        rows = [source(c, i - 4) for c in range(3)]
        for out, at in ((up, 4), (down, 0)):
            out[i, 0:4] = rows[0][at : at + 4]
            out[i, 4:8] = rows[1][at : at + 4]
            out[12 + i + 1, 0:4] = rows[2][at : at + 4]
    for out in (up, down):
        out[12, 0:4] = jnp.zeros((4, f1.shape[-1]), F32)
        out[25, 0:4] = jnp.zeros((4, f1.shape[-1]), F32)
        out[27, 6:8] = jnp.zeros((2, f1.shape[-1]), F32)
    for j in range(14):
        eta = viscosity(j - 5)
        up[12 + j, 4:8] = eta[4:8]
        down[12 + j, 4:8] = eta[0:4]
        up[26 + j // 8, j % 8 : j % 8 + 1] = eta[3:4]
        down[26 + j // 8, j % 8 : j % 8 + 1] = eta[4:5]


def middle_down(f1, eta1, xlow, xhigh, ylow, yhigh, v1, g, cx, cf, own, up, down, far_up, far_down, eta, va, pairs, rest):
    nz = f1.shape[-1]
    blank = jnp.zeros((4, nz), F32)

    def source(c, x):
        if x < 0:
            return kept("gx", 1, xlow[4 * c + x + 4])
        if x < 4:
            return f1[c, x]
        return kept("gx", -1, xhigh[4 * c + x - 4])

    def viscosity(x):
        if x < 0:
            return kept("gx", 1, xlow[12 + x + 5])
        if x < 4:
            return eta1[x + 1]
        return kept("gx", -1, xhigh[12 + x - 4])

    for c in range(3):
        for i in range(12):
            g[c, i, 8:16] = source(c, i - 4)
            g[c, i, 0:4] = blank
            g[c, i, 20:24] = blank
            for side, at, step in ((ylow, 4, 1), (yhigh, 16, -1)):
                rows = side[i, 4 * c : 4 * c + 4] if c < 2 else side[13 + i, 0:4]
                g[c, i, at : at + 4] = kept("gy", step, rows)
    for j in range(14):
        eta[j, 0:4] = blank
        eta[j, 20:24] = blank
        eta[j, 8:16] = viscosity(j - 5)
        eta[j, 4:8] = kept("gy", 1, ylow[12 + j, 4:8])
        eta[j, 3:4] = kept("gy", 1, ylow[26 + j // 8, j % 8 : j % 8 + 1])
        eta[j, 16:20] = kept("gy", -1, yhigh[12 + j, 4:8])
        eta[j, 20:21] = kept("gy", -1, yhigh[26 + j // 8, j % 8 : j % 8 + 1])

    coefficients(eta, cx, cf, 12, 0.25, U1)

    plane = jnp.zeros((24, nz), F32)
    for c in range(3):
        for i in (0, 13):
            va[c, i] = plane
            v1[c, i] = plane

    def start(i):
        for c in range(3):
            va[c, i + 1] = cf[EI, i] * g[c, i]

    planes(12, start, U1)
    sweep(va, 5, g, 4, cx, cf, 4, v1, 5, -4, 8, U1)

    def down_pair(k):
        for c in range(3):
            x = 2 * k
            total = residual(v1, 1, g, 0, cx, cf, 0, c, x) + residual(v1, 1, g, 0, cx, cf, 0, c, x + 1)
            put_plane(pairs, c * 6 + k, total)

    planes(6, down_pair, U1)

    def eta_pair(k):
        put_plane(pairs, 18 + k, eta[2 * k + 1] + eta[2 * k + 2])

    planes(6, eta_pair, U1)
    for k in range(6):
        for c in range(3):
            row_pairs(pairs, c * 6 + k, 8, 4, rest, 16 * k + 4 * c)
        row_pairs(pairs, 18 + k, 8, 4, rest, 16 * k + 12)
    coarse = split_dot(rest[...], pair_matrix(nz)) * 0.125
    for k in range(6):
        own[k] = coarse[16 * k : 16 * k + 16]
    for t in range(4):
        source_rows = own[t + 1, 0:12]
        up[t, 0:12] = source_rows
        up[t, 12:16] = own[t, 12:16]
        down[t, 0:12] = source_rows
        down[t, 12:16] = own[t + 2, 12:16]
        if t < 2:
            far_up[t, 0:12] = source_rows
            far_up[t, 12:16] = own[t, 12:16]
        else:
            far_down[t - 2, 0:12] = source_rows
            far_down[t - 2, 12:16] = own[t + 2, 12:16]


def pack_coarse_y(own, low2, low3, high2, high3, strip):
    strip[0, 0:12] = jnp.zeros((12, own.shape[-1]), F32)
    strip[17, 0:12] = jnp.zeros((12, own.shape[-1]), F32)
    for t in range(2):
        rows = kept("gx", 3, low3[t])
        strip[1 + t, 0:12] = rows[0:12]
        strip[t, 12:16] = rows[12:16]
        rows = kept("gx", -3, high3[t])
        strip[15 + t, 0:12] = rows[0:12]
        strip[16 + t, 12:16] = rows[12:16]
    for t in range(4):
        rows = kept("gx", 2, low2[t])
        strip[3 + t, 0:12] = rows[0:12]
        strip[2 + t, 12:16] = rows[12:16]
        strip[7 + t, 0:12] = own[1 + t, 0:12]
        rows = kept("gx", -2, high2[t])
        strip[11 + t, 0:12] = rows[0:12]
        strip[12 + t, 12:16] = rows[12:16]
    for t in range(6):
        strip[6 + t, 12:16] = own[t, 12:16]
    for plane, outer, mine in ((6, 5, 0), (11, 12, 5)):
        inside = strip[outer, 12:16] > 0.0
        for c in range(3):
            rows = slice(4 * c, 4 * c + 4)
            strip[plane, rows] = jnp.where(inside, strip[plane, rows], own[mine, rows])


def ascend(
    mid, ym1, ym2, yp1, yp2, v1, g1, cx1, cf1, v0, rim, g0, cx0, cf0, out,
    eta2, g2, cx2, cf2, va2, vb2, rows2, wide1, va1, vb1, rows1, wide0, va0, vb0, result, sent,
):
    nz2, nz1, nz0 = mid.shape[-1], v1.shape[-1], v0.shape[-1]
    blank = jnp.zeros((4, nz2), F32)
    sides = ((ym2, 2), (ym1, 1), (mid, 0), (yp1, -1), (yp2, -2))
    for j in range(18):
        for n, (side, step) in enumerate(sides):
            rows = kept("gy", step, side[j]) if step else side[j]
            eta2[j, 4 * n : 4 * n + 4] = rows[12:16]
            if 1 <= j <= 16:
                for c in range(3):
                    g2[c, j - 1, 4 * n : 4 * n + 4] = rows[4 * c : 4 * c + 4]
        eta2[j, 20:24] = blank
        if 1 <= j <= 16:
            for c in range(3):
                g2[c, j - 1, 20:24] = blank
    coefficients(eta2, cx2, cf2, 16, 0.0625, U2)

    def start(i):
        for c in range(3):
            va2[c, i] = cf2[EI, i] * g2[c, i]

    planes(16, start, U2)
    source, target = va2, vb2
    for s in range(1, 6):
        sweep(source, 0, g2, 0, cx2, cf2, 0, target, 0, s, 16 - s, U2)
        source, target = target, source

    for c in range(3):
        for k in range(6):
            rows2[(c * 6 + k) * 16 : (c * 6 + k) * 16 + 16] = source[c, 5 + k, 4:20]
    spread = split_dot(rows2[...], copy_matrix(nz2))
    for n in range(18):
        block = spread[n * 16 : n * 16 + 12]
        row_copies(wide1, n, block)
    for c in range(3):
        for i in range(10):
            va1[c, i] = v1[c, i + 2] + get_plane(wide1, c * 6 + (i - 3) // 2 + 2)
    sweep(va1, 3, g1, 4, cx1, cf1, 4, vb1, 3, -2, 6, U1)
    sweep(vb1, 3, g1, 4, cx1, cf1, 4, va1, 3, -1, 5, U1)

    for c in range(3):
        for k in range(6):
            rows1[(c * 6 + k) * 16 : (c * 6 + k) * 16 + 16] = va1[c, 2 + k, 6:22]
    spread = split_dot(rows1[...], copy_matrix(nz1))
    for n in range(18):
        block = spread[n * 16 : n * 16 + 12]
        row_copies(wide0, n, block)

    for k in range(6):
        for c in range(3):
            block = get_plane(wide0, c * 6 + k)
            va0[c, 2 * k] = (v0[c, 2 * k - 1] if k > 0 else rim[c, 0]) + block
            va0[c, 2 * k + 1] = (v0[c, 2 * k] if k < 5 else rim[c, 1]) + block
    sweep(va0, 2, g0, 2, cx0, cf0, 2, vb0, 2, -1, 9, U0)

    def final(x):
        for c in range(3):
            here, total = gather_sum(vb0, c, x + 2, cx0, cf0, x + 2)
            value = (1.0 / 3.0) * here + cf0[EI, x + 2] * (g0[c, x + 2] + total)
            result[c, x] = value[4:20]
        pltpu.make_async_copy(result.at[:, x], out.at[:, x], sent.at[x]).start()

    planes(8, final, U0)
    for x in range(8):
        pltpu.make_async_copy(result.at[:, x], out.at[:, x], sent.at[x]).wait()


def call(body, outs, *args, scratch=(), copies=0, where_in=pltpu.VMEM, where_out=pltpu.VMEM):
    outs = [out if isinstance(out, jax.ShapeDtypeStruct) else jax.ShapeDtypeStruct(out, F32) for out in outs]
    scratch_shapes = [pltpu.VMEM(shape, F32) for shape in scratch]
    if copies:
        scratch_shapes.append(pltpu.SemaphoreType.DMA((copies,)))
    return pl.pallas_call(
        body,
        out_shape=outs,
        in_specs=[pl.BlockSpec(memory_space=where_in)] * len(args),
        out_specs=[pl.BlockSpec(memory_space=where_out)] * len(outs),
        scratch_shapes=scratch_shapes,
        compiler_params=pltpu.CompilerParams(vmem_limit_bytes=VMEM_LIMIT),
    )(*args)


def cycled(array, axis, step):
    size = lax.axis_size(axis)
    return lax.ppermute(array, axis, [(i, (i + step) % size) for i in range(size)])


def per_device(forcing, phase_ids):
    z0 = forcing.shape[-1]
    z1, z2 = z0 // 2, z0 // 4
    xup, xdown, yup, ydown, f0, ids0 = call(
        pack_fine,
        [(9, 16, z0)] * 2 + [(13, 8, z0)] * 2 + [forcing.shape, jax.ShapeDtypeStruct(phase_ids.shape, jnp.int32)],
        *(pltpu.with_memory_space_constraint(a, pltpu.HBM) for a in (forcing, phase_ids)), copies=12, where_in=pltpu.HBM,
    )
    xlow, xhigh = cycled(xup, "gx", 1), cycled(xdown, "gx", -1)
    ylow, yhigh = cycled(yup, "gy", 1), cycled(ydown, "gy", -1)
    up, down = call(pack_corners, [(8, 8, z0)] * 2, xlow, xhigh)
    clow, chigh = cycled(up, "gy", 1), cycled(down, "gy", -1)
    v0, va, g0, eta0, cx0, cf0, f1, eta1, up, down = call(
        fine_down,
        [(3, 10, 24, z0), (3, 12, 24, z0), (3, 12, 24, z0), (14, 24, z0), (13, 24, z0), (6, 12, 24, z0), (3, 4, 8, z1), (6, 8, z1), (17, 8, z1), (17, 8, z1)],
        f0, ids0, xlow, xhigh, ylow, yhigh, clow, chigh,
        scratch=[lane_blocks(18, z0), (144, z0)],
    )
    xlow, xhigh = cycled(up, "gx", 1), cycled(down, "gx", -1)
    up, down, late_up, late_down = call(
        pack_middle_y, [(28, 8, z1)] * 2 + [(4, 16, z0)] * 2, f1, eta1, xlow, xhigh, f0, ids0
    )
    ylow, yhigh = cycled(up, "gy", 1), cycled(down, "gy", -1)
    late_low, late_high = cycled(late_up, "gx", 1), cycled(late_down, "gx", -1)
    (rim,) = call(fine_rim, [(3, 2, 24, z0)], late_low, late_high, va, g0, eta0, cx0, cf0)
    v1, g1, cx1, cf1, own, up, down, far_up, far_down = call(
        middle_down,
        [(3, 14, 24, z1), (3, 12, 24, z1), (13, 24, z1), (6, 12, 24, z1), (6, 16, z2), (4, 16, z2), (4, 16, z2), (2, 16, z2), (2, 16, z2)],
        f1, eta1, xlow, xhigh, ylow, yhigh,
        scratch=[(14, 24, z1), (3, 14, 24, z1), lane_blocks(24, z1), (96, z1)],
    )
    low2, high2 = cycled(up, "gx", 2), cycled(down, "gx", -2)
    low3, high3 = cycled(far_up, "gx", 3), cycled(far_down, "gx", -3)
    (strip,) = call(pack_coarse_y, [(18, 16, z2)], own, low2, low3, high2, high3)
    ym1, yp1 = cycled(strip, "gy", 1), cycled(strip, "gy", -1)
    ym2, yp2 = cycled(strip, "gy", 2), cycled(strip, "gy", -2)
    (velocity,) = call(
        ascend,
        [forcing.shape],
        strip, ym1, ym2, yp1, yp2, v1, g1, cx1, cf1, v0, rim, g0, cx0, cf0,
        scratch=[
            (18, 24, z2), (3, 16, 24, z2), (17, 24, z2), (6, 16, 24, z2), (3, 16, 24, z2), (3, 16, 24, z2),
            (288, z2), lane_blocks(18, z1), (3, 10, 24, z1), (3, 10, 24, z1),
            (288, z1), lane_blocks(18, z0), (3, 12, 24, z0), (3, 12, 24, z0), forcing.shape,
        ],
        copies=8,
        where_out=pltpu.HBM,
    )
    return velocity


def solution(mesh):
    return jax.shard_map(
        per_device,
        mesh=mesh,
        in_specs=(P(None, "gx", "gy", None), P("gx", "gy", None)),
        out_specs=P(None, "gx", "gy", None),
        check_vma=False,
    )
```

```python
import functools

import jax
import jax.numpy as jnp
from jax import lax
from jax.experimental import pallas as pl
from jax.experimental.pallas import tpu as pltpu
from jax.sharding import PartitionSpec as P

F32 = jnp.float32
BF16 = jnp.bfloat16
WEIGHT = 2.0 / 3.0
VMEM_LIMIT = 40 * 1024 * 1024
U0, U1, U2 = 12, 12, 16


def materials(ids):
    eta = jnp.where(ids == 3, F32(4.0), F32(0.0))
    eta = jnp.where(ids == 2, F32(1.5), eta)
    eta = jnp.where(ids == 1, F32(0.6), eta)
    return jnp.where(ids == 0, F32(0.2), eta)


def lanes_of(shape):
    return lax.broadcasted_iota(jnp.int32, shape, len(shape) - 1)


def next_row(v):
    return pltpu.roll(v, v.shape[0] - 1, 0)


def last_row(v):
    return pltpu.roll(v, 1, 0)


def next_lane(v):
    return pltpu.roll(v, v.shape[1] - 1, 1)


def last_lane(v):
    return pltpu.roll(v, 1, 1)


def planes(count, body, unroll):
    steps = count // unroll if unroll < count else 0

    def step(n, _):
        for k in range(unroll):
            body(n * unroll + k)
        return 0

    if steps > 0:
        lax.fori_loop(0, steps, step, 0)
    for i in range(steps * unroll, count):
        body(i)


def kept(axis, step, value):
    place = lax.axis_index(axis) - step
    return jnp.where((place >= 0) & (place < lax.axis_size(axis)), value, 0.0)


def split_dot(rows, matrix):
    high = rows.astype(BF16)
    low = (rows - high.astype(F32)).astype(BF16)
    return jnp.dot(high, matrix, preferred_element_type=F32) + jnp.dot(
        low, matrix, preferred_element_type=F32
    )


def pair_matrix(fine):
    shape = (fine, fine // 2)
    row = lax.broadcasted_iota(jnp.int32, shape, 0)
    col = lax.broadcasted_iota(jnp.int32, shape, 1)
    return jnp.where((row == 2 * col) | (row == 2 * col + 1), F32(1), F32(0)).astype(BF16)


def copy_matrix(coarse):
    shape = (coarse, 2 * coarse)
    row = lax.broadcasted_iota(jnp.int32, shape, 0)
    col = lax.broadcasted_iota(jnp.int32, shape, 1)
    return jnp.where((col == 2 * row) | (col == 2 * row + 1), F32(1), F32(0)).astype(BF16)


YP, YM, ZP, ZM, DG, EI = range(6)


def plane_coefficients(below, here, above, scale):
    half = 0.5 * scale
    lane = lanes_of(here.shape)
    first = lane == 0
    final = lane == here.shape[1] - 1
    yp, ym = next_row(here), last_row(here)
    zp, zm = next_lane(here), last_lane(here)

    def ghost(q):
        return jnp.where(q > 0.0, q, here)

    around = ghost(yp) + ghost(ym) + ghost(below) + ghost(above)
    around = around + jnp.where(final, here, zp) + jnp.where(first, here, zm)
    diag = scale * (3.0 * here + 0.5 * around)
    return (
        half * (here + yp),
        half * (here + ym),
        jnp.where(final, 0.0, half * (here + zp)),
        jnp.where(first, 0.0, half * (here + zm)),
        diag,
        jnp.where(here > 0.0, WEIGHT / diag, 0.0),
    )


def coefficients(eta, cx, cf, layers, scale, unroll):
    half = 0.5 * scale

    def face(i):
        cx[i] = half * (eta[i] + eta[i + 1])

    planes(layers + 1, face, unroll)

    def body(i):
        made = plane_coefficients(eta[i], eta[i + 1], eta[i + 2], scale)
        for n, value in enumerate(made):
            cf[n, i] = value

    planes(layers, body, unroll)


def gather_sum(v, comp, i, cx, cf, k):
    here = v[comp, i]
    total = cx[k] * v[comp, i - 1] + cx[k + 1] * v[comp, i + 1]
    total = total + cf[YP, k] * next_row(here) + cf[YM, k] * last_row(here)
    total = total + cf[ZP, k] * next_lane(here) + cf[ZM, k] * last_lane(here)
    return here, total


def sweep(v, vo, g, go, cx, cf, co, out, oo, low, high, unroll):
    vo, go, co, oo = vo + low, go + low, co + low, oo + low

    def body(n):
        for comp in range(3):
            here, total = gather_sum(v, comp, n + vo, cx, cf, n + co)
            out[comp, n + oo] = (1.0 / 3.0) * here + cf[EI, n + co] * (g[comp, n + go] + total)

    planes(high - low, body, unroll)


def residual(v, vo, g, go, cx, cf, co, comp, x):
    here, total = gather_sum(v, comp, x + vo, cx, cf, x + co)
    return g[comp, x + go] - cf[DG, x + co] * here + total


def pack_fine(f_in, ids_in, xup, xdown, yup, ydown, f, ids, arrived):
    copies = [pltpu.make_async_copy(ids_in.at[x : x + 2], ids.at[x : x + 2], arrived.at[8 + x // 2]) for x in (0, 2, 4, 6)]
    copies += [pltpu.make_async_copy(f_in.at[:, x], f.at[:, x], arrived.at[x]) for x in range(8)]
    for copy in copies:
        copy.start()
    for copy in copies:
        copy.wait()
    for c in range(3):
        for k in range(2):
            xup[2 * c + k] = f[c, 6 + k]
            xdown[2 * c + k] = f[c, k]
    for x in range(8):
        eta = materials(ids[x])
        if x < 3:
            xdown[6 + x] = eta
        if x > 4:
            xup[6 + x - 5] = eta
        for out, at, eta_at in ((yup, 13, 12), (ydown, 0, 0)):
            pack_rows(out, x, 8, [f[c, x, at : at + 3] for c in range(3)])
            put_eta_rows(out, 9, x, eta[eta_at : eta_at + 4])


def pack_rows(out, n, spill, rows):
    out[n, 0:3] = rows[0]
    out[n, 3:6] = rows[1]
    out[n, 6:8] = rows[2][0:2]
    out[spill + n // 8, n % 8 : n % 8 + 1] = rows[2][2:3]


def put_eta_rows(out, first, n, rows):
    at = 4 * (n % 2)
    out[first + n // 2, at : at + 4] = rows


def fine_source(f, low, high, c, x):
    if x < 0:
        return kept("gx", 1, low[2 * c + x + 2])
    if x < 8:
        return f[c, x]
    return kept("gx", -1, high[2 * c + x - 8])


def fine_eta(ids, low, high, x):
    if x < 0:
        return kept("gx", 1, low[6 + x + 3])
    if x < 8:
        return materials(ids[x])
    return kept("gx", -1, high[6 + x - 8])


def pack_corners(low, high, up, down):
    for n, x in enumerate((-2, -1, 8, 9)):
        rows = [fine_source(None, low, high, c, x) for c in range(3)]
        for out, at in ((up, 13), (down, 0)):
            pack_rows(out, n, 4, [row[at : at + 3] for row in rows])
    for n, x in enumerate((-3, -2, -1, 8, 9, 10)):
        eta = fine_eta(None, low, high, x)
        put_eta_rows(up, 5, n, eta[12:16])
        put_eta_rows(down, 5, n, eta[0:4])
    for out in (up, down):
        out[4, 4:8] = jnp.zeros((4, low.shape[-1]), F32)


def fine_down(f, ids, xlow, xhigh, ylow, yhigh, clow, chigh, v0, va, g, eta, cx, cf, f1, eta1, up, down, pairs, rest):
    nz = f.shape[-1]
    blank = jnp.zeros((1, nz), F32)
    for i in range(12):
        x = i - 2
        for c in range(3):
            g[c, i, 4:20] = fine_source(f, xlow, xhigh, c, x)
            g[c, i, 0:1] = blank
            g[c, i, 23:24] = blank
        for own, corner, at, step in ((ylow, clow, 1, 1), (yhigh, chigh, 20, -1)):
            if 0 <= x < 8:
                side, n, spill = own, x, 8
            else:
                side, n, spill = corner, (i if x < 0 else x - 6), 4
            tile = kept("gy", step, side[n])
            g[0, i, at : at + 3] = tile[0:3]
            g[1, i, at : at + 3] = tile[3:6]
            g[2, i, at : at + 2] = tile[6:8]
            g[2, i, at + 2 : at + 3] = kept("gy", step, side[spill, n : n + 1])
    for j in range(14):
        x = j - 3
        eta[j, 4:20] = fine_eta(ids, xlow, xhigh, x)
        for own, corner, row, step in ((ylow, clow, 0, 1), (yhigh, chigh, 20, -1)):
            if 0 <= x < 8:
                side, n, first = own, x, 9
            else:
                side, n, first = corner, (j if x < 0 else x - 5), 5
            at = 4 * (n % 2)
            eta[j, row : row + 4] = kept("gy", step, side[first + n // 2, at : at + 4])

    coefficients(eta, cx, cf, 12, 1.0, U0)

    def start(i):
        for c in range(3):
            va[c, i] = cf[EI, i] * g[c, i]

    planes(12, start, U0)
    sweep(va, 2, g, 2, cx, cf, 2, v0, 1, -1, 9, U0)

    def down_pair(k):
        for c in range(3):
            x = 2 * k
            total = residual(v0, 1, g, 2, cx, cf, 2, c, x) + residual(v0, 1, g, 2, cx, cf, 2, c, x + 1)
            put_plane(pairs, c * 4 + k, total)

    planes(4, down_pair, U0)

    def eta_pair(k):
        put_plane(pairs, 12 + k, eta[2 * k + 1] + eta[2 * k + 2])

    planes(6, eta_pair, U0)
    for n in range(18):
        row_pairs(pairs, n, 4, 8, rest, n * 8)
    coarse = split_dot(rest[...], pair_matrix(nz)) * 0.125
    for n in range(12):
        block = coarse[n * 8 : n * 8 + 8]
        f1[n // 4, n % 4] = block
        up[n] = block
        down[n] = block
    for n in range(6):
        block = coarse[96 + n * 8 : 96 + n * 8 + 8]
        eta1[n] = block
        if n < 5:
            up[12 + n] = block
        if n > 0:
            down[12 + n - 1] = block


def lane_blocks(planes, nz):
    width = min(nz, 128)
    return (planes, nz // width, 24, width)


def put_plane(ref, n, value):
    width = ref.shape[-1]
    for b in range(ref.shape[1]):
        ref[n, b] = value[:, b * width : b * width + width]


def row_pairs(ref, n, at, count, out, row):
    width = ref.shape[-1]
    for b in range(ref.shape[1]):
        total = ref[n, b, pl.ds(at, count, stride=2), :] + ref[n, b, pl.ds(at + 1, count, stride=2), :]
        out[row : row + count, b * width : b * width + width] = total


def row_copies(ref, n, value):
    width = ref.shape[-1]
    count = value.shape[0]
    for b in range(ref.shape[1]):
        block = value[:, b * width : b * width + width]
        ref[n, b, pl.ds(0, count, stride=2), :] = block
        ref[n, b, pl.ds(1, count, stride=2), :] = block


def get_plane(ref, n):
    return jnp.concatenate([ref[n, b] for b in range(ref.shape[1])], axis=1)


def fine_rim(low, high, va, g, eta, cx, cf, rim):
    nz = low.shape[-1]
    blank = jnp.zeros((4, nz), F32)

    for n, (side, step) in enumerate(((low, 1), (high, -1))):
        rows = [jnp.concatenate([blank, kept("gx", step, side[k]), blank], axis=0) for k in range(4)]
        edge, k, inner, face, far = ((0, 0, 1, 1, 0), (13, 11, 10, 11, 12))[n]
        weight = plane_coefficients(rows[3], eta[edge], eta[1 if n == 0 else 12], 1.0)[EI]
        for c in range(3):
            here = va[c, k]
            total = cx[far] * (weight * rows[c]) + cx[face] * va[c, inner]
            total = total + cf[YP, k] * next_row(here) + cf[YM, k] * last_row(here)
            total = total + cf[ZP, k] * next_lane(here) + cf[ZM, k] * last_lane(here)
            rim[c, n] = (1.0 / 3.0) * here + cf[EI, k] * (g[c, k] + total)


def pack_middle_y(f1, eta1, low, high, f, ids, up, down, late_up, late_down):
    for c in range(3):
        late_up[c] = f[c, 5]
        late_down[c] = f[c, 2]
    late_up[3] = materials(ids[4])
    late_down[3] = materials(ids[3])

    def source(c, x):
        if x < 0:
            return kept("gx", 1, low[4 * c + x + 4])
        if x < 4:
            return f1[c, x]
        return kept("gx", -1, high[4 * c + x - 4])

    def viscosity(x):
        if x < 0:
            return kept("gx", 1, low[12 + x + 5])
        if x < 4:
            return eta1[x + 1]
        return kept("gx", -1, high[12 + x - 4])

    for i in range(12):
        rows = [source(c, i - 4) for c in range(3)]
        for out, at in ((up, 4), (down, 0)):
            out[i, 0:4] = rows[0][at : at + 4]
            out[i, 4:8] = rows[1][at : at + 4]
            out[12 + i + 1, 0:4] = rows[2][at : at + 4]
    for out in (up, down):
        out[12, 0:4] = jnp.zeros((4, f1.shape[-1]), F32)
        out[25, 0:4] = jnp.zeros((4, f1.shape[-1]), F32)
        out[27, 6:8] = jnp.zeros((2, f1.shape[-1]), F32)
    for j in range(14):
        eta = viscosity(j - 5)
        up[12 + j, 4:8] = eta[4:8]
        down[12 + j, 4:8] = eta[0:4]
        up[26 + j // 8, j % 8 : j % 8 + 1] = eta[3:4]
        down[26 + j // 8, j % 8 : j % 8 + 1] = eta[4:5]


def middle_down(f1, eta1, xlow, xhigh, ylow, yhigh, v1, g, cx, cf, own, up, down, far_up, far_down, eta, va, pairs, rest):
    nz = f1.shape[-1]
    blank = jnp.zeros((4, nz), F32)

    def source(c, x):
        if x < 0:
            return kept("gx", 1, xlow[4 * c + x + 4])
        if x < 4:
            return f1[c, x]
        return kept("gx", -1, xhigh[4 * c + x - 4])

    def viscosity(x):
        if x < 0:
            return kept("gx", 1, xlow[12 + x + 5])
        if x < 4:
            return eta1[x + 1]
        return kept("gx", -1, xhigh[12 + x - 4])

    for c in range(3):
        for i in range(12):
            g[c, i, 8:16] = source(c, i - 4)
            g[c, i, 0:4] = blank
            g[c, i, 20:24] = blank
            for side, at, step in ((ylow, 4, 1), (yhigh, 16, -1)):
                rows = side[i, 4 * c : 4 * c + 4] if c < 2 else side[13 + i, 0:4]
                g[c, i, at : at + 4] = kept("gy", step, rows)
    for j in range(14):
        eta[j, 0:4] = blank
        eta[j, 20:24] = blank
        eta[j, 8:16] = viscosity(j - 5)
        eta[j, 4:8] = kept("gy", 1, ylow[12 + j, 4:8])
        eta[j, 3:4] = kept("gy", 1, ylow[26 + j // 8, j % 8 : j % 8 + 1])
        eta[j, 16:20] = kept("gy", -1, yhigh[12 + j, 4:8])
        eta[j, 20:21] = kept("gy", -1, yhigh[26 + j // 8, j % 8 : j % 8 + 1])

    coefficients(eta, cx, cf, 12, 0.25, U1)

    plane = jnp.zeros((24, nz), F32)
    for c in range(3):
        for i in (0, 13):
            va[c, i] = plane
            v1[c, i] = plane

    def start(i):
        for c in range(3):
            va[c, i + 1] = cf[EI, i] * g[c, i]

    planes(12, start, U1)
    sweep(va, 5, g, 4, cx, cf, 4, v1, 5, -4, 8, U1)

    def down_pair(k):
        for c in range(3):
            x = 2 * k
            total = residual(v1, 1, g, 0, cx, cf, 0, c, x) + residual(v1, 1, g, 0, cx, cf, 0, c, x + 1)
            put_plane(pairs, c * 6 + k, total)

    planes(6, down_pair, U1)

    def eta_pair(k):
        put_plane(pairs, 18 + k, eta[2 * k + 1] + eta[2 * k + 2])

    planes(6, eta_pair, U1)
    for k in range(6):
        for c in range(3):
            row_pairs(pairs, c * 6 + k, 8, 4, rest, 16 * k + 4 * c)
        row_pairs(pairs, 18 + k, 8, 4, rest, 16 * k + 12)
    coarse = split_dot(rest[...], pair_matrix(nz)) * 0.125
    for k in range(6):
        own[k] = coarse[16 * k : 16 * k + 16]
    for t in range(4):
        source_rows = own[t + 1, 0:12]
        up[t, 0:12] = source_rows
        up[t, 12:16] = own[t, 12:16]
        down[t, 0:12] = source_rows
        down[t, 12:16] = own[t + 2, 12:16]
        if t < 2:
            far_up[t, 0:12] = source_rows
            far_up[t, 12:16] = own[t, 12:16]
        else:
            far_down[t - 2, 0:12] = source_rows
            far_down[t - 2, 12:16] = own[t + 2, 12:16]


def pack_coarse_y(own, low2, low3, high2, high3, rim, strip):
    strip[0, 0:12] = jnp.zeros((12, own.shape[-1]), F32)
    strip[17, 0:12] = jnp.zeros((12, own.shape[-1]), F32)
    for t in range(2):
        rows = kept("gx", 3, low3[t])
        strip[1 + t, 0:12] = rows[0:12]
        strip[t, 12:16] = rows[12:16]
        rows = kept("gx", -3, high3[t])
        strip[15 + t, 0:12] = rows[0:12]
        strip[16 + t, 12:16] = rows[12:16]
    for t in range(4):
        rows = kept("gx", 2, low2[t])
        strip[3 + t, 0:12] = rows[0:12]
        strip[2 + t, 12:16] = rows[12:16]
        strip[7 + t, 0:12] = own[1 + t, 0:12]
        rows = kept("gx", -2, high2[t])
        strip[11 + t, 0:12] = rows[0:12]
        strip[12 + t, 12:16] = rows[12:16]
    for t in range(6):
        strip[6 + t, 12:16] = own[t, 12:16]
    for plane, outer, mine in ((6, 5, 0), (11, 12, 5)):
        inside = strip[outer, 12:16] > 0.0
        for c in range(3):
            rows = slice(4 * c, 4 * c + 4)
            strip[plane, rows] = jnp.where(inside, strip[plane, rows], own[mine, rows])


def ascend(
    mid, ym1, ym2, yp1, yp2, v1, g1, cx1, cf1, v0, rim, g0, cx0, cf0, out,
    eta2, g2, cx2, cf2, va2, vb2, rows2, wide1, va1, vb1, rows1, wide0, va0, vb0, result, sent,
):
    nz2, nz1, nz0 = mid.shape[-1], v1.shape[-1], v0.shape[-1]
    blank = jnp.zeros((4, nz2), F32)
    sides = ((ym2, 2), (ym1, 1), (mid, 0), (yp1, -1), (yp2, -2))
    for j in range(18):
        for n, (side, step) in enumerate(sides):
            rows = kept("gy", step, side[j]) if step else side[j]
            eta2[j, 4 * n : 4 * n + 4] = rows[12:16]
            if 1 <= j <= 16:
                for c in range(3):
                    g2[c, j - 1, 4 * n : 4 * n + 4] = rows[4 * c : 4 * c + 4]
        eta2[j, 20:24] = blank
        if 1 <= j <= 16:
            for c in range(3):
                g2[c, j - 1, 20:24] = blank
    coefficients(eta2, cx2, cf2, 16, 0.0625, U2)

    def start(i):
        for c in range(3):
            va2[c, i] = cf2[EI, i] * g2[c, i]

    planes(16, start, U2)
    source, target = va2, vb2
    for s in range(1, 6):
        sweep(source, 0, g2, 0, cx2, cf2, 0, target, 0, s, 16 - s, U2)
        source, target = target, source

    for c in range(3):
        for k in range(6):
            rows2[(c * 6 + k) * 16 : (c * 6 + k) * 16 + 16] = source[c, 5 + k, 4:20]
    spread = split_dot(rows2[...], copy_matrix(nz2))
    for n in range(18):
        block = spread[n * 16 : n * 16 + 12]
        row_copies(wide1, n, block)
    for c in range(3):
        for i in range(10):
            va1[c, i] = v1[c, i + 2] + get_plane(wide1, c * 6 + (i - 3) // 2 + 2)
    sweep(va1, 3, g1, 4, cx1, cf1, 4, vb1, 3, -2, 6, U1)
    sweep(vb1, 3, g1, 4, cx1, cf1, 4, va1, 3, -1, 5, U1)

    for c in range(3):
        for k in range(6):
            rows1[(c * 6 + k) * 16 : (c * 6 + k) * 16 + 16] = va1[c, 2 + k, 6:22]
    spread = split_dot(rows1[...], copy_matrix(nz1))
    for n in range(18):
        block = spread[n * 16 : n * 16 + 12]
        row_copies(wide0, n, block)

    for k in range(6):
        for c in range(3):
            block = get_plane(wide0, c * 6 + k)
            va0[c, 2 * k] = (v0[c, 2 * k - 1] if k > 0 else rim[c, 0]) + block
            va0[c, 2 * k + 1] = (v0[c, 2 * k] if k < 5 else rim[c, 1]) + block
    sweep(va0, 2, g0, 2, cx0, cf0, 2, vb0, 2, -1, 9, U0)

    def final(x):
        for c in range(3):
            here, total = gather_sum(vb0, c, x + 2, cx0, cf0, x + 2)
            value = (1.0 / 3.0) * here + cf0[EI, x + 2] * (g0[c, x + 2] + total)
            result[c, x] = value[4:20]
        pltpu.make_async_copy(result.at[:, x], out.at[:, x], sent.at[x]).start()

    planes(8, final, U0)
    for x in range(8):
        pltpu.make_async_copy(result.at[:, x], out.at[:, x], sent.at[x]).wait()


def call(body, outs, *args, scratch=(), copies=0, where_in=pltpu.VMEM, where_out=pltpu.VMEM):
    outs = [out if isinstance(out, jax.ShapeDtypeStruct) else jax.ShapeDtypeStruct(out, F32) for out in outs]
    scratch_shapes = [pltpu.VMEM(shape, F32) for shape in scratch]
    if copies:
        scratch_shapes.append(pltpu.SemaphoreType.DMA((copies,)))
    return pl.pallas_call(
        body,
        out_shape=outs,
        in_specs=[pl.BlockSpec(memory_space=where_in)] * len(args),
        out_specs=[pl.BlockSpec(memory_space=where_out)] * len(outs),
        scratch_shapes=scratch_shapes,
        compiler_params=pltpu.CompilerParams(vmem_limit_bytes=VMEM_LIMIT),
    )(*args)


def cycled(array, axis, step):
    size = lax.axis_size(axis)
    return lax.ppermute(array, axis, [(i, (i + step) % size) for i in range(size)])


def per_device(forcing, phase_ids):
    z0 = forcing.shape[-1]
    z1, z2 = z0 // 2, z0 // 4
    xup, xdown, yup, ydown, f0, ids0 = call(
        pack_fine,
        [(9, 16, z0)] * 2 + [(13, 8, z0)] * 2 + [forcing.shape, jax.ShapeDtypeStruct(phase_ids.shape, jnp.int32)],
        *(pltpu.with_memory_space_constraint(a, pltpu.HBM) for a in (forcing, phase_ids)), copies=12, where_in=pltpu.HBM,
    )
    xlow, xhigh = cycled(xup, "gx", 1), cycled(xdown, "gx", -1)
    ylow, yhigh = cycled(yup, "gy", 1), cycled(ydown, "gy", -1)
    up, down = call(pack_corners, [(8, 8, z0)] * 2, xlow, xhigh)
    clow, chigh = cycled(up, "gy", 1), cycled(down, "gy", -1)
    v0, va, g0, eta0, cx0, cf0, f1, eta1, up, down = call(
        fine_down,
        [(3, 10, 24, z0), (3, 12, 24, z0), (3, 12, 24, z0), (14, 24, z0), (13, 24, z0), (6, 12, 24, z0), (3, 4, 8, z1), (6, 8, z1), (17, 8, z1), (17, 8, z1)],
        f0, ids0, xlow, xhigh, ylow, yhigh, clow, chigh,
        scratch=[lane_blocks(18, z0), (144, z0)],
    )
    xlow, xhigh = cycled(up, "gx", 1), cycled(down, "gx", -1)
    up, down, late_up, late_down = call(
        pack_middle_y, [(28, 8, z1)] * 2 + [(4, 16, z0)] * 2, f1, eta1, xlow, xhigh, f0, ids0
    )
    ylow, yhigh = cycled(up, "gy", 1), cycled(down, "gy", -1)
    late_low, late_high = cycled(late_up, "gx", 1), cycled(late_down, "gx", -1)
    (rim,) = call(fine_rim, [(3, 2, 24, z0)], late_low, late_high, va, g0, eta0, cx0, cf0)
    v1, g1, cx1, cf1, own, up, down, far_up, far_down = call(
        middle_down,
        [(3, 14, 24, z1), (3, 12, 24, z1), (13, 24, z1), (6, 12, 24, z1), (6, 16, z2), (4, 16, z2), (4, 16, z2), (2, 16, z2), (2, 16, z2)],
        f1, eta1, xlow, xhigh, ylow, yhigh,
        scratch=[(14, 24, z1), (3, 14, 24, z1), lane_blocks(24, z1), (96, z1)],
    )
    low2, high2 = cycled(up, "gx", 2), cycled(down, "gx", -2)
    low3, high3 = cycled(far_up, "gx", 3), cycled(far_down, "gx", -3)
    (strip,) = call(pack_coarse_y, [(18, 16, z2)], own, low2, low3, high2, high3, rim)
    ym1, yp1 = cycled(strip, "gy", 1), cycled(strip, "gy", -1)
    ym2, yp2 = cycled(strip, "gy", 2), cycled(strip, "gy", -2)
    (velocity,) = call(
        ascend,
        [forcing.shape],
        strip, ym1, ym2, yp1, yp2, v1, g1, cx1, cf1, v0, rim, g0, cx0, cf0,
        scratch=[
            (18, 24, z2), (3, 16, 24, z2), (17, 24, z2), (6, 16, 24, z2), (3, 16, 24, z2), (3, 16, 24, z2),
            (288, z2), lane_blocks(18, z1), (3, 10, 24, z1), (3, 10, 24, z1),
            (288, z1), lane_blocks(18, z0), (3, 12, 24, z0), (3, 12, 24, z0), forcing.shape,
        ],
        copies=8,
        where_out=pltpu.HBM,
    )
    return velocity


def solution(mesh):
    return jax.shard_map(
        per_device,
        mesh=mesh,
        in_specs=(P(None, "gx", "gy", None), P("gx", "gy", None)),
        out_specs=P(None, "gx", "gy", None),
        check_vma=False,
    )
```

```python
import functools

import jax
import jax.numpy as jnp
from jax import lax
from jax.experimental import pallas as pl
from jax.experimental.pallas import tpu as pltpu
from jax.sharding import PartitionSpec as P

F32 = jnp.float32
BF16 = jnp.bfloat16
WEIGHT = 2.0 / 3.0
VMEM_LIMIT = 40 * 1024 * 1024
U0, U1, U2 = 12, 12, 16


def materials(ids):
    eta = jnp.where(ids == 3, F32(4.0), F32(0.0))
    eta = jnp.where(ids == 2, F32(1.5), eta)
    eta = jnp.where(ids == 1, F32(0.6), eta)
    return jnp.where(ids == 0, F32(0.2), eta)


def lanes_of(shape):
    return lax.broadcasted_iota(jnp.int32, shape, len(shape) - 1)


def next_row(v):
    return pltpu.roll(v, v.shape[0] - 1, 0)


def last_row(v):
    return pltpu.roll(v, 1, 0)


def next_lane(v):
    return pltpu.roll(v, v.shape[1] - 1, 1)


def last_lane(v):
    return pltpu.roll(v, 1, 1)


def planes(count, body, unroll):
    steps = count // unroll if unroll < count else 0

    def step(n, _):
        for k in range(unroll):
            body(n * unroll + k)
        return 0

    if steps > 0:
        lax.fori_loop(0, steps, step, 0)
    for i in range(steps * unroll, count):
        body(i)


def kept(axis, step, value):
    place = lax.axis_index(axis) - step
    return jnp.where((place >= 0) & (place < lax.axis_size(axis)), value, 0.0)


def split_dot(rows, matrix):
    high = rows.astype(BF16)
    low = (rows - high.astype(F32)).astype(BF16)
    return jnp.dot(high, matrix, preferred_element_type=F32) + jnp.dot(
        low, matrix, preferred_element_type=F32
    )


def pair_matrix(fine):
    shape = (fine, fine // 2)
    row = lax.broadcasted_iota(jnp.int32, shape, 0)
    col = lax.broadcasted_iota(jnp.int32, shape, 1)
    return jnp.where((row == 2 * col) | (row == 2 * col + 1), F32(1), F32(0)).astype(BF16)


def copy_matrix(coarse):
    shape = (coarse, 2 * coarse)
    row = lax.broadcasted_iota(jnp.int32, shape, 0)
    col = lax.broadcasted_iota(jnp.int32, shape, 1)
    return jnp.where((col == 2 * row) | (col == 2 * row + 1), F32(1), F32(0)).astype(BF16)


YP, YM, ZP, ZM, DG, EI = range(6)


def plane_coefficients(below, here, above, scale):
    half = 0.5 * scale
    lane = lanes_of(here.shape)
    first = lane == 0
    final = lane == here.shape[1] - 1
    yp, ym = next_row(here), last_row(here)
    zp, zm = next_lane(here), last_lane(here)

    def ghost(q):
        return jnp.where(q > 0.0, q, here)

    around = ghost(yp) + ghost(ym) + ghost(below) + ghost(above)
    around = around + jnp.where(final, here, zp) + jnp.where(first, here, zm)
    diag = scale * (3.0 * here + 0.5 * around)
    return (
        half * (here + yp),
        half * (here + ym),
        jnp.where(final, 0.0, half * (here + zp)),
        jnp.where(first, 0.0, half * (here + zm)),
        diag,
        jnp.where(here > 0.0, WEIGHT / diag, 0.0),
    )


def coefficients(eta, cx, cf, layers, scale, unroll):
    half = 0.5 * scale

    def face(i):
        cx[i] = half * (eta[i] + eta[i + 1])

    planes(layers + 1, face, unroll)

    def body(i):
        made = plane_coefficients(eta[i], eta[i + 1], eta[i + 2], scale)
        for n, value in enumerate(made):
            cf[n, i] = value

    planes(layers, body, unroll)


def gather_sum(v, comp, i, cx, cf, k):
    here = v[comp, i]
    total = cx[k] * v[comp, i - 1] + cx[k + 1] * v[comp, i + 1]
    total = total + cf[YP, k] * next_row(here) + cf[YM, k] * last_row(here)
    total = total + cf[ZP, k] * next_lane(here) + cf[ZM, k] * last_lane(here)
    return here, total


def sweep(v, vo, g, go, cx, cf, co, out, oo, low, high, unroll):
    vo, go, co, oo = vo + low, go + low, co + low, oo + low

    def body(n):
        for comp in range(3):
            here, total = gather_sum(v, comp, n + vo, cx, cf, n + co)
            out[comp, n + oo] = (1.0 / 3.0) * here + cf[EI, n + co] * (g[comp, n + go] + total)

    planes(high - low, body, unroll)


def residual(v, vo, g, go, cx, cf, co, comp, x):
    here, total = gather_sum(v, comp, x + vo, cx, cf, x + co)
    return g[comp, x + go] - cf[DG, x + co] * here + total


def copied(copies):
    for copy in copies:
        copy.start()
    for copy in copies:
        copy.wait()


def pack_fine_x(f_in, ids_in, xup, xdown, f, ids, arrived):
    copied(
        [pltpu.make_async_copy(ids_in.at[5 * k : 5 * k + 3], ids.at[3 * k : 3 * k + 3], arrived.at[k]) for k in range(2)]
        + [
            pltpu.make_async_copy(f_in.at[:, 6 * k + n], f.at[:, 2 * k + n], arrived.at[2 + 2 * k + n])
            for k in range(2)
            for n in range(2)
        ]
    )
    for n, out in enumerate((xdown, xup)):
        for c in range(3):
            for k in range(2):
                out[2 * c + k] = f[c, 2 * n + k]
        for k in range(3):
            out[6 + k] = materials(ids[3 * n + k])


def pack_fine_y(f_in, ids_in, yup, ydown, f, ids, arrived):
    copied(
        [pltpu.make_async_copy(ids_in.at[x : x + 2], ids.at[x : x + 2], arrived.at[8 + x // 2]) for x in (0, 2, 4, 6)]
        + [pltpu.make_async_copy(f_in.at[:, x], f.at[:, x], arrived.at[x]) for x in range(8)]
    )
    for x in range(8):
        eta = materials(ids[x])
        for out, at, eta_at in ((yup, 13, 12), (ydown, 0, 0)):
            pack_rows(out, x, 8, [f[c, x, at : at + 3] for c in range(3)])
            put_eta_rows(out, 9, x, eta[eta_at : eta_at + 4])


def pack_rows(out, n, spill, rows):
    out[n, 0:3] = rows[0]
    out[n, 3:6] = rows[1]
    out[n, 6:8] = rows[2][0:2]
    out[spill + n // 8, n % 8 : n % 8 + 1] = rows[2][2:3]


def put_eta_rows(out, first, n, rows):
    at = 4 * (n % 2)
    out[first + n // 2, at : at + 4] = rows


def fine_source(f, low, high, c, x):
    if x < 0:
        return kept("gx", 1, low[2 * c + x + 2])
    if x < 8:
        return f[c, x]
    return kept("gx", -1, high[2 * c + x - 8])


def fine_eta(ids, low, high, x):
    if x < 0:
        return kept("gx", 1, low[6 + x + 3])
    if x < 8:
        return materials(ids[x])
    return kept("gx", -1, high[6 + x - 8])


def pack_corners(low, high, up, down):
    for n, x in enumerate((-2, -1, 8, 9)):
        rows = [fine_source(None, low, high, c, x) for c in range(3)]
        for out, at in ((up, 13), (down, 0)):
            pack_rows(out, n, 4, [row[at : at + 3] for row in rows])
    for n, x in enumerate((-3, -2, -1, 8, 9, 10)):
        eta = fine_eta(None, low, high, x)
        put_eta_rows(up, 5, n, eta[12:16])
        put_eta_rows(down, 5, n, eta[0:4])
    for out in (up, down):
        out[4, 4:8] = jnp.zeros((4, low.shape[-1]), F32)


def fine_down(f, ids, xlow, xhigh, ylow, yhigh, clow, chigh, v0, va, g, eta, cx, cf, f1, eta1, up, down, pairs, rest):
    nz = f.shape[-1]
    blank = jnp.zeros((1, nz), F32)
    for i in range(12):
        x = i - 2
        for c in range(3):
            g[c, i, 4:20] = fine_source(f, xlow, xhigh, c, x)
            g[c, i, 0:1] = blank
            g[c, i, 23:24] = blank
        for own, corner, at, step in ((ylow, clow, 1, 1), (yhigh, chigh, 20, -1)):
            if 0 <= x < 8:
                side, n, spill = own, x, 8
            else:
                side, n, spill = corner, (i if x < 0 else x - 6), 4
            tile = kept("gy", step, side[n])
            g[0, i, at : at + 3] = tile[0:3]
            g[1, i, at : at + 3] = tile[3:6]
            g[2, i, at : at + 2] = tile[6:8]
            g[2, i, at + 2 : at + 3] = kept("gy", step, side[spill, n : n + 1])
    for j in range(14):
        x = j - 3
        eta[j, 4:20] = fine_eta(ids, xlow, xhigh, x)
        for own, corner, row, step in ((ylow, clow, 0, 1), (yhigh, chigh, 20, -1)):
            if 0 <= x < 8:
                side, n, first = own, x, 9
            else:
                side, n, first = corner, (j if x < 0 else x - 5), 5
            at = 4 * (n % 2)
            eta[j, row : row + 4] = kept("gy", step, side[first + n // 2, at : at + 4])

    coefficients(eta, cx, cf, 12, 1.0, U0)

    def start(i):
        for c in range(3):
            va[c, i] = cf[EI, i] * g[c, i]

    planes(12, start, U0)
    sweep(va, 2, g, 2, cx, cf, 2, v0, 1, -1, 9, U0)

    def down_pair(k):
        for c in range(3):
            x = 2 * k
            total = residual(v0, 1, g, 2, cx, cf, 2, c, x) + residual(v0, 1, g, 2, cx, cf, 2, c, x + 1)
            put_plane(pairs, c * 4 + k, total)

    planes(4, down_pair, U0)

    def eta_pair(k):
        put_plane(pairs, 12 + k, eta[2 * k + 1] + eta[2 * k + 2])

    planes(6, eta_pair, U0)
    for n in range(18):
        row_pairs(pairs, n, 4, 8, rest, n * 8)
    coarse = split_dot(rest[...], pair_matrix(nz)) * 0.125
    for n in range(12):
        block = coarse[n * 8 : n * 8 + 8]
        f1[n // 4, n % 4] = block
        up[n] = block
        down[n] = block
    for n in range(6):
        block = coarse[96 + n * 8 : 96 + n * 8 + 8]
        eta1[n] = block
        if n < 5:
            up[12 + n] = block
        if n > 0:
            down[12 + n - 1] = block


def lane_blocks(planes, nz):
    width = min(nz, 128)
    return (planes, nz // width, 24, width)


def put_plane(ref, n, value):
    width = ref.shape[-1]
    for b in range(ref.shape[1]):
        ref[n, b] = value[:, b * width : b * width + width]


def row_pairs(ref, n, at, count, out, row):
    width = ref.shape[-1]
    for b in range(ref.shape[1]):
        total = ref[n, b, pl.ds(at, count, stride=2), :] + ref[n, b, pl.ds(at + 1, count, stride=2), :]
        out[row : row + count, b * width : b * width + width] = total


def row_copies(ref, n, value):
    width = ref.shape[-1]
    count = value.shape[0]
    for b in range(ref.shape[1]):
        block = value[:, b * width : b * width + width]
        ref[n, b, pl.ds(0, count, stride=2), :] = block
        ref[n, b, pl.ds(1, count, stride=2), :] = block


def get_plane(ref, n):
    return jnp.concatenate([ref[n, b] for b in range(ref.shape[1])], axis=1)


def fine_rim(low, high, va, g, eta, cx, cf, rim):
    nz = low.shape[-1]
    blank = jnp.zeros((4, nz), F32)

    for n, (side, step) in enumerate(((low, 1), (high, -1))):
        rows = [jnp.concatenate([blank, kept("gx", step, side[k]), blank], axis=0) for k in range(4)]
        edge, k, inner, face, far = ((0, 0, 1, 1, 0), (13, 11, 10, 11, 12))[n]
        weight = plane_coefficients(rows[3], eta[edge], eta[1 if n == 0 else 12], 1.0)[EI]
        for c in range(3):
            here = va[c, k]
            total = cx[far] * (weight * rows[c]) + cx[face] * va[c, inner]
            total = total + cf[YP, k] * next_row(here) + cf[YM, k] * last_row(here)
            total = total + cf[ZP, k] * next_lane(here) + cf[ZM, k] * last_lane(here)
            rim[c, n] = (1.0 / 3.0) * here + cf[EI, k] * (g[c, k] + total)


def pack_middle_y(f1, eta1, low, high, f, ids, up, down, late_up, late_down):
    for c in range(3):
        late_up[c] = f[c, 5]
        late_down[c] = f[c, 2]
    late_up[3] = materials(ids[4])
    late_down[3] = materials(ids[3])

    def source(c, x):
        if x < 0:
            return kept("gx", 1, low[4 * c + x + 4])
        if x < 4:
            return f1[c, x]
        return kept("gx", -1, high[4 * c + x - 4])

    def viscosity(x):
        if x < 0:
            return kept("gx", 1, low[12 + x + 5])
        if x < 4:
            return eta1[x + 1]
        return kept("gx", -1, high[12 + x - 4])

    for i in range(12):
        rows = [source(c, i - 4) for c in range(3)]
        for out, at in ((up, 4), (down, 0)):
            out[i, 0:4] = rows[0][at : at + 4]
            out[i, 4:8] = rows[1][at : at + 4]
            out[12 + i + 1, 0:4] = rows[2][at : at + 4]
    for out in (up, down):
        out[12, 0:4] = jnp.zeros((4, f1.shape[-1]), F32)
        out[25, 0:4] = jnp.zeros((4, f1.shape[-1]), F32)
        out[27, 6:8] = jnp.zeros((2, f1.shape[-1]), F32)
    for j in range(14):
        eta = viscosity(j - 5)
        up[12 + j, 4:8] = eta[4:8]
        down[12 + j, 4:8] = eta[0:4]
        up[26 + j // 8, j % 8 : j % 8 + 1] = eta[3:4]
        down[26 + j // 8, j % 8 : j % 8 + 1] = eta[4:5]


def middle_down(f1, eta1, xlow, xhigh, ylow, yhigh, v1, g, cx, cf, own, up, down, far_up, far_down, eta, va, pairs, rest):
    nz = f1.shape[-1]
    blank = jnp.zeros((4, nz), F32)

    def source(c, x):
        if x < 0:
            return kept("gx", 1, xlow[4 * c + x + 4])
        if x < 4:
            return f1[c, x]
        return kept("gx", -1, xhigh[4 * c + x - 4])

    def viscosity(x):
        if x < 0:
            return kept("gx", 1, xlow[12 + x + 5])
        if x < 4:
            return eta1[x + 1]
        return kept("gx", -1, xhigh[12 + x - 4])

    for c in range(3):
        for i in range(12):
            g[c, i, 8:16] = source(c, i - 4)
            g[c, i, 0:4] = blank
            g[c, i, 20:24] = blank
            for side, at, step in ((ylow, 4, 1), (yhigh, 16, -1)):
                rows = side[i, 4 * c : 4 * c + 4] if c < 2 else side[13 + i, 0:4]
                g[c, i, at : at + 4] = kept("gy", step, rows)
    for j in range(14):
        eta[j, 0:4] = blank
        eta[j, 20:24] = blank
        eta[j, 8:16] = viscosity(j - 5)
        eta[j, 4:8] = kept("gy", 1, ylow[12 + j, 4:8])
        eta[j, 3:4] = kept("gy", 1, ylow[26 + j // 8, j % 8 : j % 8 + 1])
        eta[j, 16:20] = kept("gy", -1, yhigh[12 + j, 4:8])
        eta[j, 20:21] = kept("gy", -1, yhigh[26 + j // 8, j % 8 : j % 8 + 1])

    coefficients(eta, cx, cf, 12, 0.25, U1)

    plane = jnp.zeros((24, nz), F32)
    for c in range(3):
        for i in (0, 13):
            va[c, i] = plane
            v1[c, i] = plane

    def start(i):
        for c in range(3):
            va[c, i + 1] = cf[EI, i] * g[c, i]

    planes(12, start, U1)
    sweep(va, 5, g, 4, cx, cf, 4, v1, 5, -4, 8, U1)

    def down_pair(k):
        for c in range(3):
            x = 2 * k
            total = residual(v1, 1, g, 0, cx, cf, 0, c, x) + residual(v1, 1, g, 0, cx, cf, 0, c, x + 1)
            put_plane(pairs, c * 6 + k, total)

    planes(6, down_pair, U1)

    def eta_pair(k):
        put_plane(pairs, 18 + k, eta[2 * k + 1] + eta[2 * k + 2])

    planes(6, eta_pair, U1)
    for k in range(6):
        for c in range(3):
            row_pairs(pairs, c * 6 + k, 8, 4, rest, 16 * k + 4 * c)
        row_pairs(pairs, 18 + k, 8, 4, rest, 16 * k + 12)
    coarse = split_dot(rest[...], pair_matrix(nz)) * 0.125
    for k in range(6):
        own[k] = coarse[16 * k : 16 * k + 16]
    for t in range(4):
        source_rows = own[t + 1, 0:12]
        up[t, 0:12] = source_rows
        up[t, 12:16] = own[t, 12:16]
        down[t, 0:12] = source_rows
        down[t, 12:16] = own[t + 2, 12:16]
        if t < 2:
            far_up[t, 0:12] = source_rows
            far_up[t, 12:16] = own[t, 12:16]
        else:
            far_down[t - 2, 0:12] = source_rows
            far_down[t - 2, 12:16] = own[t + 2, 12:16]


def pack_coarse_y(own, low2, low3, high2, high3, strip):
    strip[0, 0:12] = jnp.zeros((12, own.shape[-1]), F32)
    strip[17, 0:12] = jnp.zeros((12, own.shape[-1]), F32)
    for t in range(2):
        rows = kept("gx", 3, low3[t])
        strip[1 + t, 0:12] = rows[0:12]
        strip[t, 12:16] = rows[12:16]
        rows = kept("gx", -3, high3[t])
        strip[15 + t, 0:12] = rows[0:12]
        strip[16 + t, 12:16] = rows[12:16]
    for t in range(4):
        rows = kept("gx", 2, low2[t])
        strip[3 + t, 0:12] = rows[0:12]
        strip[2 + t, 12:16] = rows[12:16]
        strip[7 + t, 0:12] = own[1 + t, 0:12]
        rows = kept("gx", -2, high2[t])
        strip[11 + t, 0:12] = rows[0:12]
        strip[12 + t, 12:16] = rows[12:16]
    for t in range(6):
        strip[6 + t, 12:16] = own[t, 12:16]
    for plane, outer, mine in ((6, 5, 0), (11, 12, 5)):
        inside = strip[outer, 12:16] > 0.0
        for c in range(3):
            rows = slice(4 * c, 4 * c + 4)
            strip[plane, rows] = jnp.where(inside, strip[plane, rows], own[mine, rows])


def ascend(
    mid, ym1, ym2, yp1, yp2, v1, g1, cx1, cf1, v0, rim, g0, cx0, cf0, out,
    eta2, g2, cx2, cf2, va2, vb2, rows2, wide1, va1, vb1, rows1, wide0, va0, vb0, result, sent,
):
    nz2, nz1, nz0 = mid.shape[-1], v1.shape[-1], v0.shape[-1]
    blank = jnp.zeros((4, nz2), F32)
    sides = ((ym2, 2), (ym1, 1), (mid, 0), (yp1, -1), (yp2, -2))
    for j in range(18):
        for n, (side, step) in enumerate(sides):
            rows = kept("gy", step, side[j]) if step else side[j]
            eta2[j, 4 * n : 4 * n + 4] = rows[12:16]
            if 1 <= j <= 16:
                for c in range(3):
                    g2[c, j - 1, 4 * n : 4 * n + 4] = rows[4 * c : 4 * c + 4]
        eta2[j, 20:24] = blank
        if 1 <= j <= 16:
            for c in range(3):
                g2[c, j - 1, 20:24] = blank
    coefficients(eta2, cx2, cf2, 16, 0.0625, U2)

    def start(i):
        for c in range(3):
            va2[c, i] = cf2[EI, i] * g2[c, i]

    planes(16, start, U2)
    source, target = va2, vb2
    for s in range(1, 6):
        sweep(source, 0, g2, 0, cx2, cf2, 0, target, 0, s, 16 - s, U2)
        source, target = target, source

    for c in range(3):
        for k in range(6):
            rows2[(c * 6 + k) * 16 : (c * 6 + k) * 16 + 16] = source[c, 5 + k, 4:20]
    spread = split_dot(rows2[...], copy_matrix(nz2))
    for n in range(18):
        block = spread[n * 16 : n * 16 + 12]
        row_copies(wide1, n, block)
    for c in range(3):
        for i in range(10):
            va1[c, i] = v1[c, i + 2] + get_plane(wide1, c * 6 + (i - 3) // 2 + 2)
    sweep(va1, 3, g1, 4, cx1, cf1, 4, vb1, 3, -2, 6, U1)
    sweep(vb1, 3, g1, 4, cx1, cf1, 4, va1, 3, -1, 5, U1)

    for c in range(3):
        for k in range(6):
            rows1[(c * 6 + k) * 16 : (c * 6 + k) * 16 + 16] = va1[c, 2 + k, 6:22]
    spread = split_dot(rows1[...], copy_matrix(nz1))
    for n in range(18):
        block = spread[n * 16 : n * 16 + 12]
        row_copies(wide0, n, block)

    for k in range(6):
        for c in range(3):
            block = get_plane(wide0, c * 6 + k)
            va0[c, 2 * k] = (v0[c, 2 * k - 1] if k > 0 else rim[c, 0]) + block
            va0[c, 2 * k + 1] = (v0[c, 2 * k] if k < 5 else rim[c, 1]) + block
    sweep(va0, 2, g0, 2, cx0, cf0, 2, vb0, 2, -1, 9, U0)

    def final(x):
        for c in range(3):
            here, total = gather_sum(vb0, c, x + 2, cx0, cf0, x + 2)
            value = (1.0 / 3.0) * here + cf0[EI, x + 2] * (g0[c, x + 2] + total)
            result[c, x] = value[4:20]
        pltpu.make_async_copy(result.at[:, x], out.at[:, x], sent.at[x]).start()

    planes(8, final, U0)
    for x in range(8):
        pltpu.make_async_copy(result.at[:, x], out.at[:, x], sent.at[x]).wait()


def typed(shape):
    return shape if isinstance(shape, jax.ShapeDtypeStruct) else jax.ShapeDtypeStruct(shape, F32)


def call(body, outs, *args, scratch=(), copies=0, where_in=pltpu.VMEM, where_out=pltpu.VMEM):
    outs = [typed(out) for out in outs]
    scratch_shapes = [pltpu.VMEM(typed(shape).shape, typed(shape).dtype) for shape in scratch]
    if copies:
        scratch_shapes.append(pltpu.SemaphoreType.DMA((copies,)))
    return pl.pallas_call(
        body,
        out_shape=outs,
        in_specs=[pl.BlockSpec(memory_space=where_in)] * len(args),
        out_specs=[pl.BlockSpec(memory_space=where_out)] * len(outs),
        scratch_shapes=scratch_shapes,
        compiler_params=pltpu.CompilerParams(vmem_limit_bytes=VMEM_LIMIT),
    )(*args)


def cycled(array, axis, step):
    size = lax.axis_size(axis)
    return lax.ppermute(array, axis, [(i, (i + step) % size) for i in range(size)])


def per_device(forcing, phase_ids):
    z0 = forcing.shape[-1]
    z1, z2 = z0 // 2, z0 // 4
    inputs = [pltpu.with_memory_space_constraint(a, pltpu.HBM) for a in (forcing, phase_ids)]
    xup, xdown = call(
        pack_fine_x, [(9, 16, z0)] * 2, *inputs,
        scratch=[(3, 4, 16, z0), jax.ShapeDtypeStruct((6, 16, z0), jnp.int32)], copies=6, where_in=pltpu.HBM,
    )
    yup, ydown, f0, ids0 = call(
        pack_fine_y,
        [(13, 8, z0)] * 2 + [forcing.shape, jax.ShapeDtypeStruct(phase_ids.shape, jnp.int32)],
        *inputs, copies=12, where_in=pltpu.HBM,
    )
    xlow, xhigh = cycled(xup, "gx", 1), cycled(xdown, "gx", -1)
    ylow, yhigh = cycled(yup, "gy", 1), cycled(ydown, "gy", -1)
    up, down = call(pack_corners, [(8, 8, z0)] * 2, xlow, xhigh)
    clow, chigh = cycled(up, "gy", 1), cycled(down, "gy", -1)
    v0, va, g0, eta0, cx0, cf0, f1, eta1, up, down = call(
        fine_down,
        [(3, 10, 24, z0), (3, 12, 24, z0), (3, 12, 24, z0), (14, 24, z0), (13, 24, z0), (6, 12, 24, z0), (3, 4, 8, z1), (6, 8, z1), (17, 8, z1), (17, 8, z1)],
        f0, ids0, xlow, xhigh, ylow, yhigh, clow, chigh,
        scratch=[lane_blocks(18, z0), (144, z0)],
    )
    xlow, xhigh = cycled(up, "gx", 1), cycled(down, "gx", -1)
    up, down, late_up, late_down = call(
        pack_middle_y, [(28, 8, z1)] * 2 + [(4, 16, z0)] * 2, f1, eta1, xlow, xhigh, f0, ids0
    )
    ylow, yhigh = cycled(up, "gy", 1), cycled(down, "gy", -1)
    late_low, late_high = cycled(late_up, "gx", 1), cycled(late_down, "gx", -1)
    (rim,) = call(fine_rim, [(3, 2, 24, z0)], late_low, late_high, va, g0, eta0, cx0, cf0)
    v1, g1, cx1, cf1, own, up, down, far_up, far_down = call(
        middle_down,
        [(3, 14, 24, z1), (3, 12, 24, z1), (13, 24, z1), (6, 12, 24, z1), (6, 16, z2), (4, 16, z2), (4, 16, z2), (2, 16, z2), (2, 16, z2)],
        f1, eta1, xlow, xhigh, ylow, yhigh,
        scratch=[(14, 24, z1), (3, 14, 24, z1), lane_blocks(24, z1), (96, z1)],
    )
    low2, high2 = cycled(up, "gx", 2), cycled(down, "gx", -2)
    low3, high3 = cycled(far_up, "gx", 3), cycled(far_down, "gx", -3)
    (strip,) = call(pack_coarse_y, [(18, 16, z2)], own, low2, low3, high2, high3)
    ym1, yp1 = cycled(strip, "gy", 1), cycled(strip, "gy", -1)
    ym2, yp2 = cycled(strip, "gy", 2), cycled(strip, "gy", -2)
    (velocity,) = call(
        ascend,
        [forcing.shape],
        strip, ym1, ym2, yp1, yp2, v1, g1, cx1, cf1, v0, rim, g0, cx0, cf0,
        scratch=[
            (18, 24, z2), (3, 16, 24, z2), (17, 24, z2), (6, 16, 24, z2), (3, 16, 24, z2), (3, 16, 24, z2),
            (288, z2), lane_blocks(18, z1), (3, 10, 24, z1), (3, 10, 24, z1),
            (288, z1), lane_blocks(18, z0), (3, 12, 24, z0), (3, 12, 24, z0), forcing.shape,
        ],
        copies=8,
        where_out=pltpu.HBM,
    )
    return velocity


def solution(mesh):
    return jax.shard_map(
        per_device,
        mesh=mesh,
        in_specs=(P(None, "gx", "gy", None), P("gx", "gy", None)),
        out_specs=P(None, "gx", "gy", None),
        check_vma=False,
    )
```

```python
import functools

import jax
import jax.numpy as jnp
from jax import lax
from jax.experimental import pallas as pl
from jax.experimental.pallas import tpu as pltpu
from jax.sharding import PartitionSpec as P

F32 = jnp.float32
BF16 = jnp.bfloat16
WEIGHT = 2.0 / 3.0
VMEM_LIMIT = 24 * 1024 * 1024
U0, U1, U2 = 12, 12, 16


def materials(ids):
    eta = jnp.where(ids == 3, F32(4.0), F32(0.0))
    eta = jnp.where(ids == 2, F32(1.5), eta)
    eta = jnp.where(ids == 1, F32(0.6), eta)
    return jnp.where(ids == 0, F32(0.2), eta)


def lanes_of(shape):
    return lax.broadcasted_iota(jnp.int32, shape, len(shape) - 1)


def next_row(v):
    return pltpu.roll(v, v.shape[0] - 1, 0)


def last_row(v):
    return pltpu.roll(v, 1, 0)


def next_lane(v):
    return pltpu.roll(v, v.shape[1] - 1, 1)


def last_lane(v):
    return pltpu.roll(v, 1, 1)


def planes(count, body, unroll):
    steps = count // unroll if unroll < count else 0

    def step(n, _):
        for k in range(unroll):
            body(n * unroll + k)
        return 0

    if steps > 0:
        lax.fori_loop(0, steps, step, 0)
    for i in range(steps * unroll, count):
        body(i)


def kept(axis, step, value):
    place = lax.axis_index(axis) - step
    return jnp.where((place >= 0) & (place < lax.axis_size(axis)), value, 0.0)


class Spliced:
    def __init__(self, middle, outer, first, count, flat=False):
        self.middle, self.outer, self.first, self.count, self.flat = middle, outer, first, count, flat

    def place(self, key):
        lead, i = ((), key) if self.flat else ((key[0],), key[1])
        rest = () if self.flat else tuple(key[2:])
        if self.first <= i < self.first + self.count:
            return self.middle, lead + (i - self.first,) + rest
        return self.outer, lead + (i if i < self.first else i - self.count,) + rest

    def __getitem__(self, key):
        ref, at = self.place(key)
        return ref[at]

    def __setitem__(self, key, value):
        ref, at = self.place(key)
        ref[at] = value


def fine_set(inner, outer):
    spans = ((3, 4), (3, 6), (2, 8), (3, 8), (3, 7), (3, 6))
    return [Spliced(a, b, *span, flat=n in (3, 4)) for n, (a, b, span) in enumerate(zip(inner, outer, spans))]


def split_dot(rows, matrix):
    high = rows.astype(BF16)
    low = (rows - high.astype(F32)).astype(BF16)
    return jnp.dot(high, matrix, preferred_element_type=F32) + jnp.dot(
        low, matrix, preferred_element_type=F32
    )


def pair_matrix(fine):
    shape = (fine, fine // 2)
    row = lax.broadcasted_iota(jnp.int32, shape, 0)
    col = lax.broadcasted_iota(jnp.int32, shape, 1)
    return jnp.where((row == 2 * col) | (row == 2 * col + 1), F32(1), F32(0)).astype(BF16)


def copy_matrix(coarse):
    shape = (coarse, 2 * coarse)
    row = lax.broadcasted_iota(jnp.int32, shape, 0)
    col = lax.broadcasted_iota(jnp.int32, shape, 1)
    return jnp.where((col == 2 * row) | (col == 2 * row + 1), F32(1), F32(0)).astype(BF16)


YP, YM, ZP, ZM, DG, EI = range(6)


def plane_coefficients(below, here, above, scale):
    half = 0.5 * scale
    lane = lanes_of(here.shape)
    first = lane == 0
    final = lane == here.shape[1] - 1
    yp, ym = next_row(here), last_row(here)
    zp, zm = next_lane(here), last_lane(here)

    def ghost(q):
        return jnp.where(q > 0.0, q, here)

    around = ghost(yp) + ghost(ym) + ghost(below) + ghost(above)
    around = around + jnp.where(final, here, zp) + jnp.where(first, here, zm)
    diag = scale * (3.0 * here + 0.5 * around)
    return (
        half * (here + yp),
        half * (here + ym),
        jnp.where(final, 0.0, half * (here + zp)),
        jnp.where(first, 0.0, half * (here + zm)),
        diag,
        jnp.where(here > 0.0, WEIGHT / diag, 0.0),
    )


def coefficients(eta, cx, cf, layers, scale, unroll):
    planes(layers + 1, lambda i: face_plane(eta, cx, i, scale), unroll)
    planes(layers, lambda i: cell_plane(eta, cf, i, scale), unroll)


def face_plane(eta, cx, i, scale):
    cx[i] = (0.5 * scale) * (eta[i] + eta[i + 1])


def cell_plane(eta, cf, i, scale):
    made = plane_coefficients(eta[i], eta[i + 1], eta[i + 2], scale)
    for n, value in enumerate(made):
        cf[n, i] = value


def gather_sum(v, comp, i, cx, cf, k):
    here = v[comp, i]
    total = cx[k] * v[comp, i - 1] + cx[k + 1] * v[comp, i + 1]
    total = total + cf[YP, k] * next_row(here) + cf[YM, k] * last_row(here)
    total = total + cf[ZP, k] * next_lane(here) + cf[ZM, k] * last_lane(here)
    return here, total


def sweep(v, vo, g, go, cx, cf, co, out, oo, low, high, unroll):
    vo, go, co, oo = vo + low, go + low, co + low, oo + low

    def body(n):
        for comp in range(3):
            here, total = gather_sum(v, comp, n + vo, cx, cf, n + co)
            out[comp, n + oo] = (1.0 / 3.0) * here + cf[EI, n + co] * (g[comp, n + go] + total)

    planes(high - low, body, unroll)


def residual(v, vo, g, go, cx, cf, co, comp, x):
    here, total = gather_sum(v, comp, x + vo, cx, cf, x + co)
    return g[comp, x + go] - cf[DG, x + co] * here + total


def copied(copies):
    for copy in copies:
        copy.start()
    for copy in copies:
        copy.wait()


def pack_fine_x(f_in, ids_in, xup, xdown, f, ids, arrived):
    copied(
        [pltpu.make_async_copy(ids_in.at[5 * k : 5 * k + 3], ids.at[3 * k : 3 * k + 3], arrived.at[k]) for k in range(2)]
        + [
            pltpu.make_async_copy(f_in.at[:, 6 * k + n], f.at[:, 2 * k + n], arrived.at[2 + 2 * k + n])
            for k in range(2)
            for n in range(2)
        ]
    )
    for n, out in enumerate((xdown, xup)):
        for c in range(3):
            for k in range(2):
                out[2 * c + k] = f[c, 2 * n + k]
        for k in range(3):
            out[6 + k] = materials(ids[3 * n + k])


def pack_fine_y(f_in, ids_in, yup, ydown, f, ids, arrived):
    copied(
        [pltpu.make_async_copy(ids_in.at[x : x + 2], ids.at[x : x + 2], arrived.at[8 + x // 2]) for x in (0, 2, 4, 6)]
        + [pltpu.make_async_copy(f_in.at[:, x], f.at[:, x], arrived.at[x]) for x in range(8)]
    )
    for x in range(8):
        eta = materials(ids[x])
        for out, at, eta_at in ((yup, 13, 12), (ydown, 0, 0)):
            pack_rows(out, x, 8, [f[c, x, at : at + 3] for c in range(3)])
            put_eta_rows(out, 9, x, eta[eta_at : eta_at + 4])


def pack_rows(out, n, spill, rows):
    out[n, 0:3] = rows[0]
    out[n, 3:6] = rows[1]
    out[n, 6:8] = rows[2][0:2]
    out[spill + n // 8, n % 8 : n % 8 + 1] = rows[2][2:3]


def put_eta_rows(out, first, n, rows):
    at = 4 * (n % 2)
    out[first + n // 2, at : at + 4] = rows


def fine_source(f, low, high, c, x):
    if x < 0:
        return kept("gx", 1, low[2 * c + x + 2])
    if x < 8:
        return f[c, x]
    return kept("gx", -1, high[2 * c + x - 8])


def fine_eta(ids, low, high, x):
    if x < 0:
        return kept("gx", 1, low[6 + x + 3])
    if x < 8:
        return materials(ids[x])
    return kept("gx", -1, high[6 + x - 8])


def pack_corners(low, high, up, down):
    for n, x in enumerate((-2, -1, 8, 9)):
        rows = [fine_source(None, low, high, c, x) for c in range(3)]
        for out, at in ((up, 13), (down, 0)):
            pack_rows(out, n, 4, [row[at : at + 3] for row in rows])
    for n, x in enumerate((-3, -2, -1, 8, 9, 10)):
        eta = fine_eta(None, low, high, x)
        put_eta_rows(up, 5, n, eta[12:16])
        put_eta_rows(down, 5, n, eta[0:4])
    for out in (up, down):
        out[4, 4:8] = jnp.zeros((4, low.shape[-1]), F32)


def fine_rows(g, eta, i, source, viscosity, low, high, n, spill, first):
    blank = jnp.zeros((1, source[0].shape[-1]), F32) if source else None
    if source:
        for c in range(3):
            g[c, i, 4:20] = source[c]
            g[c, i, 0:1] = blank
            g[c, i, 23:24] = blank
    for side, at, row, step in ((low, 1, 0, 1), (high, 20, 20, -1)):
        if source:
            tile = kept("gy", step, side[n, 0:8])
            g[0, i, at : at + 3] = tile[0:3]
            g[1, i, at : at + 3] = tile[3:6]
            g[2, i, at : at + 2] = tile[6:8]
            g[2, i, at + 2 : at + 3] = kept("gy", step, side[spill, n : n + 1])
        else:
            part = 4 * (n % 2)
            eta[i, row : row + 4] = kept("gy", step, side[first + n // 2, part : part + 4])
    if viscosity is not None:
        eta[i, 4:20] = viscosity


def fine_first(va, g, cf, i):
    for c in range(3):
        va[c, i] = cf[EI, i] * g[c, i]


def fine_inner(f, ids, ylow, yhigh, v0, va, g, eta, cx, cf):
    for x in range(8):
        fine_rows(g, eta, x, [f[c, x] for c in range(3)], None, ylow, yhigh, x, 8, 9)
        fine_rows(g, eta, x, None, materials(ids[x]), ylow, yhigh, x, 8, 9)
    for i in range(7):
        face_plane(eta, cx, i, 1.0)
    for i in range(6):
        cell_plane(eta, cf, i, 1.0)
        for c in range(3):
            va[c, i] = cf[EI, i] * g[c, i + 1]
    sweep(va, 0, g, 1, cx, cf, 0, v0, -1, 1, 5, U0)


def fine_down(*refs):
    xlow, xhigh, clow, chigh = refs[0:4]
    inner, outer = refs[4:10], refs[10:16]
    f1, eta1, up, down, pairs, rest = refs[16:22]
    v0, va, g, eta, cx, cf = fine_set(inner, outer)
    nz = xlow.shape[-1]
    for n, x in enumerate((-2, -1, 8, 9)):
        rows = [fine_source(None, xlow, xhigh, c, x) for c in range(3)]
        fine_rows(outer[2], None, n, rows, None, clow, chigh, n, 4, 5)
    for n, x in enumerate((-3, -2, -1, 8, 9, 10)):
        fine_rows(None, outer[3], n, None, fine_eta(None, xlow, xhigh, x), clow, chigh, n, 4, 5)
    for i in (0, 1, 2, 10, 11, 12):
        face_plane(eta, cx, i, 1.0)
    for i in (0, 1, 2, 9, 10, 11):
        cell_plane(eta, cf, i, 1.0)
        fine_first(va, g, cf, i)
    sweep(va, 2, g, 2, cx, cf, 2, v0, 1, -1, 2, U0)
    sweep(va, 2, g, 2, cx, cf, 2, v0, 1, 6, 9, U0)

    def down_pair(k):
        for c in range(3):
            x = 2 * k
            total = residual(v0, 1, g, 2, cx, cf, 2, c, x) + residual(v0, 1, g, 2, cx, cf, 2, c, x + 1)
            put_plane(pairs, c * 4 + k, total)

    planes(4, down_pair, U0)

    def eta_pair(k):
        put_plane(pairs, 12 + k, eta[2 * k + 1] + eta[2 * k + 2])

    planes(6, eta_pair, U0)
    for n in range(18):
        row_pairs(pairs, n, 4, 8, rest, n * 8)
    coarse = split_dot(rest[...], pair_matrix(nz)) * 0.125
    for n in range(12):
        block = coarse[n * 8 : n * 8 + 8]
        f1[n // 4, n % 4] = block
        up[n] = block
        down[n] = block
    for n in range(6):
        block = coarse[96 + n * 8 : 96 + n * 8 + 8]
        eta1[n] = block
        if n < 5:
            up[12 + n] = block
        if n > 0:
            down[12 + n - 1] = block


def lane_blocks(planes, nz):
    width = min(nz, 128)
    return (planes, nz // width, 24, width)


def put_plane(ref, n, value):
    width = ref.shape[-1]
    for b in range(ref.shape[1]):
        ref[n, b] = value[:, b * width : b * width + width]


def row_pairs(ref, n, at, count, out, row):
    width = ref.shape[-1]
    for b in range(ref.shape[1]):
        total = ref[n, b, pl.ds(at, count, stride=2), :] + ref[n, b, pl.ds(at + 1, count, stride=2), :]
        out[row : row + count, b * width : b * width + width] = total


def row_copies(ref, n, value):
    width = ref.shape[-1]
    count = value.shape[0]
    for b in range(ref.shape[1]):
        block = value[:, b * width : b * width + width]
        ref[n, b, pl.ds(0, count, stride=2), :] = block
        ref[n, b, pl.ds(1, count, stride=2), :] = block


def get_plane(ref, n):
    return jnp.concatenate([ref[n, b] for b in range(ref.shape[1])], axis=1)


def fine_rim(low, high, *refs):
    _, va, g, eta, cx, cf = fine_set(refs[0:6], refs[6:12])
    rim = refs[12]
    nz = low.shape[-1]
    blank = jnp.zeros((4, nz), F32)
    for n, (side, step) in enumerate(((low, 1), (high, -1))):
        rows = [jnp.concatenate([blank, kept("gx", step, side[k]), blank], axis=0) for k in range(4)]
        edge, k, inner, face, far = ((0, 0, 1, 1, 0), (13, 11, 10, 11, 12))[n]
        weight = plane_coefficients(rows[3], eta[edge], eta[1 if n == 0 else 12], 1.0)[EI]
        for c in range(3):
            here = va[c, k]
            total = cx[far] * (weight * rows[c]) + cx[face] * va[c, inner]
            total = total + cf[YP, k] * next_row(here) + cf[YM, k] * last_row(here)
            total = total + cf[ZP, k] * next_lane(here) + cf[ZM, k] * last_lane(here)
            rim[c, n] = (1.0 / 3.0) * here + cf[EI, k] * (g[c, k] + total)


def pack_middle_y(f1, eta1, low, high, f, ids, up, down, late_up, late_down):
    for c in range(3):
        late_up[c] = f[c, 5]
        late_down[c] = f[c, 2]
    late_up[3] = materials(ids[4])
    late_down[3] = materials(ids[3])

    def source(c, x):
        if x < 0:
            return kept("gx", 1, low[4 * c + x + 4])
        if x < 4:
            return f1[c, x]
        return kept("gx", -1, high[4 * c + x - 4])

    def viscosity(x):
        if x < 0:
            return kept("gx", 1, low[12 + x + 5])
        if x < 4:
            return eta1[x + 1]
        return kept("gx", -1, high[12 + x - 4])

    for i in range(12):
        rows = [source(c, i - 4) for c in range(3)]
        for out, at in ((up, 4), (down, 0)):
            out[i, 0:4] = rows[0][at : at + 4]
            out[i, 4:8] = rows[1][at : at + 4]
            out[12 + i + 1, 0:4] = rows[2][at : at + 4]
    for out in (up, down):
        out[12, 0:4] = jnp.zeros((4, f1.shape[-1]), F32)
        out[25, 0:4] = jnp.zeros((4, f1.shape[-1]), F32)
        out[27, 6:8] = jnp.zeros((2, f1.shape[-1]), F32)
    for j in range(14):
        eta = viscosity(j - 5)
        up[12 + j, 4:8] = eta[4:8]
        down[12 + j, 4:8] = eta[0:4]
        up[26 + j // 8, j % 8 : j % 8 + 1] = eta[3:4]
        down[26 + j // 8, j % 8 : j % 8 + 1] = eta[4:5]


def middle_down(f1, eta1, xlow, xhigh, ylow, yhigh, v1, g, cx, cf, own, up, down, far_up, far_down, eta, va, pairs, rest):
    nz = f1.shape[-1]
    blank = jnp.zeros((4, nz), F32)

    def source(c, x):
        if x < 0:
            return kept("gx", 1, xlow[4 * c + x + 4])
        if x < 4:
            return f1[c, x]
        return kept("gx", -1, xhigh[4 * c + x - 4])

    def viscosity(x):
        if x < 0:
            return kept("gx", 1, xlow[12 + x + 5])
        if x < 4:
            return eta1[x + 1]
        return kept("gx", -1, xhigh[12 + x - 4])

    for c in range(3):
        for i in range(12):
            g[c, i, 8:16] = source(c, i - 4)
            g[c, i, 0:4] = blank
            g[c, i, 20:24] = blank
            for side, at, step in ((ylow, 4, 1), (yhigh, 16, -1)):
                rows = side[i, 4 * c : 4 * c + 4] if c < 2 else side[13 + i, 0:4]
                g[c, i, at : at + 4] = kept("gy", step, rows)
    for j in range(14):
        eta[j, 0:4] = blank
        eta[j, 20:24] = blank
        eta[j, 8:16] = viscosity(j - 5)
        eta[j, 4:8] = kept("gy", 1, ylow[12 + j, 4:8])
        eta[j, 3:4] = kept("gy", 1, ylow[26 + j // 8, j % 8 : j % 8 + 1])
        eta[j, 16:20] = kept("gy", -1, yhigh[12 + j, 4:8])
        eta[j, 20:21] = kept("gy", -1, yhigh[26 + j // 8, j % 8 : j % 8 + 1])

    coefficients(eta, cx, cf, 12, 0.25, U1)

    plane = jnp.zeros((24, nz), F32)
    for c in range(3):
        for i in (0, 13):
            va[c, i] = plane
            v1[c, i] = plane

    def start(i):
        for c in range(3):
            va[c, i + 1] = cf[EI, i] * g[c, i]

    planes(12, start, U1)
    sweep(va, 5, g, 4, cx, cf, 4, v1, 5, -4, 8, U1)

    def down_pair(k):
        for c in range(3):
            x = 2 * k
            total = residual(v1, 1, g, 0, cx, cf, 0, c, x) + residual(v1, 1, g, 0, cx, cf, 0, c, x + 1)
            put_plane(pairs, c * 6 + k, total)

    planes(6, down_pair, U1)

    def eta_pair(k):
        put_plane(pairs, 18 + k, eta[2 * k + 1] + eta[2 * k + 2])

    planes(6, eta_pair, U1)
    for k in range(6):
        for c in range(3):
            row_pairs(pairs, c * 6 + k, 8, 4, rest, 16 * k + 4 * c)
        row_pairs(pairs, 18 + k, 8, 4, rest, 16 * k + 12)
    coarse = split_dot(rest[...], pair_matrix(nz)) * 0.125
    for k in range(6):
        own[k] = coarse[16 * k : 16 * k + 16]
    for t in range(4):
        source_rows = own[t + 1, 0:12]
        up[t, 0:12] = source_rows
        up[t, 12:16] = own[t, 12:16]
        down[t, 0:12] = source_rows
        down[t, 12:16] = own[t + 2, 12:16]
        if t < 2:
            far_up[t, 0:12] = source_rows
            far_up[t, 12:16] = own[t, 12:16]
        else:
            far_down[t - 2, 0:12] = source_rows
            far_down[t - 2, 12:16] = own[t + 2, 12:16]


def pack_coarse_y(own, low2, low3, high2, high3, strip):
    strip[0, 0:12] = jnp.zeros((12, own.shape[-1]), F32)
    strip[17, 0:12] = jnp.zeros((12, own.shape[-1]), F32)
    for t in range(2):
        rows = kept("gx", 3, low3[t])
        strip[1 + t, 0:12] = rows[0:12]
        strip[t, 12:16] = rows[12:16]
        rows = kept("gx", -3, high3[t])
        strip[15 + t, 0:12] = rows[0:12]
        strip[16 + t, 12:16] = rows[12:16]
    for t in range(4):
        rows = kept("gx", 2, low2[t])
        strip[3 + t, 0:12] = rows[0:12]
        strip[2 + t, 12:16] = rows[12:16]
        strip[7 + t, 0:12] = own[1 + t, 0:12]
        rows = kept("gx", -2, high2[t])
        strip[11 + t, 0:12] = rows[0:12]
        strip[12 + t, 12:16] = rows[12:16]
    for t in range(6):
        strip[6 + t, 12:16] = own[t, 12:16]
    for plane, outer, mine in ((6, 5, 0), (11, 12, 5)):
        inside = strip[outer, 12:16] > 0.0
        for c in range(3):
            rows = slice(4 * c, 4 * c + 4)
            strip[plane, rows] = jnp.where(inside, strip[plane, rows], own[mine, rows])


def ascend(
    mid, ym1, ym2, yp1, yp2, v1, g1, cx1, cf1, rim,
    v0i, vai, g0i, eta0i, cx0i, cf0i, v0o, vao, g0o, eta0o, cx0o, cf0o, out,
    eta2, g2, cx2, cf2, va2, vb2, rows2, wide1, va1, vb1, rows1, wide0, va0, vb0, result, sent,
):
    v0, _, g0, _, cx0, cf0 = fine_set((v0i, vai, g0i, eta0i, cx0i, cf0i), (v0o, vao, g0o, eta0o, cx0o, cf0o))
    nz2, nz1 = mid.shape[-1], v1.shape[-1]
    blank = jnp.zeros((4, nz2), F32)
    sides = ((ym2, 2), (ym1, 1), (mid, 0), (yp1, -1), (yp2, -2))
    for j in range(18):
        for n, (side, step) in enumerate(sides):
            rows = kept("gy", step, side[j]) if step else side[j]
            eta2[j, 4 * n : 4 * n + 4] = rows[12:16]
            if 1 <= j <= 16:
                for c in range(3):
                    g2[c, j - 1, 4 * n : 4 * n + 4] = rows[4 * c : 4 * c + 4]
        eta2[j, 20:24] = blank
        if 1 <= j <= 16:
            for c in range(3):
                g2[c, j - 1, 20:24] = blank
    coefficients(eta2, cx2, cf2, 16, 0.0625, U2)

    def start(i):
        for c in range(3):
            va2[c, i] = cf2[EI, i] * g2[c, i]

    planes(16, start, U2)
    source, target = va2, vb2
    for s in range(1, 6):
        sweep(source, 0, g2, 0, cx2, cf2, 0, target, 0, s, 16 - s, U2)
        source, target = target, source

    for c in range(3):
        for k in range(6):
            rows2[(c * 6 + k) * 16 : (c * 6 + k) * 16 + 16] = source[c, 5 + k, 4:20]
    spread = split_dot(rows2[...], copy_matrix(nz2))
    for n in range(18):
        block = spread[n * 16 : n * 16 + 12]
        row_copies(wide1, n, block)
    for c in range(3):
        for i in range(10):
            va1[c, i] = v1[c, i + 2] + get_plane(wide1, c * 6 + (i - 3) // 2 + 2)
    sweep(va1, 3, g1, 4, cx1, cf1, 4, vb1, 3, -2, 6, U1)
    sweep(vb1, 3, g1, 4, cx1, cf1, 4, va1, 3, -1, 5, U1)

    for c in range(3):
        for k in range(6):
            rows1[(c * 6 + k) * 16 : (c * 6 + k) * 16 + 16] = va1[c, 2 + k, 6:22]
    spread = split_dot(rows1[...], copy_matrix(nz1))
    for n in range(18):
        block = spread[n * 16 : n * 16 + 12]
        row_copies(wide0, n, block)

    for k in range(6):
        for c in range(3):
            block = get_plane(wide0, c * 6 + k)
            va0[c, 2 * k] = (v0[c, 2 * k - 1] if k > 0 else rim[c, 0]) + block
            va0[c, 2 * k + 1] = (v0[c, 2 * k] if k < 5 else rim[c, 1]) + block
    sweep(va0, 2, g0, 2, cx0, cf0, 2, vb0, 2, -1, 9, U0)

    def final(x):
        for c in range(3):
            here, total = gather_sum(vb0, c, x + 2, cx0, cf0, x + 2)
            value = (1.0 / 3.0) * here + cf0[EI, x + 2] * (g0[c, x + 2] + total)
            result[c, x] = value[4:20]
        pltpu.make_async_copy(result.at[:, x], out.at[:, x], sent.at[x]).start()

    planes(8, final, U0)
    for x in range(8):
        pltpu.make_async_copy(result.at[:, x], out.at[:, x], sent.at[x]).wait()


def typed(shape):
    return shape if isinstance(shape, jax.ShapeDtypeStruct) else jax.ShapeDtypeStruct(shape, F32)


def call(body, outs, *args, scratch=(), copies=0, where_in=pltpu.VMEM, where_out=pltpu.VMEM):
    outs = [typed(out) for out in outs]
    scratch_shapes = [pltpu.VMEM(typed(shape).shape, typed(shape).dtype) for shape in scratch]
    if copies:
        scratch_shapes.append(pltpu.SemaphoreType.DMA((copies,)))
    return pl.pallas_call(
        body,
        out_shape=outs,
        in_specs=[pl.BlockSpec(memory_space=where_in)] * len(args),
        out_specs=[pl.BlockSpec(memory_space=where_out)] * len(outs),
        scratch_shapes=scratch_shapes,
        compiler_params=pltpu.CompilerParams(vmem_limit_bytes=VMEM_LIMIT),
    )(*args)


def cycled(array, axis, step):
    size = lax.axis_size(axis)
    return lax.ppermute(array, axis, [(i, (i + step) % size) for i in range(size)])


def per_device(forcing, phase_ids):
    z0 = forcing.shape[-1]
    z1, z2 = z0 // 2, z0 // 4
    inputs = [pltpu.with_memory_space_constraint(a, pltpu.HBM) for a in (forcing, phase_ids)]
    xup, xdown = call(
        pack_fine_x, [(9, 16, z0)] * 2, *inputs,
        scratch=[(3, 4, 16, z0), jax.ShapeDtypeStruct((6, 16, z0), jnp.int32)], copies=6, where_in=pltpu.HBM,
    )
    yup, ydown, f0, ids0 = call(
        pack_fine_y,
        [(13, 8, z0)] * 2 + [forcing.shape, jax.ShapeDtypeStruct(phase_ids.shape, jnp.int32)],
        *inputs, copies=12, where_in=pltpu.HBM,
    )
    xlow, xhigh = cycled(xup, "gx", 1), cycled(xdown, "gx", -1)
    ylow, yhigh = cycled(yup, "gy", 1), cycled(ydown, "gy", -1)
    up, down = call(pack_corners, [(8, 8, z0)] * 2, xlow, xhigh)
    clow, chigh = cycled(up, "gy", 1), cycled(down, "gy", -1)
    inner = call(
        fine_inner,
        [(3, 4, 24, z0), (3, 6, 24, z0), (3, 8, 24, z0), (8, 24, z0), (7, 24, z0), (6, 6, 24, z0)],
        f0, ids0, ylow, yhigh,
    )
    *outer, f1, eta1, up, down = call(
        fine_down,
        [(3, 6, 24, z0), (3, 6, 24, z0), (3, 4, 24, z0), (6, 24, z0), (6, 24, z0), (6, 6, 24, z0), (3, 4, 8, z1), (6, 8, z1), (17, 8, z1), (17, 8, z1)],
        xlow, xhigh, clow, chigh, *inner,
        scratch=[lane_blocks(18, z0), (144, z0)],
    )
    xlow, xhigh = cycled(up, "gx", 1), cycled(down, "gx", -1)
    up, down, late_up, late_down = call(
        pack_middle_y, [(28, 8, z1)] * 2 + [(4, 16, z0)] * 2, f1, eta1, xlow, xhigh, f0, ids0
    )
    ylow, yhigh = cycled(up, "gy", 1), cycled(down, "gy", -1)
    late_low, late_high = cycled(late_up, "gx", 1), cycled(late_down, "gx", -1)
    (rim,) = call(fine_rim, [(3, 2, 24, z0)], late_low, late_high, *inner, *outer)
    v1, g1, cx1, cf1, own, up, down, far_up, far_down = call(
        middle_down,
        [(3, 14, 24, z1), (3, 12, 24, z1), (13, 24, z1), (6, 12, 24, z1), (6, 16, z2), (4, 16, z2), (4, 16, z2), (2, 16, z2), (2, 16, z2)],
        f1, eta1, xlow, xhigh, ylow, yhigh,
        scratch=[(14, 24, z1), (3, 14, 24, z1), lane_blocks(24, z1), (96, z1)],
    )
    low2, high2 = cycled(up, "gx", 2), cycled(down, "gx", -2)
    low3, high3 = cycled(far_up, "gx", 3), cycled(far_down, "gx", -3)
    (strip,) = call(pack_coarse_y, [(18, 16, z2)], own, low2, low3, high2, high3)
    ym1, yp1 = cycled(strip, "gy", 1), cycled(strip, "gy", -1)
    ym2, yp2 = cycled(strip, "gy", 2), cycled(strip, "gy", -2)
    (velocity,) = call(
        ascend,
        [forcing.shape],
        strip, ym1, ym2, yp1, yp2, v1, g1, cx1, cf1, rim, *inner, *outer,
        scratch=[
            (18, 24, z2), (3, 16, 24, z2), (17, 24, z2), (6, 16, 24, z2), (3, 16, 24, z2), (3, 16, 24, z2),
            (288, z2), lane_blocks(18, z1), (3, 10, 24, z1), (3, 10, 24, z1),
            (288, z1), lane_blocks(18, z0), (3, 12, 24, z0), (3, 12, 24, z0), forcing.shape,
        ],
        copies=8,
        where_out=pltpu.HBM,
    )
    return velocity


def solution(mesh):
    return jax.shard_map(
        per_device,
        mesh=mesh,
        in_specs=(P(None, "gx", "gy", None), P("gx", "gy", None)),
        out_specs=P(None, "gx", "gy", None),
        check_vma=False,
    )
```

```python
import functools

import jax
import jax.numpy as jnp
from jax import lax
from jax.experimental import pallas as pl
from jax.experimental.pallas import tpu as pltpu
from jax.sharding import PartitionSpec as P

F32 = jnp.float32
BF16 = jnp.bfloat16
WEIGHT = 2.0 / 3.0
VMEM_LIMIT = 24 * 1024 * 1024
U0, U1, U2 = 12, 12, 16


def materials(ids):
    eta = jnp.where(ids == 3, F32(4.0), F32(0.0))
    eta = jnp.where(ids == 2, F32(1.5), eta)
    eta = jnp.where(ids == 1, F32(0.6), eta)
    return jnp.where(ids == 0, F32(0.2), eta)


def lanes_of(shape):
    return lax.broadcasted_iota(jnp.int32, shape, len(shape) - 1)


def next_row(v):
    return pltpu.roll(v, v.shape[0] - 1, 0)


def last_row(v):
    return pltpu.roll(v, 1, 0)


def next_lane(v):
    return pltpu.roll(v, v.shape[1] - 1, 1)


def last_lane(v):
    return pltpu.roll(v, 1, 1)


def planes(count, body, unroll):
    steps = count // unroll if unroll < count else 0

    def step(n, _):
        for k in range(unroll):
            body(n * unroll + k)
        return 0

    if steps > 0:
        lax.fori_loop(0, steps, step, 0)
    for i in range(steps * unroll, count):
        body(i)


def kept(axis, step, value):
    place = lax.axis_index(axis) - step
    return jnp.where((place >= 0) & (place < lax.axis_size(axis)), value, 0.0)


class Spliced:
    def __init__(self, middle, outer, first, count, flat=False):
        self.middle, self.outer, self.first, self.count, self.flat = middle, outer, first, count, flat

    def place(self, key):
        lead, i = ((), key) if self.flat else ((key[0],), key[1])
        rest = () if self.flat else tuple(key[2:])
        if self.first <= i < self.first + self.count:
            return self.middle, lead + (i - self.first,) + rest
        return self.outer, lead + (i if i < self.first else i - self.count,) + rest

    def __getitem__(self, key):
        ref, at = self.place(key)
        return ref[at]

    def __setitem__(self, key, value):
        ref, at = self.place(key)
        ref[at] = value


def fine_set(inner, outer):
    spans = ((3, 4), (3, 6), (2, 8), (3, 8), (3, 7), (3, 6))
    return [Spliced(a, b, *span, flat=n in (3, 4)) for n, (a, b, span) in enumerate(zip(inner, outer, spans))]


def split_dot(rows, matrix):
    high = rows.astype(BF16)
    low = (rows - high.astype(F32)).astype(BF16)
    return jnp.dot(high, matrix, preferred_element_type=F32) + jnp.dot(
        low, matrix, preferred_element_type=F32
    )


def pair_matrix(fine):
    shape = (fine, fine // 2)
    row = lax.broadcasted_iota(jnp.int32, shape, 0)
    col = lax.broadcasted_iota(jnp.int32, shape, 1)
    return jnp.where((row == 2 * col) | (row == 2 * col + 1), F32(1), F32(0)).astype(BF16)


def copy_matrix(coarse):
    shape = (coarse, 2 * coarse)
    row = lax.broadcasted_iota(jnp.int32, shape, 0)
    col = lax.broadcasted_iota(jnp.int32, shape, 1)
    return jnp.where((col == 2 * row) | (col == 2 * row + 1), F32(1), F32(0)).astype(BF16)


YP, YM, ZP, ZM, DG, EI = range(6)


def plane_coefficients(below, here, above, scale):
    half = 0.5 * scale
    lane = lanes_of(here.shape)
    first = lane == 0
    final = lane == here.shape[1] - 1
    yp, ym = next_row(here), last_row(here)
    zp, zm = next_lane(here), last_lane(here)

    def ghost(q):
        return jnp.where(q > 0.0, q, here)

    around = ghost(yp) + ghost(ym) + ghost(below) + ghost(above)
    around = around + jnp.where(final, here, zp) + jnp.where(first, here, zm)
    diag = scale * (3.0 * here + 0.5 * around)
    return (
        half * (here + yp),
        half * (here + ym),
        jnp.where(final, 0.0, half * (here + zp)),
        jnp.where(first, 0.0, half * (here + zm)),
        diag,
        jnp.where(here > 0.0, WEIGHT / diag, 0.0),
    )


def coefficients(eta, cx, cf, layers, scale, unroll):
    planes(layers + 1, lambda i: face_plane(eta, cx, i, scale), unroll)
    planes(layers, lambda i: cell_plane(eta, cf, i, scale), unroll)


def face_plane(eta, cx, i, scale):
    cx[i] = (0.5 * scale) * (eta[i] + eta[i + 1])


def cell_plane(eta, cf, i, scale):
    made = plane_coefficients(eta[i], eta[i + 1], eta[i + 2], scale)
    for n, value in enumerate(made):
        cf[n, i] = value


def gather_sum(v, comp, i, cx, cf, k):
    here = v[comp, i]
    total = cx[k] * v[comp, i - 1] + cx[k + 1] * v[comp, i + 1]
    total = total + cf[YP, k] * next_row(here) + cf[YM, k] * last_row(here)
    total = total + cf[ZP, k] * next_lane(here) + cf[ZM, k] * last_lane(here)
    return here, total


def sweep(v, vo, g, go, cx, cf, co, out, oo, low, high, unroll):
    vo, go, co, oo = vo + low, go + low, co + low, oo + low

    def body(n):
        for comp in range(3):
            here, total = gather_sum(v, comp, n + vo, cx, cf, n + co)
            out[comp, n + oo] = (1.0 / 3.0) * here + cf[EI, n + co] * (g[comp, n + go] + total)

    planes(high - low, body, unroll)


def residual(v, vo, g, go, cx, cf, co, comp, x):
    here, total = gather_sum(v, comp, x + vo, cx, cf, x + co)
    return g[comp, x + go] - cf[DG, x + co] * here + total


def copied(copies):
    for copy in copies:
        copy.start()
    for copy in copies:
        copy.wait()


def pack_fine_x(f_in, ids_in, xup, xdown, f, ids, arrived):
    copied(
        [pltpu.make_async_copy(ids_in.at[5 * k : 5 * k + 3], ids.at[3 * k : 3 * k + 3], arrived.at[k]) for k in range(2)]
        + [
            pltpu.make_async_copy(f_in.at[:, 6 * k + n], f.at[:, 2 * k + n], arrived.at[2 + 2 * k + n])
            for k in range(2)
            for n in range(2)
        ]
    )
    for n, out in enumerate((xdown, xup)):
        for c in range(3):
            for k in range(2):
                out[2 * c + k] = f[c, 2 * n + k]
        for k in range(3):
            out[6 + k] = materials(ids[3 * n + k])


def pack_fine_y(f_in, ids_in, yup, ydown, f, ids, arrived):
    copied(
        [pltpu.make_async_copy(ids_in.at[x : x + 2], ids.at[x : x + 2], arrived.at[8 + x // 2]) for x in (0, 2, 4, 6)]
        + [pltpu.make_async_copy(f_in.at[:, x], f.at[:, x], arrived.at[x]) for x in range(8)]
    )
    for x in range(8):
        eta = materials(ids[x])
        for out, at, eta_at in ((yup, 13, 12), (ydown, 0, 0)):
            pack_rows(out, x, 8, [f[c, x, at : at + 3] for c in range(3)])
            put_eta_rows(out, 9, x, eta[eta_at : eta_at + 4])


def pack_rows(out, n, spill, rows):
    out[n, 0:3] = rows[0]
    out[n, 3:6] = rows[1]
    out[n, 6:8] = rows[2][0:2]
    out[spill + n // 8, n % 8 : n % 8 + 1] = rows[2][2:3]


def put_eta_rows(out, first, n, rows):
    at = 4 * (n % 2)
    out[first + n // 2, at : at + 4] = rows


def fine_source(f, low, high, c, x):
    if x < 0:
        return kept("gx", 1, low[2 * c + x + 2])
    if x < 8:
        return f[c, x]
    return kept("gx", -1, high[2 * c + x - 8])


def fine_eta(ids, low, high, x):
    if x < 0:
        return kept("gx", 1, low[6 + x + 3])
    if x < 8:
        return materials(ids[x])
    return kept("gx", -1, high[6 + x - 8])


def pack_corners(low, high, up, down):
    for n, x in enumerate((-2, -1, 8, 9)):
        rows = [fine_source(None, low, high, c, x) for c in range(3)]
        for out, at in ((up, 13), (down, 0)):
            pack_rows(out, n, 4, [row[at : at + 3] for row in rows])
    for n, x in enumerate((-3, -2, -1, 8, 9, 10)):
        eta = fine_eta(None, low, high, x)
        put_eta_rows(up, 5, n, eta[12:16])
        put_eta_rows(down, 5, n, eta[0:4])
    for out in (up, down):
        out[4, 4:8] = jnp.zeros((4, low.shape[-1]), F32)


def fine_rows(g, eta, i, source, viscosity, low, high, n, spill, first):
    blank = jnp.zeros((1, source[0].shape[-1]), F32) if source else None
    if source:
        for c in range(3):
            g[c, i, 4:20] = source[c]
            g[c, i, 0:1] = blank
            g[c, i, 23:24] = blank
    for side, at, row, step in ((low, 1, 0, 1), (high, 20, 20, -1)):
        if source:
            tile = kept("gy", step, side[n, 0:8])
            g[0, i, at : at + 3] = tile[0:3]
            g[1, i, at : at + 3] = tile[3:6]
            g[2, i, at : at + 2] = tile[6:8]
            g[2, i, at + 2 : at + 3] = kept("gy", step, side[spill, n : n + 1])
        else:
            part = 4 * (n % 2)
            eta[i, row : row + 4] = kept("gy", step, side[first + n // 2, part : part + 4])
    if viscosity is not None:
        eta[i, 4:20] = viscosity


def fine_first(va, g, cf, i):
    for c in range(3):
        va[c, i] = cf[EI, i] * g[c, i]


def fine_inner(f, ids, ylow, yhigh, v0, va, g, eta, cx, cf):
    for x in range(8):
        fine_rows(g, eta, x, [f[c, x] for c in range(3)], None, ylow, yhigh, x, 8, 9)
        fine_rows(g, eta, x, None, materials(ids[x]), ylow, yhigh, x, 8, 9)
    for i in range(7):
        face_plane(eta, cx, i, 1.0)
    for i in range(6):
        cell_plane(eta, cf, i, 1.0)
        for c in range(3):
            va[c, i] = cf[EI, i] * g[c, i + 1]
    sweep(va, 0, g, 1, cx, cf, 0, v0, -1, 1, 5, U0)


def fine_down(*refs):
    xlow, xhigh, clow, chigh = refs[0:4]
    inner, outer = refs[4:10], refs[10:16]
    f1, eta1, up, down, pairs, rest = refs[16:22]
    v0, va, g, eta, cx, cf = fine_set(inner, outer)
    nz = xlow.shape[-1]
    for n, x in enumerate((-2, -1, 8, 9)):
        rows = [fine_source(None, xlow, xhigh, c, x) for c in range(3)]
        fine_rows(outer[2], None, n, rows, None, clow, chigh, n, 4, 5)
    for n, x in enumerate((-3, -2, -1, 8, 9, 10)):
        fine_rows(None, outer[3], n, None, fine_eta(None, xlow, xhigh, x), clow, chigh, n, 4, 5)
    for i in (0, 1, 2, 10, 11, 12):
        face_plane(eta, cx, i, 1.0)
    for i in (0, 1, 2, 9, 10, 11):
        cell_plane(eta, cf, i, 1.0)
        fine_first(va, g, cf, i)
    sweep(va, 2, g, 2, cx, cf, 2, v0, 1, -1, 2, U0)
    sweep(va, 2, g, 2, cx, cf, 2, v0, 1, 6, 9, U0)

    def down_pair(k):
        for c in range(3):
            x = 2 * k
            total = residual(v0, 1, g, 2, cx, cf, 2, c, x) + residual(v0, 1, g, 2, cx, cf, 2, c, x + 1)
            put_plane(pairs, c * 4 + k, total)

    planes(4, down_pair, U0)

    def eta_pair(k):
        put_plane(pairs, 12 + k, eta[2 * k + 1] + eta[2 * k + 2])

    planes(6, eta_pair, U0)
    for n in range(18):
        row_pairs(pairs, n, 4, 8, rest, n * 8)
    coarse = split_dot(rest[...], pair_matrix(nz)) * 0.125
    for n in range(12):
        block = coarse[n * 8 : n * 8 + 8]
        f1[n // 4, n % 4] = block
        up[n] = block
        down[n] = block
    for n in range(6):
        block = coarse[96 + n * 8 : 96 + n * 8 + 8]
        eta1[n] = block
        if n < 5:
            up[12 + n] = block
        if n > 0:
            down[12 + n - 1] = block


def lane_blocks(planes, nz):
    width = min(nz, 128)
    return (planes, nz // width, 24, width)


def put_plane(ref, n, value):
    width = ref.shape[-1]
    for b in range(ref.shape[1]):
        ref[n, b] = value[:, b * width : b * width + width]


def row_pairs(ref, n, at, count, out, row):
    width = ref.shape[-1]
    for b in range(ref.shape[1]):
        total = ref[n, b, pl.ds(at, count, stride=2), :] + ref[n, b, pl.ds(at + 1, count, stride=2), :]
        out[row : row + count, b * width : b * width + width] = total


def row_copies(ref, n, value):
    width = ref.shape[-1]
    count = value.shape[0]
    for b in range(ref.shape[1]):
        block = value[:, b * width : b * width + width]
        ref[n, b, pl.ds(0, count, stride=2), :] = block
        ref[n, b, pl.ds(1, count, stride=2), :] = block


def get_plane(ref, n):
    return jnp.concatenate([ref[n, b] for b in range(ref.shape[1])], axis=1)


def fine_rim(low, high, *refs):
    _, va, g, eta, cx, cf = fine_set(refs[0:6], refs[6:12])
    rim = refs[12]
    nz = low.shape[-1]
    blank = jnp.zeros((4, nz), F32)
    for n, (side, step) in enumerate(((low, 1), (high, -1))):
        rows = [jnp.concatenate([blank, kept("gx", step, side[k]), blank], axis=0) for k in range(4)]
        edge, k, inner, face, far = ((0, 0, 1, 1, 0), (13, 11, 10, 11, 12))[n]
        weight = plane_coefficients(rows[3], eta[edge], eta[1 if n == 0 else 12], 1.0)[EI]
        for c in range(3):
            here = va[c, k]
            total = cx[far] * (weight * rows[c]) + cx[face] * va[c, inner]
            total = total + cf[YP, k] * next_row(here) + cf[YM, k] * last_row(here)
            total = total + cf[ZP, k] * next_lane(here) + cf[ZM, k] * last_lane(here)
            rim[c, n] = (1.0 / 3.0) * here + cf[EI, k] * (g[c, k] + total)


def pack_middle_y(f1, eta1, low, high, f, ids, up, down, late_up, late_down):
    for c in range(3):
        late_up[c] = f[c, 5]
        late_down[c] = f[c, 2]
    late_up[3] = materials(ids[4])
    late_down[3] = materials(ids[3])

    def source(c, x):
        if x < 0:
            return kept("gx", 1, low[4 * c + x + 4])
        if x < 4:
            return f1[c, x]
        return kept("gx", -1, high[4 * c + x - 4])

    def viscosity(x):
        if x < 0:
            return kept("gx", 1, low[12 + x + 5])
        if x < 4:
            return eta1[x + 1]
        return kept("gx", -1, high[12 + x - 4])

    for i in range(12):
        rows = [source(c, i - 4) for c in range(3)]
        for out, at in ((up, 4), (down, 0)):
            out[i, 0:4] = rows[0][at : at + 4]
            out[i, 4:8] = rows[1][at : at + 4]
            out[12 + i + 1, 0:4] = rows[2][at : at + 4]
    for out in (up, down):
        out[12, 0:4] = jnp.zeros((4, f1.shape[-1]), F32)
        out[25, 0:4] = jnp.zeros((4, f1.shape[-1]), F32)
        out[27, 6:8] = jnp.zeros((2, f1.shape[-1]), F32)
    for j in range(14):
        eta = viscosity(j - 5)
        up[12 + j, 4:8] = eta[4:8]
        down[12 + j, 4:8] = eta[0:4]
        up[26 + j // 8, j % 8 : j % 8 + 1] = eta[3:4]
        down[26 + j // 8, j % 8 : j % 8 + 1] = eta[4:5]


def middle_down(f1, eta1, xlow, xhigh, ylow, yhigh, v1, g, cx, cf, own, up, down, far_up, far_down, eta, va, pairs, rest):
    nz = f1.shape[-1]
    blank = jnp.zeros((4, nz), F32)

    def source(c, x):
        if x < 0:
            return kept("gx", 1, xlow[4 * c + x + 4])
        if x < 4:
            return f1[c, x]
        return kept("gx", -1, xhigh[4 * c + x - 4])

    def viscosity(x):
        if x < 0:
            return kept("gx", 1, xlow[12 + x + 5])
        if x < 4:
            return eta1[x + 1]
        return kept("gx", -1, xhigh[12 + x - 4])

    for c in range(3):
        for i in range(12):
            g[c, i, 8:16] = source(c, i - 4)
            g[c, i, 0:4] = blank
            g[c, i, 20:24] = blank
            for side, at, step in ((ylow, 4, 1), (yhigh, 16, -1)):
                rows = side[i, 4 * c : 4 * c + 4] if c < 2 else side[13 + i, 0:4]
                g[c, i, at : at + 4] = kept("gy", step, rows)
    for j in range(14):
        eta[j, 0:4] = blank
        eta[j, 20:24] = blank
        eta[j, 8:16] = viscosity(j - 5)
        eta[j, 4:8] = kept("gy", 1, ylow[12 + j, 4:8])
        eta[j, 3:4] = kept("gy", 1, ylow[26 + j // 8, j % 8 : j % 8 + 1])
        eta[j, 16:20] = kept("gy", -1, yhigh[12 + j, 4:8])
        eta[j, 20:21] = kept("gy", -1, yhigh[26 + j // 8, j % 8 : j % 8 + 1])

    coefficients(eta, cx, cf, 12, 0.25, U1)

    plane = jnp.zeros((24, nz), F32)
    for c in range(3):
        for i in (0, 13):
            va[c, i] = plane
            v1[c, i] = plane

    def start(i):
        for c in range(3):
            va[c, i + 1] = cf[EI, i] * g[c, i]

    planes(12, start, U1)
    sweep(va, 5, g, 4, cx, cf, 4, v1, 5, -4, 8, U1)

    def down_pair(k):
        for c in range(3):
            x = 2 * k
            total = residual(v1, 1, g, 0, cx, cf, 0, c, x) + residual(v1, 1, g, 0, cx, cf, 0, c, x + 1)
            put_plane(pairs, c * 6 + k, total)

    planes(6, down_pair, U1)

    def eta_pair(k):
        put_plane(pairs, 18 + k, eta[2 * k + 1] + eta[2 * k + 2])

    planes(6, eta_pair, U1)
    for k in range(6):
        for c in range(3):
            row_pairs(pairs, c * 6 + k, 8, 4, rest, 16 * k + 4 * c)
        row_pairs(pairs, 18 + k, 8, 4, rest, 16 * k + 12)
    coarse = split_dot(rest[...], pair_matrix(nz)) * 0.125
    for k in range(6):
        own[k] = coarse[16 * k : 16 * k + 16]
    for t in range(4):
        source_rows = own[t + 1, 0:12]
        up[t, 0:12] = source_rows
        up[t, 12:16] = own[t, 12:16]
        down[t, 0:12] = source_rows
        down[t, 12:16] = own[t + 2, 12:16]
        if t < 2:
            far_up[t, 0:12] = source_rows
            far_up[t, 12:16] = own[t, 12:16]
        else:
            far_down[t - 2, 0:12] = source_rows
            far_down[t - 2, 12:16] = own[t + 2, 12:16]


def pack_coarse_y(own, low2, low3, high2, high3, rim, strip):
    strip[0, 0:12] = jnp.zeros((12, own.shape[-1]), F32)
    strip[17, 0:12] = jnp.zeros((12, own.shape[-1]), F32)
    for t in range(2):
        rows = kept("gx", 3, low3[t])
        strip[1 + t, 0:12] = rows[0:12]
        strip[t, 12:16] = rows[12:16]
        rows = kept("gx", -3, high3[t])
        strip[15 + t, 0:12] = rows[0:12]
        strip[16 + t, 12:16] = rows[12:16]
    for t in range(4):
        rows = kept("gx", 2, low2[t])
        strip[3 + t, 0:12] = rows[0:12]
        strip[2 + t, 12:16] = rows[12:16]
        strip[7 + t, 0:12] = own[1 + t, 0:12]
        rows = kept("gx", -2, high2[t])
        strip[11 + t, 0:12] = rows[0:12]
        strip[12 + t, 12:16] = rows[12:16]
    for t in range(6):
        strip[6 + t, 12:16] = own[t, 12:16]
    for plane, outer, mine in ((6, 5, 0), (11, 12, 5)):
        inside = strip[outer, 12:16] > 0.0
        for c in range(3):
            rows = slice(4 * c, 4 * c + 4)
            strip[plane, rows] = jnp.where(inside, strip[plane, rows], own[mine, rows])


def ascend(
    mid, ym1, ym2, yp1, yp2, v1, g1, cx1, cf1, rim,
    v0i, vai, g0i, eta0i, cx0i, cf0i, v0o, vao, g0o, eta0o, cx0o, cf0o, out,
    eta2, g2, cx2, cf2, va2, vb2, rows2, wide1, va1, vb1, rows1, wide0, va0, vb0, result, sent,
):
    v0, _, g0, _, cx0, cf0 = fine_set((v0i, vai, g0i, eta0i, cx0i, cf0i), (v0o, vao, g0o, eta0o, cx0o, cf0o))
    nz2, nz1 = mid.shape[-1], v1.shape[-1]
    blank = jnp.zeros((4, nz2), F32)
    sides = ((ym2, 2), (ym1, 1), (mid, 0), (yp1, -1), (yp2, -2))
    for j in range(18):
        for n, (side, step) in enumerate(sides):
            rows = kept("gy", step, side[j]) if step else side[j]
            eta2[j, 4 * n : 4 * n + 4] = rows[12:16]
            if 1 <= j <= 16:
                for c in range(3):
                    g2[c, j - 1, 4 * n : 4 * n + 4] = rows[4 * c : 4 * c + 4]
        eta2[j, 20:24] = blank
        if 1 <= j <= 16:
            for c in range(3):
                g2[c, j - 1, 20:24] = blank
    coefficients(eta2, cx2, cf2, 16, 0.0625, U2)

    def start(i):
        for c in range(3):
            va2[c, i] = cf2[EI, i] * g2[c, i]

    planes(16, start, U2)
    source, target = va2, vb2
    for s in range(1, 6):
        sweep(source, 0, g2, 0, cx2, cf2, 0, target, 0, s, 16 - s, U2)
        source, target = target, source

    for c in range(3):
        for k in range(6):
            rows2[(c * 6 + k) * 16 : (c * 6 + k) * 16 + 16] = source[c, 5 + k, 4:20]
    spread = split_dot(rows2[...], copy_matrix(nz2))
    for n in range(18):
        block = spread[n * 16 : n * 16 + 12]
        row_copies(wide1, n, block)
    for c in range(3):
        for i in range(10):
            va1[c, i] = v1[c, i + 2] + get_plane(wide1, c * 6 + (i - 3) // 2 + 2)
    sweep(va1, 3, g1, 4, cx1, cf1, 4, vb1, 3, -2, 6, U1)
    sweep(vb1, 3, g1, 4, cx1, cf1, 4, va1, 3, -1, 5, U1)

    for c in range(3):
        for k in range(6):
            rows1[(c * 6 + k) * 16 : (c * 6 + k) * 16 + 16] = va1[c, 2 + k, 6:22]
    spread = split_dot(rows1[...], copy_matrix(nz1))
    for n in range(18):
        block = spread[n * 16 : n * 16 + 12]
        row_copies(wide0, n, block)

    for k in range(6):
        for c in range(3):
            block = get_plane(wide0, c * 6 + k)
            va0[c, 2 * k] = (v0[c, 2 * k - 1] if k > 0 else rim[c, 0]) + block
            va0[c, 2 * k + 1] = (v0[c, 2 * k] if k < 5 else rim[c, 1]) + block
    sweep(va0, 2, g0, 2, cx0, cf0, 2, vb0, 2, -1, 9, U0)

    def final(x):
        for c in range(3):
            here, total = gather_sum(vb0, c, x + 2, cx0, cf0, x + 2)
            value = (1.0 / 3.0) * here + cf0[EI, x + 2] * (g0[c, x + 2] + total)
            result[c, x] = value[4:20]
        pltpu.make_async_copy(result.at[:, x], out.at[:, x], sent.at[x]).start()

    planes(8, final, U0)
    for x in range(8):
        pltpu.make_async_copy(result.at[:, x], out.at[:, x], sent.at[x]).wait()


def typed(shape):
    return shape if isinstance(shape, jax.ShapeDtypeStruct) else jax.ShapeDtypeStruct(shape, F32)


def call(body, outs, *args, scratch=(), copies=0, where_in=pltpu.VMEM, where_out=pltpu.VMEM):
    outs = [typed(out) for out in outs]
    scratch_shapes = [pltpu.VMEM(typed(shape).shape, typed(shape).dtype) for shape in scratch]
    if copies:
        scratch_shapes.append(pltpu.SemaphoreType.DMA((copies,)))
    return pl.pallas_call(
        body,
        out_shape=outs,
        in_specs=[pl.BlockSpec(memory_space=where_in)] * len(args),
        out_specs=[pl.BlockSpec(memory_space=where_out)] * len(outs),
        scratch_shapes=scratch_shapes,
        compiler_params=pltpu.CompilerParams(vmem_limit_bytes=VMEM_LIMIT),
    )(*args)


def cycled(array, axis, step):
    size = lax.axis_size(axis)
    return lax.ppermute(array, axis, [(i, (i + step) % size) for i in range(size)])


def per_device(forcing, phase_ids):
    z0 = forcing.shape[-1]
    z1, z2 = z0 // 2, z0 // 4
    inputs = [pltpu.with_memory_space_constraint(a, pltpu.HBM) for a in (forcing, phase_ids)]
    xup, xdown = call(
        pack_fine_x, [(9, 16, z0)] * 2, *inputs,
        scratch=[(3, 4, 16, z0), jax.ShapeDtypeStruct((6, 16, z0), jnp.int32)], copies=6, where_in=pltpu.HBM,
    )
    yup, ydown, f0, ids0 = call(
        pack_fine_y,
        [(13, 8, z0)] * 2 + [forcing.shape, jax.ShapeDtypeStruct(phase_ids.shape, jnp.int32)],
        *inputs, copies=12, where_in=pltpu.HBM,
    )
    xlow, xhigh = cycled(xup, "gx", 1), cycled(xdown, "gx", -1)
    ylow, yhigh = cycled(yup, "gy", 1), cycled(ydown, "gy", -1)
    up, down = call(pack_corners, [(8, 8, z0)] * 2, xlow, xhigh)
    clow, chigh = cycled(up, "gy", 1), cycled(down, "gy", -1)
    inner = call(
        fine_inner,
        [(3, 4, 24, z0), (3, 6, 24, z0), (3, 8, 24, z0), (8, 24, z0), (7, 24, z0), (6, 6, 24, z0)],
        f0, ids0, ylow, yhigh,
    )
    *outer, f1, eta1, up, down = call(
        fine_down,
        [(3, 6, 24, z0), (3, 6, 24, z0), (3, 4, 24, z0), (6, 24, z0), (6, 24, z0), (6, 6, 24, z0), (3, 4, 8, z1), (6, 8, z1), (17, 8, z1), (17, 8, z1)],
        xlow, xhigh, clow, chigh, *inner,
        scratch=[lane_blocks(18, z0), (144, z0)],
    )
    xlow, xhigh = cycled(up, "gx", 1), cycled(down, "gx", -1)
    up, down, late_up, late_down = call(
        pack_middle_y, [(28, 8, z1)] * 2 + [(4, 16, z0)] * 2, f1, eta1, xlow, xhigh, f0, ids0
    )
    ylow, yhigh = cycled(up, "gy", 1), cycled(down, "gy", -1)
    late_low, late_high = cycled(late_up, "gx", 1), cycled(late_down, "gx", -1)
    (rim,) = call(fine_rim, [(3, 2, 24, z0)], late_low, late_high, *inner, *outer)
    v1, g1, cx1, cf1, own, up, down, far_up, far_down = call(
        middle_down,
        [(3, 14, 24, z1), (3, 12, 24, z1), (13, 24, z1), (6, 12, 24, z1), (6, 16, z2), (4, 16, z2), (4, 16, z2), (2, 16, z2), (2, 16, z2)],
        f1, eta1, xlow, xhigh, ylow, yhigh,
        scratch=[(14, 24, z1), (3, 14, 24, z1), lane_blocks(24, z1), (96, z1)],
    )
    low2, high2 = cycled(up, "gx", 2), cycled(down, "gx", -2)
    low3, high3 = cycled(far_up, "gx", 3), cycled(far_down, "gx", -3)
    (strip,) = call(pack_coarse_y, [(18, 16, z2)], own, low2, low3, high2, high3, rim)
    ym1, yp1 = cycled(strip, "gy", 1), cycled(strip, "gy", -1)
    ym2, yp2 = cycled(strip, "gy", 2), cycled(strip, "gy", -2)
    (velocity,) = call(
        ascend,
        [forcing.shape],
        strip, ym1, ym2, yp1, yp2, v1, g1, cx1, cf1, rim, *inner, *outer,
        scratch=[
            (18, 24, z2), (3, 16, 24, z2), (17, 24, z2), (6, 16, 24, z2), (3, 16, 24, z2), (3, 16, 24, z2),
            (288, z2), lane_blocks(18, z1), (3, 10, 24, z1), (3, 10, 24, z1),
            (288, z1), lane_blocks(18, z0), (3, 12, 24, z0), (3, 12, 24, z0), forcing.shape,
        ],
        copies=8,
        where_out=pltpu.HBM,
    )
    return velocity


def solution(mesh):
    return jax.shard_map(
        per_device,
        mesh=mesh,
        in_specs=(P(None, "gx", "gy", None), P("gx", "gy", None)),
        out_specs=P(None, "gx", "gy", None),
        check_vma=False,
    )
```

```python
import functools

import jax
import jax.numpy as jnp
from jax import lax
from jax.experimental import pallas as pl
from jax.experimental.pallas import tpu as pltpu
from jax.sharding import PartitionSpec as P

F32 = jnp.float32
BF16 = jnp.bfloat16
WEIGHT = 2.0 / 3.0
VMEM_LIMIT = 24 * 1024 * 1024
U0, U1, U2 = 12, 12, 16


def materials(ids):
    eta = jnp.where(ids == 3, F32(4.0), F32(0.0))
    eta = jnp.where(ids == 2, F32(1.5), eta)
    eta = jnp.where(ids == 1, F32(0.6), eta)
    return jnp.where(ids == 0, F32(0.2), eta)


def lanes_of(shape):
    return lax.broadcasted_iota(jnp.int32, shape, len(shape) - 1)


def next_row(v):
    return pltpu.roll(v, v.shape[0] - 1, 0)


def last_row(v):
    return pltpu.roll(v, 1, 0)


def next_lane(v):
    return pltpu.roll(v, v.shape[1] - 1, 1)


def last_lane(v):
    return pltpu.roll(v, 1, 1)


def planes(count, body, unroll):
    steps = count // unroll if unroll < count else 0

    def step(n, _):
        for k in range(unroll):
            body(n * unroll + k)
        return 0

    if steps > 0:
        lax.fori_loop(0, steps, step, 0)
    for i in range(steps * unroll, count):
        body(i)


def kept(axis, step, value):
    place = lax.axis_index(axis) - step
    return jnp.where((place >= 0) & (place < lax.axis_size(axis)), value, 0.0)


class Spliced:
    def __init__(self, middle, outer, first, count, flat=False):
        self.middle, self.outer, self.first, self.count, self.flat = middle, outer, first, count, flat

    def place(self, key):
        lead, i = ((), key) if self.flat else ((key[0],), key[1])
        rest = () if self.flat else tuple(key[2:])
        if self.first <= i < self.first + self.count:
            return self.middle, lead + (i - self.first,) + rest
        return self.outer, lead + (i if i < self.first else i - self.count,) + rest

    def __getitem__(self, key):
        ref, at = self.place(key)
        return ref[at]

    def __setitem__(self, key, value):
        ref, at = self.place(key)
        ref[at] = value


def fine_set(inner, outer):
    spans = ((3, 4), (3, 6), (2, 8), (3, 8), (3, 7), (3, 6))
    return [Spliced(a, b, *span, flat=n in (3, 4)) for n, (a, b, span) in enumerate(zip(inner, outer, spans))]


def split_dot(rows, matrix):
    high = rows.astype(BF16)
    low = (rows - high.astype(F32)).astype(BF16)
    return jnp.dot(high, matrix, preferred_element_type=F32) + jnp.dot(
        low, matrix, preferred_element_type=F32
    )


def pair_matrix(fine):
    shape = (fine, fine // 2)
    row = lax.broadcasted_iota(jnp.int32, shape, 0)
    col = lax.broadcasted_iota(jnp.int32, shape, 1)
    return jnp.where((row == 2 * col) | (row == 2 * col + 1), F32(1), F32(0)).astype(BF16)


def copy_matrix(coarse):
    shape = (coarse, 2 * coarse)
    row = lax.broadcasted_iota(jnp.int32, shape, 0)
    col = lax.broadcasted_iota(jnp.int32, shape, 1)
    return jnp.where((col == 2 * row) | (col == 2 * row + 1), F32(1), F32(0)).astype(BF16)


YP, YM, ZP, ZM, DG, EI = range(6)


def plane_coefficients(below, here, above, scale):
    half = 0.5 * scale
    lane = lanes_of(here.shape)
    first = lane == 0
    final = lane == here.shape[1] - 1
    yp, ym = next_row(here), last_row(here)
    zp, zm = next_lane(here), last_lane(here)

    def ghost(q):
        return jnp.where(q > 0.0, q, here)

    around = ghost(yp) + ghost(ym) + ghost(below) + ghost(above)
    around = around + jnp.where(final, here, zp) + jnp.where(first, here, zm)
    diag = scale * (3.0 * here + 0.5 * around)
    return (
        half * (here + yp),
        half * (here + ym),
        jnp.where(final, 0.0, half * (here + zp)),
        jnp.where(first, 0.0, half * (here + zm)),
        diag,
        jnp.where(here > 0.0, WEIGHT / diag, 0.0),
    )


def coefficients(eta, cx, cf, layers, scale, unroll):
    planes(layers + 1, lambda i: face_plane(eta, cx, i, scale), unroll)
    planes(layers, lambda i: cell_plane(eta, cf, i, scale), unroll)


def face_plane(eta, cx, i, scale):
    cx[i] = (0.5 * scale) * (eta[i] + eta[i + 1])


def cell_plane(eta, cf, i, scale):
    made = plane_coefficients(eta[i], eta[i + 1], eta[i + 2], scale)
    for n, value in enumerate(made):
        cf[n, i] = value


def gather_sum(v, comp, i, cx, cf, k):
    here = v[comp, i]
    total = cx[k] * v[comp, i - 1] + cx[k + 1] * v[comp, i + 1]
    total = total + cf[YP, k] * next_row(here) + cf[YM, k] * last_row(here)
    total = total + cf[ZP, k] * next_lane(here) + cf[ZM, k] * last_lane(here)
    return here, total


def sweep(v, vo, g, go, cx, cf, co, out, oo, low, high, unroll):
    vo, go, co, oo = vo + low, go + low, co + low, oo + low

    def body(n):
        for comp in range(3):
            here, total = gather_sum(v, comp, n + vo, cx, cf, n + co)
            out[comp, n + oo] = (1.0 / 3.0) * here + cf[EI, n + co] * (g[comp, n + go] + total)

    planes(high - low, body, unroll)


def residual(v, vo, g, go, cx, cf, co, comp, x):
    here, total = gather_sum(v, comp, x + vo, cx, cf, x + co)
    return g[comp, x + go] - cf[DG, x + co] * here + total


def copied(copies):
    for copy in copies:
        copy.start()
    for copy in copies:
        copy.wait()


def pack_fine_x(f_in, ids_in, xup, xdown, ids, arrived):
    copies = [pltpu.make_async_copy(ids_in.at[5 * k : 5 * k + 3], ids.at[3 * k : 3 * k + 3], arrived.at[k]) for k in range(2)]
    for c in range(3):
        for k, out in enumerate((xdown, xup)):
            copies.append(
                pltpu.make_async_copy(f_in.at[c, 6 * k : 6 * k + 2], out.at[2 * c : 2 * c + 2], arrived.at[2 + 2 * c + k])
            )
    copied(copies)
    for n, out in enumerate((xdown, xup)):
        for k in range(3):
            out[6 + k] = materials(ids[3 * n + k])


def pack_fine_y(f_in, ids_in, yup, ydown, f, ids, arrived):
    copied(
        [pltpu.make_async_copy(ids_in.at[x : x + 2], ids.at[x : x + 2], arrived.at[8 + x // 2]) for x in (0, 2, 4, 6)]
        + [pltpu.make_async_copy(f_in.at[:, x], f.at[:, x], arrived.at[x]) for x in range(8)]
    )
    for x in range(8):
        eta = materials(ids[x])
        for out, at, eta_at in ((yup, 13, 12), (ydown, 0, 0)):
            pack_rows(out, x, 8, [f[c, x, at : at + 3] for c in range(3)])
            put_eta_rows(out, 9, x, eta[eta_at : eta_at + 4])


def pack_rows(out, n, spill, rows):
    out[n, 0:3] = rows[0]
    out[n, 3:6] = rows[1]
    out[n, 6:8] = rows[2][0:2]
    out[spill + n // 8, n % 8 : n % 8 + 1] = rows[2][2:3]


def put_eta_rows(out, first, n, rows):
    at = 4 * (n % 2)
    out[first + n // 2, at : at + 4] = rows


def fine_source(f, low, high, c, x):
    if x < 0:
        return kept("gx", 1, low[2 * c + x + 2])
    if x < 8:
        return f[c, x]
    return kept("gx", -1, high[2 * c + x - 8])


def fine_eta(ids, low, high, x):
    if x < 0:
        return kept("gx", 1, low[6 + x + 3])
    if x < 8:
        return materials(ids[x])
    return kept("gx", -1, high[6 + x - 8])


def pack_corners(low, high, up, down):
    for n, x in enumerate((-2, -1, 8, 9)):
        rows = [fine_source(None, low, high, c, x) for c in range(3)]
        for out, at in ((up, 13), (down, 0)):
            pack_rows(out, n, 4, [row[at : at + 3] for row in rows])
    for n, x in enumerate((-3, -2, -1, 8, 9, 10)):
        eta = fine_eta(None, low, high, x)
        put_eta_rows(up, 5, n, eta[12:16])
        put_eta_rows(down, 5, n, eta[0:4])
    for out in (up, down):
        out[4, 4:8] = jnp.zeros((4, low.shape[-1]), F32)


def fine_rows(g, eta, i, source, viscosity, low, high, n, spill, first):
    blank = jnp.zeros((1, source[0].shape[-1]), F32) if source else None
    if source:
        for c in range(3):
            g[c, i, 4:20] = source[c]
            g[c, i, 0:1] = blank
            g[c, i, 23:24] = blank
    for side, at, row, step in ((low, 1, 0, 1), (high, 20, 20, -1)):
        if source:
            tile = kept("gy", step, side[n, 0:8])
            g[0, i, at : at + 3] = tile[0:3]
            g[1, i, at : at + 3] = tile[3:6]
            g[2, i, at : at + 2] = tile[6:8]
            g[2, i, at + 2 : at + 3] = kept("gy", step, side[spill, n : n + 1])
        else:
            part = 4 * (n % 2)
            eta[i, row : row + 4] = kept("gy", step, side[first + n // 2, part : part + 4])
    if viscosity is not None:
        eta[i, 4:20] = viscosity


def fine_first(va, g, cf, i):
    for c in range(3):
        va[c, i] = cf[EI, i] * g[c, i]


def fine_inner(f, ids, ylow, yhigh, v0, va, g, eta, cx, cf):
    for x in range(8):
        fine_rows(g, eta, x, [f[c, x] for c in range(3)], None, ylow, yhigh, x, 8, 9)
        fine_rows(g, eta, x, None, materials(ids[x]), ylow, yhigh, x, 8, 9)
    for i in range(7):
        face_plane(eta, cx, i, 1.0)
    for i in range(6):
        cell_plane(eta, cf, i, 1.0)
        for c in range(3):
            va[c, i] = cf[EI, i] * g[c, i + 1]
    sweep(va, 0, g, 1, cx, cf, 0, v0, -1, 1, 5, U0)


def fine_down(*refs):
    xlow, xhigh, clow, chigh = refs[0:4]
    inner, outer = refs[4:10], refs[10:16]
    f1, eta1, up, down, pairs, rest = refs[16:22]
    v0, va, g, eta, cx, cf = fine_set(inner, outer)
    nz = xlow.shape[-1]
    for n, x in enumerate((-2, -1, 8, 9)):
        rows = [fine_source(None, xlow, xhigh, c, x) for c in range(3)]
        fine_rows(outer[2], None, n, rows, None, clow, chigh, n, 4, 5)
    for n, x in enumerate((-3, -2, -1, 8, 9, 10)):
        fine_rows(None, outer[3], n, None, fine_eta(None, xlow, xhigh, x), clow, chigh, n, 4, 5)
    for i in (0, 1, 2, 10, 11, 12):
        face_plane(eta, cx, i, 1.0)
    for i in (0, 1, 2, 9, 10, 11):
        cell_plane(eta, cf, i, 1.0)
        fine_first(va, g, cf, i)
    sweep(va, 2, g, 2, cx, cf, 2, v0, 1, -1, 2, U0)
    sweep(va, 2, g, 2, cx, cf, 2, v0, 1, 6, 9, U0)

    def down_pair(k):
        for c in range(3):
            x = 2 * k
            total = residual(v0, 1, g, 2, cx, cf, 2, c, x) + residual(v0, 1, g, 2, cx, cf, 2, c, x + 1)
            put_plane(pairs, c * 4 + k, total)

    planes(4, down_pair, U0)

    def eta_pair(k):
        put_plane(pairs, 12 + k, eta[2 * k + 1] + eta[2 * k + 2])

    planes(6, eta_pair, U0)
    for n in range(18):
        row_pairs(pairs, n, 4, 8, rest, n * 8)
    coarse = split_dot(rest[...], pair_matrix(nz)) * 0.125
    for n in range(12):
        block = coarse[n * 8 : n * 8 + 8]
        f1[n // 4, n % 4] = block
        up[n] = block
        down[n] = block
    for n in range(6):
        block = coarse[96 + n * 8 : 96 + n * 8 + 8]
        eta1[n] = block
        if n < 5:
            up[12 + n] = block
        if n > 0:
            down[12 + n - 1] = block


def lane_blocks(planes, nz):
    width = min(nz, 128)
    return (planes, nz // width, 24, width)


def put_plane(ref, n, value):
    width = ref.shape[-1]
    for b in range(ref.shape[1]):
        ref[n, b] = value[:, b * width : b * width + width]


def row_pairs(ref, n, at, count, out, row):
    width = ref.shape[-1]
    for b in range(ref.shape[1]):
        total = ref[n, b, pl.ds(at, count, stride=2), :] + ref[n, b, pl.ds(at + 1, count, stride=2), :]
        out[row : row + count, b * width : b * width + width] = total


def row_copies(ref, n, value):
    width = ref.shape[-1]
    count = value.shape[0]
    for b in range(ref.shape[1]):
        block = value[:, b * width : b * width + width]
        ref[n, b, pl.ds(0, count, stride=2), :] = block
        ref[n, b, pl.ds(1, count, stride=2), :] = block


def get_plane(ref, n):
    return jnp.concatenate([ref[n, b] for b in range(ref.shape[1])], axis=1)


def fine_rim(low, high, *refs):
    _, va, g, eta, cx, cf = fine_set(refs[0:6], refs[6:12])
    rim = refs[12]
    nz = low.shape[-1]
    blank = jnp.zeros((4, nz), F32)
    for n, (side, step) in enumerate(((low, 1), (high, -1))):
        rows = [jnp.concatenate([blank, kept("gx", step, side[k]), blank], axis=0) for k in range(4)]
        edge, k, inner, face, far = ((0, 0, 1, 1, 0), (13, 11, 10, 11, 12))[n]
        weight = plane_coefficients(rows[3], eta[edge], eta[1 if n == 0 else 12], 1.0)[EI]
        for c in range(3):
            here = va[c, k]
            total = cx[far] * (weight * rows[c]) + cx[face] * va[c, inner]
            total = total + cf[YP, k] * next_row(here) + cf[YM, k] * last_row(here)
            total = total + cf[ZP, k] * next_lane(here) + cf[ZM, k] * last_lane(here)
            rim[c, n] = (1.0 / 3.0) * here + cf[EI, k] * (g[c, k] + total)


def pack_middle_y(f1, eta1, low, high, f, ids, up, down, late_up, late_down):
    for c in range(3):
        late_up[c] = f[c, 5]
        late_down[c] = f[c, 2]
    late_up[3] = materials(ids[4])
    late_down[3] = materials(ids[3])

    def source(c, x):
        if x < 0:
            return kept("gx", 1, low[4 * c + x + 4])
        if x < 4:
            return f1[c, x]
        return kept("gx", -1, high[4 * c + x - 4])

    def viscosity(x):
        if x < 0:
            return kept("gx", 1, low[12 + x + 5])
        if x < 4:
            return eta1[x + 1]
        return kept("gx", -1, high[12 + x - 4])

    for i in range(12):
        rows = [source(c, i - 4) for c in range(3)]
        for out, at in ((up, 4), (down, 0)):
            out[i, 0:4] = rows[0][at : at + 4]
            out[i, 4:8] = rows[1][at : at + 4]
            out[12 + i + 1, 0:4] = rows[2][at : at + 4]
    for out in (up, down):
        out[12, 0:4] = jnp.zeros((4, f1.shape[-1]), F32)
        out[25, 0:4] = jnp.zeros((4, f1.shape[-1]), F32)
        out[27, 6:8] = jnp.zeros((2, f1.shape[-1]), F32)
    for j in range(14):
        eta = viscosity(j - 5)
        up[12 + j, 4:8] = eta[4:8]
        down[12 + j, 4:8] = eta[0:4]
        up[26 + j // 8, j % 8 : j % 8 + 1] = eta[3:4]
        down[26 + j // 8, j % 8 : j % 8 + 1] = eta[4:5]


def middle_down(f1, eta1, xlow, xhigh, ylow, yhigh, v1, g, cx, cf, own, up, down, far_up, far_down, eta, va, pairs, rest):
    nz = f1.shape[-1]
    blank = jnp.zeros((4, nz), F32)

    def source(c, x):
        if x < 0:
            return kept("gx", 1, xlow[4 * c + x + 4])
        if x < 4:
            return f1[c, x]
        return kept("gx", -1, xhigh[4 * c + x - 4])

    def viscosity(x):
        if x < 0:
            return kept("gx", 1, xlow[12 + x + 5])
        if x < 4:
            return eta1[x + 1]
        return kept("gx", -1, xhigh[12 + x - 4])

    for c in range(3):
        for i in range(12):
            g[c, i, 8:16] = source(c, i - 4)
            g[c, i, 0:4] = blank
            g[c, i, 20:24] = blank
            for side, at, step in ((ylow, 4, 1), (yhigh, 16, -1)):
                rows = side[i, 4 * c : 4 * c + 4] if c < 2 else side[13 + i, 0:4]
                g[c, i, at : at + 4] = kept("gy", step, rows)
    for j in range(14):
        eta[j, 0:4] = blank
        eta[j, 20:24] = blank
        eta[j, 8:16] = viscosity(j - 5)
        eta[j, 4:8] = kept("gy", 1, ylow[12 + j, 4:8])
        eta[j, 3:4] = kept("gy", 1, ylow[26 + j // 8, j % 8 : j % 8 + 1])
        eta[j, 16:20] = kept("gy", -1, yhigh[12 + j, 4:8])
        eta[j, 20:21] = kept("gy", -1, yhigh[26 + j // 8, j % 8 : j % 8 + 1])

    coefficients(eta, cx, cf, 12, 0.25, U1)

    plane = jnp.zeros((24, nz), F32)
    for c in range(3):
        for i in (0, 13):
            va[c, i] = plane
            v1[c, i] = plane

    def start(i):
        for c in range(3):
            va[c, i + 1] = cf[EI, i] * g[c, i]

    planes(12, start, U1)
    sweep(va, 5, g, 4, cx, cf, 4, v1, 5, -4, 8, U1)

    def down_pair(k):
        for c in range(3):
            x = 2 * k
            total = residual(v1, 1, g, 0, cx, cf, 0, c, x) + residual(v1, 1, g, 0, cx, cf, 0, c, x + 1)
            put_plane(pairs, c * 6 + k, total)

    planes(6, down_pair, U1)

    def eta_pair(k):
        put_plane(pairs, 18 + k, eta[2 * k + 1] + eta[2 * k + 2])

    planes(6, eta_pair, U1)
    for k in range(6):
        for c in range(3):
            row_pairs(pairs, c * 6 + k, 8, 4, rest, 16 * k + 4 * c)
        row_pairs(pairs, 18 + k, 8, 4, rest, 16 * k + 12)
    coarse = split_dot(rest[...], pair_matrix(nz)) * 0.125
    for k in range(6):
        own[k] = coarse[16 * k : 16 * k + 16]
    for t in range(4):
        source_rows = own[t + 1, 0:12]
        up[t, 0:12] = source_rows
        up[t, 12:16] = own[t, 12:16]
        down[t, 0:12] = source_rows
        down[t, 12:16] = own[t + 2, 12:16]
        if t < 2:
            far_up[t, 0:12] = source_rows
            far_up[t, 12:16] = own[t, 12:16]
        else:
            far_down[t - 2, 0:12] = source_rows
            far_down[t - 2, 12:16] = own[t + 2, 12:16]


def pack_coarse_y(own, low2, low3, high2, high3, strip):
    strip[0, 0:12] = jnp.zeros((12, own.shape[-1]), F32)
    strip[17, 0:12] = jnp.zeros((12, own.shape[-1]), F32)
    for t in range(2):
        rows = kept("gx", 3, low3[t])
        strip[1 + t, 0:12] = rows[0:12]
        strip[t, 12:16] = rows[12:16]
        rows = kept("gx", -3, high3[t])
        strip[15 + t, 0:12] = rows[0:12]
        strip[16 + t, 12:16] = rows[12:16]
    for t in range(4):
        rows = kept("gx", 2, low2[t])
        strip[3 + t, 0:12] = rows[0:12]
        strip[2 + t, 12:16] = rows[12:16]
        strip[7 + t, 0:12] = own[1 + t, 0:12]
        rows = kept("gx", -2, high2[t])
        strip[11 + t, 0:12] = rows[0:12]
        strip[12 + t, 12:16] = rows[12:16]
    for t in range(6):
        strip[6 + t, 12:16] = own[t, 12:16]
    for plane, outer, mine in ((6, 5, 0), (11, 12, 5)):
        inside = strip[outer, 12:16] > 0.0
        for c in range(3):
            rows = slice(4 * c, 4 * c + 4)
            strip[plane, rows] = jnp.where(inside, strip[plane, rows], own[mine, rows])


def ascend(
    mid, ym1, ym2, yp1, yp2, v1, g1, cx1, cf1, rim,
    v0i, vai, g0i, eta0i, cx0i, cf0i, v0o, vao, g0o, eta0o, cx0o, cf0o, out,
    eta2, g2, cx2, cf2, va2, vb2, rows2, wide1, va1, vb1, rows1, wide0, va0, vb0, result, sent,
):
    v0, _, g0, _, cx0, cf0 = fine_set((v0i, vai, g0i, eta0i, cx0i, cf0i), (v0o, vao, g0o, eta0o, cx0o, cf0o))
    nz2, nz1 = mid.shape[-1], v1.shape[-1]
    blank = jnp.zeros((4, nz2), F32)
    sides = ((ym2, 2), (ym1, 1), (mid, 0), (yp1, -1), (yp2, -2))
    for j in range(18):
        for n, (side, step) in enumerate(sides):
            rows = kept("gy", step, side[j]) if step else side[j]
            eta2[j, 4 * n : 4 * n + 4] = rows[12:16]
            if 1 <= j <= 16:
                for c in range(3):
                    g2[c, j - 1, 4 * n : 4 * n + 4] = rows[4 * c : 4 * c + 4]
        eta2[j, 20:24] = blank
        if 1 <= j <= 16:
            for c in range(3):
                g2[c, j - 1, 20:24] = blank
    coefficients(eta2, cx2, cf2, 16, 0.0625, U2)

    def start(i):
        for c in range(3):
            va2[c, i] = cf2[EI, i] * g2[c, i]

    planes(16, start, U2)
    source, target = va2, vb2
    for s in range(1, 6):
        sweep(source, 0, g2, 0, cx2, cf2, 0, target, 0, s, 16 - s, U2)
        source, target = target, source

    for c in range(3):
        for k in range(6):
            rows2[(c * 6 + k) * 16 : (c * 6 + k) * 16 + 16] = source[c, 5 + k, 4:20]
    spread = split_dot(rows2[...], copy_matrix(nz2))
    for n in range(18):
        block = spread[n * 16 : n * 16 + 12]
        row_copies(wide1, n, block)
    for c in range(3):
        for i in range(10):
            va1[c, i] = v1[c, i + 2] + get_plane(wide1, c * 6 + (i - 3) // 2 + 2)
    sweep(va1, 3, g1, 4, cx1, cf1, 4, vb1, 3, -2, 6, U1)
    sweep(vb1, 3, g1, 4, cx1, cf1, 4, va1, 3, -1, 5, U1)

    for c in range(3):
        for k in range(6):
            rows1[(c * 6 + k) * 16 : (c * 6 + k) * 16 + 16] = va1[c, 2 + k, 6:22]
    spread = split_dot(rows1[...], copy_matrix(nz1))
    for n in range(18):
        block = spread[n * 16 : n * 16 + 12]
        row_copies(wide0, n, block)

    for k in range(6):
        for c in range(3):
            block = get_plane(wide0, c * 6 + k)
            va0[c, 2 * k] = (v0[c, 2 * k - 1] if k > 0 else rim[c, 0]) + block
            va0[c, 2 * k + 1] = (v0[c, 2 * k] if k < 5 else rim[c, 1]) + block
    sweep(va0, 2, g0, 2, cx0, cf0, 2, vb0, 2, -1, 9, U0)

    def final(x):
        for c in range(3):
            here, total = gather_sum(vb0, c, x + 2, cx0, cf0, x + 2)
            value = (1.0 / 3.0) * here + cf0[EI, x + 2] * (g0[c, x + 2] + total)
            result[c, x] = value[4:20]
        pltpu.make_async_copy(result.at[:, x], out.at[:, x], sent.at[x]).start()

    planes(8, final, U0)
    for x in range(8):
        pltpu.make_async_copy(result.at[:, x], out.at[:, x], sent.at[x]).wait()


def typed(shape):
    return shape if isinstance(shape, jax.ShapeDtypeStruct) else jax.ShapeDtypeStruct(shape, F32)


def call(body, outs, *args, scratch=(), copies=0, where_in=pltpu.VMEM, where_out=pltpu.VMEM):
    outs = [typed(out) for out in outs]
    scratch_shapes = [pltpu.VMEM(typed(shape).shape, typed(shape).dtype) for shape in scratch]
    if copies:
        scratch_shapes.append(pltpu.SemaphoreType.DMA((copies,)))
    return pl.pallas_call(
        body,
        out_shape=outs,
        in_specs=[pl.BlockSpec(memory_space=where_in)] * len(args),
        out_specs=[pl.BlockSpec(memory_space=where_out)] * len(outs),
        scratch_shapes=scratch_shapes,
        compiler_params=pltpu.CompilerParams(vmem_limit_bytes=VMEM_LIMIT),
    )(*args)


def cycled(array, axis, step):
    size = lax.axis_size(axis)
    return lax.ppermute(array, axis, [(i, (i + step) % size) for i in range(size)])


def per_device(forcing, phase_ids):
    z0 = forcing.shape[-1]
    z1, z2 = z0 // 2, z0 // 4
    inputs = [pltpu.with_memory_space_constraint(a, pltpu.HBM) for a in (forcing, phase_ids)]
    xup, xdown = call(
        pack_fine_x, [(9, 16, z0)] * 2, *inputs,
        scratch=[jax.ShapeDtypeStruct((6, 16, z0), jnp.int32)], copies=8, where_in=pltpu.HBM,
    )
    yup, ydown, f0, ids0 = call(
        pack_fine_y,
        [(13, 8, z0)] * 2 + [forcing.shape, jax.ShapeDtypeStruct(phase_ids.shape, jnp.int32)],
        *inputs, copies=12, where_in=pltpu.HBM,
    )
    xlow, xhigh = cycled(xup, "gx", 1), cycled(xdown, "gx", -1)
    ylow, yhigh = cycled(yup, "gy", 1), cycled(ydown, "gy", -1)
    up, down = call(pack_corners, [(8, 8, z0)] * 2, xlow, xhigh)
    clow, chigh = cycled(up, "gy", 1), cycled(down, "gy", -1)
    inner = call(
        fine_inner,
        [(3, 4, 24, z0), (3, 6, 24, z0), (3, 8, 24, z0), (8, 24, z0), (7, 24, z0), (6, 6, 24, z0)],
        f0, ids0, ylow, yhigh,
    )
    *outer, f1, eta1, up, down = call(
        fine_down,
        [(3, 6, 24, z0), (3, 6, 24, z0), (3, 4, 24, z0), (6, 24, z0), (6, 24, z0), (6, 6, 24, z0), (3, 4, 8, z1), (6, 8, z1), (17, 8, z1), (17, 8, z1)],
        xlow, xhigh, clow, chigh, *inner,
        scratch=[lane_blocks(18, z0), (144, z0)],
    )
    xlow, xhigh = cycled(up, "gx", 1), cycled(down, "gx", -1)
    up, down, late_up, late_down = call(
        pack_middle_y, [(28, 8, z1)] * 2 + [(4, 16, z0)] * 2, f1, eta1, xlow, xhigh, f0, ids0
    )
    ylow, yhigh = cycled(up, "gy", 1), cycled(down, "gy", -1)
    late_low, late_high = cycled(late_up, "gx", 1), cycled(late_down, "gx", -1)
    (rim,) = call(fine_rim, [(3, 2, 24, z0)], late_low, late_high, *inner, *outer)
    v1, g1, cx1, cf1, own, up, down, far_up, far_down = call(
        middle_down,
        [(3, 14, 24, z1), (3, 12, 24, z1), (13, 24, z1), (6, 12, 24, z1), (6, 16, z2), (4, 16, z2), (4, 16, z2), (2, 16, z2), (2, 16, z2)],
        f1, eta1, xlow, xhigh, ylow, yhigh,
        scratch=[(14, 24, z1), (3, 14, 24, z1), lane_blocks(24, z1), (96, z1)],
    )
    low2, high2 = cycled(up, "gx", 2), cycled(down, "gx", -2)
    low3, high3 = cycled(far_up, "gx", 3), cycled(far_down, "gx", -3)
    (strip,) = call(pack_coarse_y, [(18, 16, z2)], own, low2, low3, high2, high3)
    ym1, yp1 = cycled(strip, "gy", 1), cycled(strip, "gy", -1)
    ym2, yp2 = cycled(strip, "gy", 2), cycled(strip, "gy", -2)
    (velocity,) = call(
        ascend,
        [forcing.shape],
        strip, ym1, ym2, yp1, yp2, v1, g1, cx1, cf1, rim, *inner, *outer,
        scratch=[
            (18, 24, z2), (3, 16, 24, z2), (17, 24, z2), (6, 16, 24, z2), (3, 16, 24, z2), (3, 16, 24, z2),
            (288, z2), lane_blocks(18, z1), (3, 10, 24, z1), (3, 10, 24, z1),
            (288, z1), lane_blocks(18, z0), (3, 12, 24, z0), (3, 12, 24, z0), forcing.shape,
        ],
        copies=8,
        where_out=pltpu.HBM,
    )
    return velocity


def solution(mesh):
    return jax.shard_map(
        per_device,
        mesh=mesh,
        in_specs=(P(None, "gx", "gy", None), P("gx", "gy", None)),
        out_specs=P(None, "gx", "gy", None),
        check_vma=False,
    )
```
